256 devices in a mesh: dp: 32 (over z_hi, x, core), tensor: 8 (over z_lo, y).
Axes of the slice: x: 4, y: 4, z: 8 (z_hi: 4, z_lo: 2; z = z_hi * 2 + z_lo), core: 2. Of those that a mesh axis runs over, the one named last changes fastest.
Arguments:
- hidden: bfloat16 [16384, 16384], P('dp')
- head: bfloat16 [2048, 16384], P('tensor', 'dp')
- targets: int32 [16384], P('dp'), may hold values from 0 to 127999, as said below
- block_index: int32 [2], replicated, may hold values from 0 to 124, as said below
- lse_rest: float32 [16384], P('dp'), may hold values from 6 to 12
- cotangent: float32 [16384], P('dp'), may hold values from 0.5 to 1.5
Outputs:
- loss: float32 [16384], P('dp')
- head_grad: float32 [2048, 16384], P('tensor', 'dp')
The draws below stay inside these ranges and needn't reach their ends.
Inputs may be any that keep to these rules, and one draw needn't show every extreme that they name: `block_index`: distinct block numbers of the vocabulary. Every target lies in one of the window's blocks: targets // 1024 is an entry of block_index.
All inputs are finite; a program needn't handle non-finite values.
Results may differ from the reference program's by a relative error of at most 0.003.
Values may be sent and summed in bfloat16 or wider, within the bound.
No kernel may reach another device: no remote copies, remote signals or barrier semaphores. Data moves between devices by JAX's collectives and lax.ppermute only.
A program may use at most 128 MiB of HBM per device.

```python
import jax
import jax.numpy as jnp
from jax import lax

D = 16384
VOCAB = 128256
BLOCK = 1024
NCH = 2
TOKENS = 16384
VW = 2048


def window_rows(key):
    return jax.random.normal(jax.random.fold_in(key, 11), (VW, D), jnp.float32) * D ** (-0.5)


def pick_blocks(key):
    last_block = VOCAB // BLOCK - 1
    order = jax.random.permutation(jax.random.fold_in(key, 21), last_block)
    chosen = jnp.concatenate([order[:NCH - 1].astype(jnp.int32), jnp.full((1,), last_block, jnp.int32)])
    turn = jax.random.randint(jax.random.fold_in(key, 22), (), 0, NCH)
    return jnp.roll(chosen, turn).astype(jnp.int32)


def draw_head(key, part):
    return window_rows(key).astype(jnp.bfloat16)


def draw_hidden(key, part):
    key = jax.random.fold_in(key, 2)
    scale_key, base_key = jax.random.split(key, 2)
    scales = jnp.exp(jax.random.uniform(scale_key, (TOKENS, 1), jnp.float32, jnp.log(1.5), jnp.log(12.0)))
    return (jax.random.normal(base_key, (TOKENS, D), jnp.float32) * scales).astype(jnp.bfloat16)


def draw_block_index(key, part):
    chosen = pick_blocks(key)
    return chosen


def draw_targets(key, part):
    chosen = pick_blocks(key)
    key = jax.random.fold_in(key, 3)
    block_key, offset_key = jax.random.split(key)
    which = jax.random.randint(block_key, (TOKENS,), 0, NCH)
    offset = jax.random.randint(offset_key, (TOKENS,), 0, BLOCK)
    which = which.at[TOKENS - 1].set(jnp.argmax(chosen).astype(which.dtype))
    offset = offset.at[TOKENS - 1].set(BLOCK - 1)
    return (chosen[which] * BLOCK + offset).astype(jnp.int32)


def levels(stream_key, extent, cuts, low, top_value):
    def one(position, blocks):
        heights = jax.random.uniform(jax.random.fold_in(jax.random.fold_in(stream_key, 6), position), (blocks,), jnp.float32, low / len(cuts), top_value / len(cuts))
        return jnp.repeat(jnp.exp(heights), extent[position] // blocks).reshape((-1,) + (1,) * (len(extent) - position - 1))

    gain = one(*cuts[0])
    for cut in cuts[1:]:
        gain = gain * one(*cut)
    return gain


def setup_inputs(seed: int = 0) -> dict:
    streams_of = jax.random.split(jax.random.key(seed), 7)
    return {
        "hidden": draw_hidden(jax.random.fold_in(streams_of[6], 71), 0),
        "head": draw_head(jax.random.fold_in(streams_of[6], 71), 0),
        "targets": draw_targets(jax.random.fold_in(streams_of[6], 71), 0),
        "block_index": draw_block_index(jax.random.fold_in(streams_of[6], 71), 0),
        "lse_rest": jnp.clip(6.0 + 6.0 * jax.random.uniform(streams_of[4], (TOKENS,), jnp.float32) ** levels(streams_of[4], (TOKENS,), ((0, 32),), -0.2, 0.2), 6.0, 12.0),
        "cotangent": jnp.clip(0.5 + 1.0 * jax.random.uniform(streams_of[5], (TOKENS,), jnp.float32) ** levels(streams_of[5], (TOKENS,), ((0, 32),), -0.2, 0.2), 0.5, 1.5),
    }


z_weight = 1e-4


def reference(hidden, head, targets, block_index, lse_rest, cotangent):
    row_ids = jnp.arange(VW, dtype=jnp.int32)
    vocab_ids = block_index[row_ids // BLOCK] * BLOCK + row_ids % BLOCK
    logits = lax.dot_general(hidden, head, (((1,), (1,)), ((), ())), preferred_element_type=jnp.float32)
    row_max = jnp.max(logits, axis=1)
    row_total = jnp.sum(jnp.exp(logits - row_max[:, None]), axis=1)
    lse_window = row_max + jnp.log(row_total)
    larger = jnp.maximum(lse_window, lse_rest)
    log_total = larger + jnp.log(jnp.exp(lse_window - larger) + jnp.exp(lse_rest - larger))
    target_hit = vocab_ids[None, :] == targets[:, None]
    target_logit = jnp.sum(jnp.where(target_hit, logits, jnp.float32(0.0)), axis=1)
    loss = log_total - target_logit + z_weight * log_total * log_total
    softmax = jnp.exp(logits - log_total[:, None])
    grad_logits = (cotangent[:, None] * (softmax * (1.0 + 2.0 * z_weight * log_total)[:, None] - target_hit.astype(jnp.float32))).astype(jnp.bfloat16)
    head_grad = lax.dot_general(grad_logits, hidden, (((0,), (0,)), ((), ())), preferred_element_type=jnp.float32)
    return loss, head_grad
```

```python
import jax
import jax.numpy as jnp
from jax import lax
from jax.sharding import Mesh
from jax.sharding import PartitionSpec as P

BLOCK = 1024
z_weight = 0.0001

AXES = ("zh", "x", "c", "zl", "y")
SIZES = (4, 4, 2, 2, 4)
DP = ("zh", "x", "c")
TENSOR = ("zl", "y")


def move(value, axis, by):
    n = SIZES[AXES.index(axis)]
    return lax.ppermute(value, axis, [(i, (i + by) % n) for i in range(n)])


def gather(value, axis):
    half = value.shape[0] // 2
    behind = move(value, axis, 1)
    ahead = move(value, axis, -1)
    far = jnp.concatenate([move(behind[:half], axis, 1), move(ahead[half:], axis, -1)], axis=0)
    return [value, ahead, far, behind]


def scatter(blocks, axis):
    half = blocks[0].shape[0] // 2
    low = jnp.bfloat16
    far = blocks[2].astype(low)
    from_behind = move(far[:half], axis, 1).astype(jnp.float32)
    from_ahead = move(far[half:], axis, -1).astype(jnp.float32)
    up_direct = move(blocks[1][half:].astype(low), axis, 1)
    down_direct = move(blocks[3][:half].astype(low), axis, -1)
    up = move((blocks[1][:half] + from_behind).astype(low), axis, 1)
    down = move((blocks[3][half:] + from_ahead).astype(low), axis, -1)
    first = blocks[0][:half] + up.astype(jnp.float32) + down_direct.astype(jnp.float32)
    second = blocks[0][half:] + up_direct.astype(jnp.float32) + down.astype(jnp.float32)
    return jnp.concatenate([first, second], axis=0)


def shards(hidden, head, targets, block_index, lse_rest, cotangent):
    vocab_rows, width = head.shape
    tokens = hidden.shape[0]
    zh, x, c = (lax.axis_index(a) for a in DP)
    first_row = lax.axis_index(TENSOR) * vocab_rows
    row_ids = first_row + lax.iota(jnp.int32, vocab_rows)
    block_of = row_ids // BLOCK
    block_match = (block_of[:, None] == lax.iota(jnp.int32, block_index.shape[0])[None, :]).astype(
        jnp.int32
    )
    vocab_ids = jnp.sum(block_match * block_index[None, :], axis=1) * BLOCK + row_ids % BLOCK

    def columns(dz, dx, core):
        at = (((zh + dz) % 4) * 4 + (x + dx) % 4) * 2 + core
        return lax.dynamic_slice(hidden, (0, at * width), (tokens, width))

    mine, sibling = {}, {}
    for dz in range(4):
        for dx in range(4):
            mine[dz, dx] = columns(dz, dx, c)
        theirs = jnp.stack([columns(dz, dx, 1 - c) for dx in range(4)])
        theirs = move(theirs, "c", 1)
        for dx in range(4):
            sibling[dz, dx] = theirs[dx]
    facts = jnp.stack([targets.astype(jnp.float32), lse_rest, cotangent])
    facts = jnp.concatenate([facts, move(facts, "c", 1)], axis=1)
    targets, lse_rest, cotangent = facts[0].astype(jnp.int32), facts[1], facts[2]

    by_z = gather(head, "zh")
    logits_mine = logits_sibling = None
    for dz in (0, 1, 3, 2):
        rows = gather(by_z[dz], "x")
        for dx in (0, 1, 3, 2):
            a = lax.dot_general(
                rows[dx], mine[dz, dx], (((1,), (1,)), ((), ())), preferred_element_type=jnp.float32
            )
            b = lax.dot_general(
                rows[dx], sibling[dz, dx], (((1,), (1,)), ((), ())), preferred_element_type=jnp.float32
            )
            logits_mine = a if logits_mine is None else logits_mine + a
            logits_sibling = b if logits_sibling is None else logits_sibling + b
    logits = jnp.concatenate([logits_mine, logits_sibling], axis=1)
    other = move(logits, "c", 1)
    logits = logits + jnp.concatenate([other[:, tokens:], other[:, :tokens]], axis=1)

    target_hit = vocab_ids[:, None] == targets[None, :]
    target_pick = jnp.sum(jnp.where(target_hit, logits, jnp.float32(0.0)), axis=0)
    local_max = jnp.max(logits, axis=0)
    local_sum = jnp.sum(jnp.exp(logits - local_max[None, :]), axis=0)
    stats = jnp.stack([local_max, local_sum, target_pick])
    stats = lax.all_to_all(
        jnp.broadcast_to(stats[None], (8,) + stats.shape), TENSOR, split_axis=0, concat_axis=0, tiled=True
    )
    row_max = jnp.max(stats[:, 0], axis=0)
    row_total = jnp.sum(stats[:, 1] * jnp.exp(stats[:, 0] - row_max[None]), axis=0)
    target_logit = jnp.sum(stats[:, 2], axis=0)
    lse_window = row_max + jnp.log(row_total)
    larger = jnp.maximum(lse_window, lse_rest)
    log_total = larger + jnp.log(jnp.exp(lse_window - larger) + jnp.exp(lse_rest - larger))
    loss = (log_total - target_logit + z_weight * log_total * log_total)[:tokens]
    softmax = jnp.exp(logits - log_total[None, :])
    grad_logits = (
        cotangent[None, :]
        * (softmax * (1.0 + 2.0 * z_weight * log_total)[None, :] - target_hit.astype(jnp.float32))
    ).astype(jnp.bfloat16)
    grad_mine, grad_sibling = grad_logits[:, :tokens], grad_logits[:, tokens:]

    def term(dz, dx):
        return lax.dot(grad_mine, mine[dz, dx], preferred_element_type=jnp.float32) + lax.dot(
            grad_sibling, sibling[dz, dx], preferred_element_type=jnp.float32
        )

    sums = [None] * 4
    for dz in (2, 1, 3, 0):
        sums[dz] = scatter([term(dz, dx) for dx in range(4)], "x")
    head_grad = scatter(sums, "zh")
    return loss, head_grad


def solution(mesh):
    mesh = Mesh(mesh.devices.reshape(SIZES), AXES)
    placed = (P(DP, None), P(TENSOR, DP), P(DP), P(), P(DP), P(DP))
    return jax.shard_map(
        shards, mesh=mesh, in_specs=placed, out_specs=(P(DP), P(TENSOR, DP)), check_vma=False
    )
```

```python
import functools

import jax
import jax.numpy as jnp
from jax import lax
from jax.experimental import pallas as pl
from jax.experimental.pallas import tpu as pltpu
from jax.sharding import Mesh
from jax.sharding import PartitionSpec as P

BLOCK = 1024
z_weight = 0.0001

AXES = ("zh", "x", "c", "zl", "y")
SIZES = (4, 4, 2, 2, 4)
DP = ("zh", "x", "c")
TENSOR = ("zl", "y")

ROWS = 256
TOK = 512
WIDE = 512
PR, QR = 192, 64
PH, QH, RH = PR // 2, QR // 2, ROWS // 2

F32 = jnp.float32
BF16 = jnp.bfloat16
MIB = 1024 * 1024


def move(value, axis, by):
    n = SIZES[AXES.index(axis)]
    return lax.ppermute(value, axis, [(i, (i + by) % n) for i in range(n)])


def params(mib=52):
    return pltpu.CompilerParams(vmem_limit_bytes=mib * MIB)


def whole(shape):
    return pl.BlockSpec(shape, lambda *_: (0,) * len(shape))


def local_call(body, outs, *args):
    size = sum(a.size * a.dtype.itemsize for a in args) + sum(
        o.size * o.dtype.itemsize for o in outs
    )
    return pl.pallas_call(
        body,
        out_shape=outs,
        in_specs=[whole(a.shape) for a in args],
        out_specs=[whole(o.shape) for o in outs],
        compiler_params=params(24),
        cost_estimate=pl.CostEstimate(flops=0, bytes_accessed=size, transcendentals=0),
    )(*args)


def pick(hidden, at):
    n = at.shape[0]

    def body(at_ref, h_ref, o_ref):
        o_ref[0] = h_ref[...]

    return pl.pallas_call(
        body,
        out_shape=jax.ShapeDtypeStruct((n, TOK, WIDE), BF16),
        grid_spec=pltpu.PrefetchScalarGridSpec(
            num_scalar_prefetch=1,
            grid=(n,),
            in_specs=[pl.BlockSpec((TOK, WIDE), lambda i, at: (0, at[i]))],
            out_specs=pl.BlockSpec((1, TOK, WIDE), lambda i, at: (i, 0, 0)),
        ),
        compiler_params=params(),
        cost_estimate=pl.CostEstimate(
            flops=0, bytes_accessed=2 * n * TOK * WIDE * 2, transcendentals=0
        ),
    )(at, hidden)


def add_logits(total, plan, pieces, hidden, theirs, at):
    n = len(plan)
    slots = jnp.array([slot for slot, _ in plan], jnp.int32)
    index = jnp.stack([at[slots], slots])
    work = sum(r for _, parts in plan for _, _, r, _ in parts)
    has_total = total is not None

    def body(index_ref, h_ref, t_ref, *refs):
        refs, out = refs[:-1], refs[-1]
        step = pl.program_id(0)

        @pl.when(step == 0)
        def _():
            out[...] = refs[-1][...] if has_total else jnp.zeros_like(out)

        for i, (_, parts) in enumerate(plan):

            @pl.when(step == i)
            def _(parts=parts):
                for piece, start, rows, to in parts:
                    a = refs[piece][start : start + rows, :]
                    for side, ref in ((0, h_ref[...]), (1, t_ref[0])):
                        out[to : to + rows, side * TOK : (side + 1) * TOK] += lax.dot_general(
                            a, ref, (((1,), (1,)), ((), ())), preferred_element_type=F32
                        )

    extra = [total] if has_total else []
    return pl.pallas_call(
        body,
        out_shape=jax.ShapeDtypeStruct((ROWS, 2 * TOK), F32),
        grid_spec=pltpu.PrefetchScalarGridSpec(
            num_scalar_prefetch=1,
            grid=(n,),
            in_specs=[
                pl.BlockSpec((TOK, WIDE), lambda i, index: (0, index[0, i])),
                pl.BlockSpec((1, TOK, WIDE), lambda i, index: (index[1, i], 0, 0)),
            ]
            + [whole(p.shape) for p in pieces + extra],
            out_specs=whole((ROWS, 2 * TOK)),
        ),
        compiler_params=params(),
        cost_estimate=pl.CostEstimate(
            flops=2 * work * WIDE * 2 * TOK,
            bytes_accessed=2 * n * TOK * WIDE * 2 + 2 * ROWS * TOK * 8,
            transcendentals=0,
        ),
    )(index, hidden, theirs, *pieces, *extra)


def gradient_terms(plan, outs, grad, hidden, theirs, at):
    n = len(plan)
    slots = jnp.array([slot for slot, _ in plan], jnp.int32)
    index = jnp.stack([at[slots], slots])

    def body(index_ref, g_ref, h_ref, t_ref, *refs):
        outs, term = refs[:-1], refs[-1]
        step = pl.program_id(0)
        term[...] = jnp.dot(
            g_ref[:, :TOK], h_ref[...], preferred_element_type=F32
        ) + jnp.dot(g_ref[:, TOK:], t_ref[0], preferred_element_type=F32)
        for i, (_, parts) in enumerate(plan):

            @pl.when(step == i)
            def _(parts=parts):
                for out, to, start, rows in parts:
                    outs[out][to : to + rows, :] = term[start : start + rows, :].astype(
                        outs[out].dtype
                    )

    return pl.pallas_call(
        body,
        out_shape=outs,
        grid_spec=pltpu.PrefetchScalarGridSpec(
            num_scalar_prefetch=1,
            grid=(n,),
            in_specs=[
                whole((ROWS, 2 * TOK)),
                pl.BlockSpec((TOK, WIDE), lambda i, index: (0, index[0, i])),
                pl.BlockSpec((1, TOK, WIDE), lambda i, index: (index[1, i], 0, 0)),
            ],
            out_specs=[whole(o.shape) for o in outs],
            scratch_shapes=[pltpu.VMEM((ROWS, WIDE), F32)],
        ),
        compiler_params=params(),
        cost_estimate=pl.CostEstimate(
            flops=2 * n * ROWS * WIDE * 2 * TOK,
            bytes_accessed=2 * n * TOK * WIDE * 2,
            transcendentals=0,
        ),
    )(index, grad, hidden, theirs)


def statistics(partial, other, hit):
    def body(mine, theirs, hit_ref, logits, stats):
        total = mine[...] + jnp.concatenate([theirs[:, TOK:], theirs[:, :TOK]], axis=1)
        logits[...] = total
        top = jnp.max(total, axis=0, keepdims=True)
        stats[0:1, :] = top
        stats[1:2, :] = jnp.sum(jnp.exp(total - top), axis=0, keepdims=True)
        stats[2:3, :] = jnp.sum(total * hit_ref[...], axis=0, keepdims=True)

    outs = [
        jax.ShapeDtypeStruct((ROWS, 2 * TOK), F32),
        jax.ShapeDtypeStruct((3, 2 * TOK), F32),
    ]
    return local_call(body, outs, partial, other, hit)


def gradient(logits, hit, stats, lse_rest, cotangent):
    def body(logits_ref, hit_ref, s, rest, cot, loss, grad):
        top = s[0]
        row_max = jnp.max(top, axis=0, keepdims=True)
        row_total = jnp.sum(s[1] * jnp.exp(top - row_max), axis=0, keepdims=True)
        target_logit = jnp.sum(s[2], axis=0, keepdims=True)
        lse_window = row_max + jnp.log(row_total)
        larger = jnp.maximum(lse_window, rest[...])
        log_total = larger + jnp.log(
            jnp.exp(lse_window - larger) + jnp.exp(rest[...] - larger)
        )
        loss[...] = log_total - target_logit + z_weight * log_total * log_total
        softmax = jnp.exp(logits_ref[...] - log_total)
        grad[...] = (
            cot[...] * (softmax * (1.0 + 2.0 * z_weight * log_total) - hit_ref[...])
        ).astype(BF16)

    outs = [
        jax.ShapeDtypeStruct((1, 2 * TOK), F32),
        jax.ShapeDtypeStruct((ROWS, 2 * TOK), BF16),
    ]
    return local_call(body, outs, logits, hit, stats, lse_rest, cotangent)


def gathered_logits(head, hidden, theirs, at):
    zb, za = move(head[:PR], "zh", 1), move(head[:PR], "zh", -1)
    xb, xa = move(head, "x", 1), move(head, "x", -1)
    zf1, zf2 = move(zb[:PH], "zh", 1), move(za[PH:], "zh", -1)
    xf1, xf2 = move(xb[:RH], "x", 1), move(xa[RH:], "x", -1)
    p = jnp.concatenate([za, zb, zf1, zf2], axis=0)
    q = jnp.concatenate([head[PR:], xa[PR:], xb[PR:], xf2[PR - RH :]], axis=0)
    pb, pa = move(p, "x", 1), move(p, "x", -1)
    qb, qa = move(q, "zh", 1), move(q, "zh", -1)
    pf1, pf2 = move(pb[: 3 * PH], "x", 1), move(pa[3 * PH :], "x", -1)
    qf1, qf2 = move(qb[: 2 * QR], "zh", 1), move(qa[2 * QR :], "zh", -1)

    first = [
        (0, [(0, 0, ROWS, 0)]),
        (1, [(1, 0, ROWS, 0)]),
        (3, [(2, 0, ROWS, 0)]),
        (2, [(3, 0, RH, 0), (4, 0, RH, RH)]),
        (4, [(5, 0, PR, 0)]),
        (12, [(6, 0, PR, 0)]),
        (8, [(7, 0, PH, 0), (8, 0, PH, PH)]),
    ]
    total = add_logits(None, first, [head, xa, xb, xf1, xf2, za, zb, zf1, zf2], hidden, theirs, at)
    second = {slot: [] for slot in range(16)}
    for k, dz in enumerate((1, 3, 2)):
        second[dz * 4 + 1].append((0, k * PR, PR, 0))
        second[dz * 4 + 3].append((1, k * PR, PR, 0))
    for k, dx in enumerate((0, 1, 3, 2)):
        second[4 + dx].append((2, k * QR, QR, PR))
        second[12 + dx].append((3, k * QR, QR, PR))
    second = [(slot, parts) for slot, parts in second.items() if parts]
    total = add_logits(total, second, [pa, pb, qa, qb], hidden, theirs, at)
    third = [
        (4 + 2, [(0, 0, PR, 0)]),
        (12 + 2, [(0, PR, PH, 0), (1, 0, PH, PH)]),
        (8 + 2, [(1, PH, PR, 0), (3, QR, QR, PR)]),
        (8 + 0, [(2, 0, QR, PR)]),
        (8 + 1, [(2, QR, QR, PR)]),
        (8 + 3, [(3, 0, QR, PR)]),
    ]
    return add_logits(total, third, [pf1, pf2, qf1, qf2], hidden, theirs, at)


def scattered_gradient(grad, hidden, theirs, at):
    def array(rows, dtype):
        return jax.ShapeDtypeStruct((rows, WIDE), dtype)

    outs = [
        array(3 * PR, BF16),
        array(3 * PR, BF16),
        array(4 * QR, BF16),
        array(4 * QR, BF16),
        array(3 * PH, F32),
        array(3 * PH, F32),
        array(3 * PR, F32),
        array(4 * QH, F32),
        array(4 * QH, F32),
    ]
    plan = []
    for dz in (1, 2, 3):
        k = dz - 1
        for dx in range(4):
            parts = {
                0: [(6, k * PR, 0, PR)],
                1: [(4, k * PH, 0, PH), (0, k * PR + PH, PH, PH)],
                2: [(0, k * PR, 0, PH), (1, k * PR + PH, PH, PH)],
                3: [(1, k * PR, 0, PH), (5, k * PH, PH, PH)],
            }[dx]
            parts = parts + {
                1: [(7, dx * QH, PR, QH), (2, dx * QR + QH, PR + QH, QH)],
                2: [(2, dx * QR, PR, QH), (3, dx * QR + QH, PR + QH, QH)],
                3: [(3, dx * QR, PR, QH), (8, dx * QH, PR + QH, QH)],
            }[dz]
            plan.append((dz * 4 + dx, parts))
    p_up, p_down, q_up, q_down, p_ahead, p_behind, p_here, q_ahead, q_behind = gradient_terms(
        plan, outs, grad, hidden, theirs, at
    )
    p_up, p_down = move(p_up, "x", 1), move(p_down, "x", -1)
    q_up, q_down = move(q_up, "zh", 1), move(q_down, "zh", -1)
    outs = [array(4 * PR, F32), array(4 * QR, F32)]
    plan = [(dx, [(0, dx * PR, 0, PR), (1, dx * QR, PR, QR)]) for dx in range(4)]
    own, q_here = gradient_terms(plan, outs, grad, hidden, theirs, at)

    def forward(kept_ahead, kept_behind, up, down, n, half):
        def body(a, b, u, d, up_out, down_out):
            for k in range(n):
                to, first, last = k * half, 2 * k * half, (2 * k + 1) * half
                up_out[to : to + half, :] = (
                    a[to : to + half, :] + u[first : first + half, :].astype(F32)
                ).astype(BF16)
                down_out[to : to + half, :] = (
                    b[to : to + half, :] + d[last : last + half, :].astype(F32)
                ).astype(BF16)

        return local_call(
            body, [array(n * half, BF16)] * 2, kept_ahead, kept_behind, up, down
        )

    def settle(kept, up, down, up2, down2, n, half, k):
        to, first, last = k * half, 2 * k * half, (2 * k + 1) * half
        one = kept[first : first + half, :] + down[first : first + half, :].astype(F32)
        two = kept[last : last + half, :] + up[last : last + half, :].astype(F32)
        return (
            one + up2[to : to + half, :].astype(F32),
            two + down2[to : to + half, :].astype(F32),
        )

    p_up2, p_down2 = forward(p_ahead, p_behind, p_up, p_down, 3, PH)
    p_up2, p_down2 = move(p_up2, "x", 1), move(p_down2, "x", -1)
    q_up2, q_down2 = forward(q_ahead, q_behind, q_up, q_down, 4, QH)
    q_up2, q_down2 = move(q_up2, "zh", 1), move(q_down2, "zh", -1)

    def p_body(kept, up, down, up2, down2, up_out, down_out, ahead, behind):
        for dz in (1, 2, 3):
            one, two = settle(kept, up, down, up2, down2, 3, PH, dz - 1)
            if dz == 1:
                ahead[...] = one
                up_out[PH:, :] = two.astype(BF16)
            elif dz == 2:
                up_out[:PH, :] = one.astype(BF16)
                down_out[PH:, :] = two.astype(BF16)
            else:
                down_out[:PH, :] = one.astype(BF16)
                behind[...] = two

    z_up, z_down, z_ahead, z_behind = local_call(
        p_body,
        [array(PR, BF16), array(PR, BF16), array(PH, F32), array(PH, F32)],
        p_here, p_up, p_down, p_up2, p_down2,
    )
    z_up, z_down = move(z_up, "zh", 1), move(z_down, "zh", -1)

    def q_body(own, kept, up, down, up2, down2, up_out, down_out, ahead, behind, here):
        rest = PR - RH
        for dx in range(4):
            one, two = settle(kept, up, down, up2, down2, 4, QH, dx)
            first = own[dx * PR : dx * PR + RH, :]
            last = own[dx * PR + RH : (dx + 1) * PR, :]
            for ref, at_last, low in {
                0: ((here, RH, 0),),
                1: ((up_out, RH, 1),),
                2: ((down_out, RH, 1),),
                3: ((behind, 0, 0),),
            }[dx]:
                ref[at_last : at_last + rest, :] = last.astype(ref.dtype)
                ref[at_last + rest : at_last + rest + QH, :] = one.astype(ref.dtype)
                ref[at_last + rest + QH : at_last + RH, :] = two.astype(ref.dtype)
            ref = (here, ahead, up_out, down_out)[dx]
            ref[:RH, :] = first.astype(ref.dtype)

    x_up, x_down, x_ahead, x_behind, x_here = local_call(
        q_body,
        [array(ROWS, BF16), array(ROWS, BF16), array(RH, F32), array(RH, F32), array(ROWS, F32)],
        own, q_here, q_up, q_down, q_up2, q_down2,
    )
    x_up, x_down = move(x_up, "x", 1), move(x_down, "x", -1)

    z_up2, z_down2 = forward(z_ahead, z_behind, z_up, z_down, 1, PH)
    z_up2, z_down2 = move(z_up2, "zh", 1), move(z_down2, "zh", -1)
    x_up2, x_down2 = forward(x_ahead, x_behind, x_up, x_down, 1, RH)
    x_up2, x_down2 = move(x_up2, "x", 1), move(x_down2, "x", -1)

    def last_body(here, xu, xd, xu2, xd2, zu, zd, zu2, zd2, out):
        out[:RH, :] = here[:RH, :] + xd[:RH, :].astype(F32) + xu2[...].astype(F32)
        out[RH:, :] = here[RH:, :] + xu[RH:, :].astype(F32) + xd2[...].astype(F32)
        out[:PH, :] += zd[:PH, :].astype(F32) + zu2[...].astype(F32)
        out[PH:PR, :] += zu[PH:, :].astype(F32) + zd2[...].astype(F32)

    (out,) = local_call(
        last_body, [array(ROWS, F32)],
        x_here, x_up, x_down, x_up2, x_down2, z_up, z_down, z_up2, z_down2,
    )
    return out


def shards(hidden, head, targets, block_index, lse_rest, cotangent):
    zh, x, c = (lax.axis_index(a) for a in DP)
    first_row = lax.axis_index(TENSOR) * ROWS
    row_ids = first_row + lax.iota(jnp.int32, ROWS)
    block_of = row_ids // BLOCK
    block_match = (block_of[:, None] == lax.iota(jnp.int32, block_index.shape[0])[None, :]).astype(
        jnp.int32
    )
    vocab_ids = jnp.sum(block_match * block_index[None, :], axis=1) * BLOCK + row_ids % BLOCK

    k = lax.iota(jnp.int32, 16)
    at = (((zh + k // 4) % 4) * 4 + (x + k % 4) % 4) * 2
    theirs = move(pick(hidden, at + (1 - c)), "c", 1)
    at = at + c

    facts = jnp.stack([targets.astype(F32), lse_rest, cotangent])
    facts = jnp.concatenate([facts, move(facts, "c", 1)], axis=1)
    hit = (vocab_ids[:, None] == facts[0].astype(jnp.int32)[None, :]).astype(F32)

    partial = gathered_logits(head, hidden, theirs, at)
    logits, stats = statistics(partial, move(partial, "c", 1), hit)
    stats = lax.all_to_all(
        jnp.broadcast_to(stats[None], (8,) + stats.shape), TENSOR, split_axis=0, concat_axis=0, tiled=True
    )
    loss, grad = gradient(
        logits, hit, jnp.swapaxes(stats, 0, 1), facts[1:2], facts[2:3]
    )
    return loss[0, :TOK], scattered_gradient(grad, hidden, theirs, at)


def solution(mesh):
    mesh = Mesh(mesh.devices.reshape(SIZES), AXES)
    placed = (P(DP, None), P(TENSOR, DP), P(DP), P(), P(DP), P(DP))
    return jax.shard_map(
        shards, mesh=mesh, in_specs=placed, out_specs=(P(DP), P(TENSOR, DP)), check_vma=False
    )
```

```python
import jax
import jax.numpy as jnp
from jax import lax
from jax.experimental import pallas as pl
from jax.experimental.pallas import tpu as pltpu
from jax.sharding import Mesh
from jax.sharding import PartitionSpec as P

BLOCK = 1024
z_weight = 0.0001

AXES = ("zh", "x", "c", "zl", "y")
SIZES = (4, 4, 2, 2, 4)
DP = ("zh", "x", "c")
TENSOR = ("zl", "y")

ROWS = 256
TOK = 512
WIDE = 512
PR, QR = 192, 64

F32 = jnp.float32
BF16 = jnp.bfloat16
MIB = 1024 * 1024


def move(value, axis, by):
    n = SIZES[AXES.index(axis)]
    return lax.ppermute(value, axis, [(i, (i + by) % n) for i in range(n)])


def params(mib):
    return pltpu.CompilerParams(vmem_limit_bytes=mib * MIB)


def whole(shape):
    return pl.BlockSpec(shape, lambda: (0,) * len(shape))


def local_call(body, outs, *args):
    size = sum(a.size * a.dtype.itemsize for a in args) + sum(
        o.size * o.dtype.itemsize for o in outs
    )
    return pl.pallas_call(
        body,
        out_shape=outs,
        in_specs=[whole(a.shape) for a in args],
        out_specs=[whole(o.shape) for o in outs],
        compiler_params=params(16),
        cost_estimate=pl.CostEstimate(flops=0, bytes_accessed=size, transcendentals=0),
    )(*args)


def pick(hidden, at):
    n = at.shape[0]

    def body(at_ref, h_ref, o_ref, arrived):
        copies = [
            pltpu.make_async_copy(
                h_ref.at[:, pl.ds(pl.multiple_of(at_ref[k] * WIDE, WIDE), WIDE)],
                o_ref.at[k],
                arrived.at[k],
            )
            for k in range(n)
        ]
        for copy in copies:
            copy.start()
        for copy in copies:
            copy.wait()

    return pl.pallas_call(
        body,
        out_shape=jax.ShapeDtypeStruct((n, TOK, WIDE), BF16),
        in_specs=[
            pl.BlockSpec(memory_space=pltpu.SMEM),
            pl.BlockSpec(memory_space=pl.ANY),
        ],
        out_specs=pl.BlockSpec(memory_space=pltpu.VMEM),
        scratch_shapes=[pltpu.SemaphoreType.DMA((n,))],
        compiler_params=params(50),
        cost_estimate=pl.CostEstimate(
            flops=0, bytes_accessed=6 * n * TOK * WIDE * 2, transcendentals=0
        ),
    )(at, hidden)


def block_call(compute, plan, outs, mine, theirs, others, rows):
    n = len(plan)

    def body(m_ref, t0_ref, t1_ref, *refs):
        t_refs = (t0_ref, t1_ref)
        hold, arrived = refs[-2:]
        copies = [
            pltpu.make_async_copy(ref, hold.at[i, side], arrived.at[i, side])
            for i, (slot, _) in enumerate(plan)
            for side, ref in enumerate((m_ref.at[slot], t_refs[slot // 8].at[slot % 8]))
        ]
        for copy in copies:
            copy.start()
        for i, (_, parts) in enumerate(plan):
            copies[2 * i].wait()
            copies[2 * i + 1].wait()
            compute(i, parts, hold, refs[: len(others)], refs[len(others) : -2])

    return pl.pallas_call(
        body,
        out_shape=outs,
        in_specs=[pl.BlockSpec(memory_space=pl.ANY)] * 3 + [whole(o.shape) for o in others],
        out_specs=[whole(o.shape) for o in outs],
        scratch_shapes=[
            pltpu.VMEM((n, 2, TOK, WIDE), BF16),
            pltpu.SemaphoreType.DMA((n, 2)),
        ],
        compiler_params=params(50),
        cost_estimate=pl.CostEstimate(
            flops=4 * rows * WIDE * TOK,
            bytes_accessed=2 * n * TOK * WIDE * 2,
            transcendentals=0,
        ),
    )(mine, *theirs, *others)


def add_logits(total, plan, pieces, mine, theirs):
    has_total = total is not None

    def compute(i, parts, hold, refs, outs):
        (out,) = outs
        if i == 0:
            out[...] = refs[-1][...] if has_total else jnp.zeros_like(out)
        for piece, start, rows, to in parts:
            a = refs[piece][start : start + rows, :]
            for side in range(2):
                out[to : to + rows, side * TOK : (side + 1) * TOK] += lax.dot_general(
                    a, hold[i, side], (((1,), (1,)), ((), ())), preferred_element_type=F32
                )

    return block_call(
        compute,
        plan,
        [jax.ShapeDtypeStruct((ROWS, 2 * TOK), F32)],
        mine,
        theirs,
        list(pieces) + ([total] if has_total else []),
        sum(r for _, parts in plan for _, _, r, _ in parts),
    )[0]


def gradient_terms(plan, outs, grad, mine, theirs):
    def compute(i, parts, hold, refs, outs):
        (g_ref,) = refs
        term = jnp.dot(
            g_ref[:, :TOK], hold[i, 0], preferred_element_type=F32
        ) + jnp.dot(g_ref[:, TOK:], hold[i, 1], preferred_element_type=F32)
        for out, to, start, rows in parts:
            outs[out][to : to + rows, :] = term[start : start + rows, :].astype(
                outs[out].dtype
            )

    return block_call(compute, plan, outs, mine, theirs, [grad], len(plan) * ROWS)


def statistics(partial, other, hit):
    def body(mine, theirs, hit_ref, logits, stats):
        total = mine[...] + jnp.concatenate([theirs[:, TOK:], theirs[:, :TOK]], axis=1)
        logits[...] = total
        top = jnp.max(total, axis=0, keepdims=True)
        stats[0:1, :] = top
        stats[1:2, :] = jnp.sum(jnp.exp(total - top), axis=0, keepdims=True)
        stats[2:3, :] = jnp.sum(total * hit_ref[...], axis=0, keepdims=True)

    outs = [
        jax.ShapeDtypeStruct((ROWS, 2 * TOK), F32),
        jax.ShapeDtypeStruct((3, 2 * TOK), F32),
    ]
    return local_call(body, outs, partial, other, hit)


def gradient(logits, hit, stats, lse_rest, cotangent):
    def body(logits_ref, hit_ref, s, rest, cot, loss, grad):
        top = s[0]
        row_max = jnp.max(top, axis=0, keepdims=True)
        row_total = jnp.sum(s[1] * jnp.exp(top - row_max), axis=0, keepdims=True)
        target_logit = jnp.sum(s[2], axis=0, keepdims=True)
        lse_window = row_max + jnp.log(row_total)
        larger = jnp.maximum(lse_window, rest[...])
        log_total = larger + jnp.log(
            jnp.exp(lse_window - larger) + jnp.exp(rest[...] - larger)
        )
        loss[...] = log_total - target_logit + z_weight * log_total * log_total
        softmax = jnp.exp(logits_ref[...] - log_total)
        grad[...] = (
            cot[...] * (softmax * (1.0 + 2.0 * z_weight * log_total) - hit_ref[...])
        ).astype(BF16)

    outs = [
        jax.ShapeDtypeStruct((1, 2 * TOK), F32),
        jax.ShapeDtypeStruct((ROWS, 2 * TOK), BF16),
    ]
    return local_call(body, outs, logits, hit, stats, lse_rest, cotangent)


def gathered_logits(head, hidden, at, sibling_at):
    zb, za, zf = (move(head[:PR], "zh", by) for by in (1, -1, 2))
    xb, xa, xf = (move(head, "x", by) for by in (1, -1, 2))
    part = move(pick(hidden, sibling_at[:8]), "c", 1)
    zb, rest_at = lax.optimization_barrier((zb, sibling_at[8:]))
    theirs = (part, move(pick(hidden, rest_at), "c", 1))
    mine = pick(hidden, at)
    p = jnp.concatenate([za, zb, zf], axis=0)
    q = jnp.concatenate([head[PR:], xa[PR:], xb[PR:], xf[PR:]], axis=0)
    pb, pa, pf = (move(p, "x", by) for by in (1, -1, 2))
    qb, qa, qf = (move(q, "zh", by) for by in (1, -1, 2))

    first = [
        (0, [(0, 0, ROWS, 0)]),
        (1, [(1, 0, ROWS, 0)]),
        (3, [(2, 0, ROWS, 0)]),
        (2, [(3, 0, ROWS, 0)]),
        (4, [(4, 0, PR, 0)]),
        (12, [(5, 0, PR, 0)]),
        (8, [(6, 0, PR, 0)]),
    ]
    total = add_logits(None, first, [head, xa, xb, xf, za, zb, zf], mine, theirs)
    second = {slot: [] for slot in range(16)}
    third = {slot: [] for slot in range(16)}
    for k, dz in enumerate((1, 3, 2)):
        second[dz * 4 + 1].append((0, k * PR, PR, 0))
        second[dz * 4 + 3].append((1, k * PR, PR, 0))
        third[dz * 4 + 2].append((0, k * PR, PR, 0))
    for k, dx in enumerate((0, 1, 3, 2)):
        second[4 + dx].append((2, k * QR, QR, PR))
        second[12 + dx].append((3, k * QR, QR, PR))
        third[8 + dx].append((1, k * QR, QR, PR))
    second = [(slot, parts) for slot, parts in second.items() if parts]
    third = [(slot, parts) for slot, parts in third.items() if parts]
    total = add_logits(total, second, [pa, pb, qa, qb], mine, theirs)
    return add_logits(total, third, [pf, qf], mine, theirs), mine, theirs


def scattered_gradient(grad, mine, theirs):
    def array(rows, dtype):
        return jax.ShapeDtypeStruct((rows, WIDE), dtype)

    outs = [array(3 * PR, BF16)] * 3 + [array(3 * PR, F32)] + [array(4 * QR, BF16)] * 3
    plan = []
    for dz in (1, 2, 3):
        for dx in (1, 2, 3, 0):
            p_out = 3 if dx == 0 else dx - 1
            plan.append(
                (dz * 4 + dx, [(p_out, (dz - 1) * PR, 0, PR), (3 + dz, dx * QR, PR, QR)])
            )
    p1, p2, p3, p_here, q1, q2, q3 = gradient_terms(plan, outs, grad, mine, theirs)
    p1, p2, p3 = move(p1, "x", 1), move(p2, "x", 2), move(p3, "x", -1)
    q1, q2, q3 = move(q1, "zh", 1), move(q2, "zh", 2), move(q3, "zh", -1)
    outs = [array(4 * PR, F32), array(4 * QR, F32)]
    plan = [(dx, [(0, dx * PR, 0, PR), (1, dx * QR, PR, QR)]) for dx in range(4)]
    own, q_here = gradient_terms(plan, outs, grad, mine, theirs)

    def settle(kept, one, two, three, k, rows):
        at = pl.ds(k * rows, rows)
        return kept[at, :] + (
            one[at, :].astype(F32) + two[at, :].astype(F32) + three[at, :].astype(F32)
        )

    def p_body(kept, one, two, three, *outs):
        for k in range(3):
            outs[k][...] = settle(kept, one, two, three, k, PR).astype(BF16)

    z1, z2, z3 = local_call(p_body, [array(PR, BF16)] * 3, p_here, p1, p2, p3)
    z1, z2, z3 = move(z1, "zh", 1), move(z2, "zh", 2), move(z3, "zh", -1)

    def q_body(own, kept, one, two, three, *outs):
        for dx in range(4):
            out = outs[dx]
            out[:PR, :] = own[dx * PR : (dx + 1) * PR, :].astype(out.dtype)
            out[PR:, :] = settle(kept, one, two, three, dx, QR).astype(out.dtype)

    x_here, x1, x2, x3 = local_call(
        q_body, [array(ROWS, F32)] + [array(ROWS, BF16)] * 3, own, q_here, q1, q2, q3
    )
    x1, x2, x3 = move(x1, "x", 1), move(x2, "x", 2), move(x3, "x", -1)

    def last_body(here, x1, x2, x3, z1, z2, z3, out):
        out[...] = settle(here, x1, x2, x3, 0, ROWS)
        out[:PR, :] += z1[...].astype(F32) + z2[...].astype(F32) + z3[...].astype(F32)

    (out,) = local_call(last_body, [array(ROWS, F32)], x_here, x1, x2, x3, z1, z2, z3)
    return out


def shards(hidden, head, targets, block_index, lse_rest, cotangent):
    zh, x, c = (lax.axis_index(a) for a in DP)
    first_row = lax.axis_index(TENSOR) * ROWS
    row_ids = first_row + lax.iota(jnp.int32, ROWS)
    block_of = row_ids // BLOCK
    block_match = (block_of[:, None] == lax.iota(jnp.int32, block_index.shape[0])[None, :]).astype(
        jnp.int32
    )
    vocab_ids = jnp.sum(block_match * block_index[None, :], axis=1) * BLOCK + row_ids % BLOCK

    k = lax.iota(jnp.int32, 16)
    at = (((zh + k // 4) % 4) * 4 + (x + k % 4) % 4) * 2
    at, sibling_at = at + c, at + (1 - c)

    facts = jnp.stack([targets.astype(F32), lse_rest, cotangent])
    facts = jnp.concatenate([facts, move(facts, "c", 1)], axis=1)
    hit = (vocab_ids[:, None] == facts[0].astype(jnp.int32)[None, :]).astype(F32)

    partial, mine, theirs = gathered_logits(head, hidden, at, sibling_at)
    logits, stats = statistics(partial, move(partial, "c", 1), hit)
    stats = lax.all_to_all(
        jnp.broadcast_to(stats[None], (8,) + stats.shape), TENSOR, split_axis=0, concat_axis=0, tiled=True
    )
    loss, grad = gradient(
        logits, hit, jnp.swapaxes(stats, 0, 1), facts[1:2], facts[2:3]
    )
    return loss[0, :TOK], scattered_gradient(grad, mine, theirs)


def solution(mesh):
    mesh = Mesh(mesh.devices.reshape(SIZES), AXES)
    placed = (P(DP, None), P(TENSOR, DP), P(DP), P(), P(DP), P(DP))
    return jax.shard_map(
        shards, mesh=mesh, in_specs=placed, out_specs=(P(DP), P(TENSOR, DP)), check_vma=False
    )
```

```python
import jax
import jax.numpy as jnp
from jax import lax
from jax.experimental import pallas as pl
from jax.experimental.pallas import tpu as pltpu
from jax.sharding import Mesh
from jax.sharding import PartitionSpec as P

BLOCK = 1024
z_weight = 0.0001

AXES = ("zh", "x", "c", "zl", "y")
SIZES = (4, 4, 2, 2, 4)
DP = ("zh", "x", "c")
TENSOR = ("zl", "y")

ROWS = 256
TOK = 512
WIDE = 512
PR, QR = 192, 64
PH, QH, RH = PR // 2, QR // 2, ROWS // 2

F32 = jnp.float32
BF16 = jnp.bfloat16
MIB = 1024 * 1024


def move(value, axis, by):
    n = SIZES[AXES.index(axis)]
    return lax.ppermute(value, axis, [(i, (i + by) % n) for i in range(n)])


def params(mib):
    return pltpu.CompilerParams(vmem_limit_bytes=mib * MIB)


def whole(shape):
    return pl.BlockSpec(shape, lambda: (0,) * len(shape))


def local_call(body, outs, *args):
    size = sum(a.size * a.dtype.itemsize for a in args) + sum(
        o.size * o.dtype.itemsize for o in outs
    )
    return pl.pallas_call(
        body,
        out_shape=outs,
        in_specs=[whole(a.shape) for a in args],
        out_specs=[whole(o.shape) for o in outs],
        compiler_params=params(16),
        cost_estimate=pl.CostEstimate(flops=0, bytes_accessed=size, transcendentals=0),
    )(*args)


def pick(hidden, at):
    n = at.shape[0]

    def body(at_ref, h_ref, o_ref, arrived):
        copies = [
            pltpu.make_async_copy(
                h_ref.at[:, pl.ds(pl.multiple_of(at_ref[k] * WIDE, WIDE), WIDE)],
                o_ref.at[k],
                arrived.at[k],
            )
            for k in range(n)
        ]
        for copy in copies:
            copy.start()
        for copy in copies:
            copy.wait()

    return pl.pallas_call(
        body,
        out_shape=jax.ShapeDtypeStruct((n, TOK, WIDE), BF16),
        in_specs=[
            pl.BlockSpec(memory_space=pltpu.SMEM),
            pl.BlockSpec(memory_space=pl.ANY),
        ],
        out_specs=pl.BlockSpec(memory_space=pltpu.VMEM),
        scratch_shapes=[pltpu.SemaphoreType.DMA((n,))],
        compiler_params=params(50),
        cost_estimate=pl.CostEstimate(
            flops=0, bytes_accessed=2 * n * TOK * WIDE * 2, transcendentals=0
        ),
    )(at, hidden)


def block_call(compute, plan, outs, blocks, others, rows):
    n = len(plan)
    at, hidden, theirs = blocks

    def body(at_ref, h_ref, t_ref, *refs):
        hold, arrived = refs[-2:]

        def sources(slot):
            start = pl.multiple_of(at_ref[slot] * WIDE, WIDE)
            return h_ref.at[:, pl.ds(start, WIDE)], t_ref.at[slot]

        copies = [
            pltpu.make_async_copy(ref, hold.at[i, side], arrived.at[i, side])
            for i, (slot, _) in enumerate(plan)
            for side, ref in enumerate(sources(slot))
        ]
        for copy in copies:
            copy.start()
        for i, (_, parts) in enumerate(plan):
            copies[2 * i].wait()
            copies[2 * i + 1].wait()
            compute(i, parts, hold, refs[: len(others)], refs[len(others) : -2])

    return pl.pallas_call(
        body,
        out_shape=outs,
        in_specs=[pl.BlockSpec(memory_space=pltpu.SMEM)]
        + [pl.BlockSpec(memory_space=pl.ANY)] * 2
        + [whole(o.shape) for o in others],
        out_specs=[whole(o.shape) for o in outs],
        scratch_shapes=[
            pltpu.VMEM((n, 2, TOK, WIDE), BF16),
            pltpu.SemaphoreType.DMA((n, 2)),
        ],
        compiler_params=params(50),
        cost_estimate=pl.CostEstimate(
            flops=4 * rows * WIDE * TOK,
            bytes_accessed=2 * n * TOK * WIDE * 2,
            transcendentals=0,
        ),
    )(at, hidden, theirs, *others)


def add_logits(total, plan, pieces, blocks):
    has_total = total is not None

    def compute(i, parts, hold, refs, outs):
        (out,) = outs
        if i == 0:
            out[...] = refs[-1][...] if has_total else jnp.zeros_like(out)
        for piece, start, rows, to in parts:
            a = refs[piece][start : start + rows, :]
            for side in range(2):
                out[to : to + rows, side * TOK : (side + 1) * TOK] += lax.dot_general(
                    a, hold[i, side], (((1,), (1,)), ((), ())), preferred_element_type=F32
                )

    return block_call(
        compute,
        plan,
        [jax.ShapeDtypeStruct((ROWS, 2 * TOK), F32)],
        blocks,
        list(pieces) + ([total] if has_total else []),
        sum(r for _, parts in plan for _, _, r, _ in parts),
    )[0]


def gradient_terms(plan, outs, grad, blocks):
    def compute(i, parts, hold, refs, outs):
        (g_ref,) = refs
        term = jnp.dot(
            g_ref[:, :TOK], hold[i, 0], preferred_element_type=F32
        ) + jnp.dot(g_ref[:, TOK:], hold[i, 1], preferred_element_type=F32)
        for out, to, start, rows in parts:
            outs[out][to : to + rows, :] = term[start : start + rows, :].astype(
                outs[out].dtype
            )

    return block_call(compute, plan, outs, blocks, [grad], len(plan) * ROWS)


def statistics(partial, other, hit):
    def body(mine, theirs, hit_ref, logits, stats):
        total = mine[...] + jnp.concatenate([theirs[:, TOK:], theirs[:, :TOK]], axis=1)
        logits[...] = total
        top = jnp.max(total, axis=0, keepdims=True)
        stats[0:1, :] = top
        stats[1:2, :] = jnp.sum(jnp.exp(total - top), axis=0, keepdims=True)
        stats[2:3, :] = jnp.sum(total * hit_ref[...], axis=0, keepdims=True)

    outs = [
        jax.ShapeDtypeStruct((ROWS, 2 * TOK), F32),
        jax.ShapeDtypeStruct((3, 2 * TOK), F32),
    ]
    return local_call(body, outs, partial, other, hit)


def gradient(logits, hit, stats, lse_rest, cotangent):
    def body(logits_ref, hit_ref, s, rest, cot, loss, grad):
        top = s[0]
        row_max = jnp.max(top, axis=0, keepdims=True)
        row_total = jnp.sum(s[1] * jnp.exp(top - row_max), axis=0, keepdims=True)
        target_logit = jnp.sum(s[2], axis=0, keepdims=True)
        lse_window = row_max + jnp.log(row_total)
        larger = jnp.maximum(lse_window, rest[...])
        log_total = larger + jnp.log(
            jnp.exp(lse_window - larger) + jnp.exp(rest[...] - larger)
        )
        loss[...] = log_total - target_logit + z_weight * log_total * log_total
        softmax = jnp.exp(logits_ref[...] - log_total)
        grad[...] = (
            cot[...] * (softmax * (1.0 + 2.0 * z_weight * log_total) - hit_ref[...])
        ).astype(BF16)

    outs = [
        jax.ShapeDtypeStruct((1, 2 * TOK), F32),
        jax.ShapeDtypeStruct((ROWS, 2 * TOK), BF16),
    ]
    return local_call(body, outs, logits, hit, stats, lse_rest, cotangent)


def gathered_logits(head, hidden, at, sibling_at):
    zb, za = move(head[:PR], "zh", 1), move(head[:PR], "zh", -1)
    xb, xa = move(head, "x", 1), move(head, "x", -1)
    theirs = move(pick(hidden, sibling_at), "c", 1)
    zf1, zf2 = move(zb[:PH], "zh", 1), move(za[PH:], "zh", -1)
    xf1, xf2 = move(xb[:RH], "x", 1), move(xa[RH:], "x", -1)
    zf1, zf2, xf1, xf2 = lax.optimization_barrier((zf1, zf2, xf1, xf2))
    p = jnp.concatenate([za, zb, zf1, zf2], axis=0)
    q = jnp.concatenate([head[PR:], xa[PR:], xb[PR:], xf2[PR - RH :]], axis=0)
    pb, pa = move(p, "x", 1), move(p, "x", -1)
    qb, qa = move(q, "zh", 1), move(q, "zh", -1)
    pf1, pf2 = move(pb[: 3 * PH], "x", 1), move(pa[3 * PH :], "x", -1)
    qf1, qf2 = move(qb[: 2 * QR], "zh", 1), move(qa[2 * QR :], "zh", -1)

    blocks = (at, hidden, theirs)
    first = [
        (0, [(0, 0, ROWS, 0)]),
        (1, [(1, 0, ROWS, 0)]),
        (3, [(2, 0, ROWS, 0)]),
        (2, [(3, 0, RH, 0), (4, 0, RH, RH)]),
        (4, [(5, 0, PR, 0)]),
        (12, [(6, 0, PR, 0)]),
        (8, [(7, 0, PH, 0), (8, 0, PH, PH)]),
    ]
    total = add_logits(None, first, [head, xa, xb, xf1, xf2, za, zb, zf1, zf2], blocks)
    second = {slot: [] for slot in range(16)}
    for k, dz in enumerate((1, 3, 2)):
        second[dz * 4 + 1].append((0, k * PR, PR, 0))
        second[dz * 4 + 3].append((1, k * PR, PR, 0))
    for k, dx in enumerate((0, 1, 3, 2)):
        second[4 + dx].append((2, k * QR, QR, PR))
        second[12 + dx].append((3, k * QR, QR, PR))
    second = [(slot, parts) for slot, parts in second.items() if parts]
    total = add_logits(total, second, [pa, pb, qa, qb], blocks)
    third = [
        (4 + 2, [(0, 0, PR, 0)]),
        (12 + 2, [(0, PR, PH, 0), (1, 0, PH, PH)]),
        (8 + 2, [(1, PH, PR, 0), (3, QR, QR, PR)]),
        (8 + 0, [(2, 0, QR, PR)]),
        (8 + 1, [(2, QR, QR, PR)]),
        (8 + 3, [(3, 0, QR, PR)]),
    ]
    return add_logits(total, third, [pf1, pf2, qf1, qf2], blocks), blocks


def scattered_gradient(grad, blocks):
    def array(rows, dtype):
        return jax.ShapeDtypeStruct((rows, WIDE), dtype)

    outs = [
        array(3 * PR, BF16),
        array(3 * PR, BF16),
        array(4 * QR, BF16),
        array(4 * QR, BF16),
        array(3 * PH, F32),
        array(3 * PH, F32),
        array(3 * PR, F32),
        array(4 * QH, F32),
        array(4 * QH, F32),
    ]
    plan = []
    for dz in (1, 2, 3):
        k = dz - 1
        for dx in range(4):
            parts = {
                0: [(6, k * PR, 0, PR)],
                1: [(4, k * PH, 0, PH), (0, k * PR + PH, PH, PH)],
                2: [(0, k * PR, 0, PH), (1, k * PR + PH, PH, PH)],
                3: [(1, k * PR, 0, PH), (5, k * PH, PH, PH)],
            }[dx]
            parts = parts + {
                1: [(7, dx * QH, PR, QH), (2, dx * QR + QH, PR + QH, QH)],
                2: [(2, dx * QR, PR, QH), (3, dx * QR + QH, PR + QH, QH)],
                3: [(3, dx * QR, PR, QH), (8, dx * QH, PR + QH, QH)],
            }[dz]
            plan.append((dz * 4 + dx, parts))
    p_up, p_down, q_up, q_down, p_ahead, p_behind, p_here, q_ahead, q_behind = gradient_terms(
        plan, outs, grad, blocks
    )
    p_up, p_down = move(p_up, "x", 1), move(p_down, "x", -1)
    q_up, q_down = move(q_up, "zh", 1), move(q_down, "zh", -1)
    outs = [array(4 * PR, F32), array(4 * QR, F32)]
    plan = [(dx, [(0, dx * PR, 0, PR), (1, dx * QR, PR, QR)]) for dx in range(4)]
    own, q_here = gradient_terms(plan, outs, grad, blocks)

    def forward(kept_ahead, kept_behind, up, down, n, half):
        def body(a, b, u, d, up_out, down_out):
            for k in range(n):
                to, first, last = k * half, 2 * k * half, (2 * k + 1) * half
                up_out[to : to + half, :] = (
                    a[to : to + half, :] + u[first : first + half, :].astype(F32)
                ).astype(BF16)
                down_out[to : to + half, :] = (
                    b[to : to + half, :] + d[last : last + half, :].astype(F32)
                ).astype(BF16)

        return local_call(
            body, [array(n * half, BF16)] * 2, kept_ahead, kept_behind, up, down
        )

    def settle(kept, up, down, up2, down2, n, half, k):
        to, first, last = k * half, 2 * k * half, (2 * k + 1) * half
        one = kept[first : first + half, :] + down[first : first + half, :].astype(F32)
        two = kept[last : last + half, :] + up[last : last + half, :].astype(F32)
        return (
            one + up2[to : to + half, :].astype(F32),
            two + down2[to : to + half, :].astype(F32),
        )

    p_up2, p_down2 = forward(p_ahead, p_behind, p_up, p_down, 3, PH)
    p_up2, p_down2 = move(p_up2, "x", 1), move(p_down2, "x", -1)
    q_up2, q_down2 = forward(q_ahead, q_behind, q_up, q_down, 4, QH)
    q_up2, q_down2 = move(q_up2, "zh", 1), move(q_down2, "zh", -1)

    def p_body(kept, up, down, up2, down2, up_out, down_out, ahead, behind):
        for dz in (1, 2, 3):
            one, two = settle(kept, up, down, up2, down2, 3, PH, dz - 1)
            if dz == 1:
                ahead[...] = one
                up_out[PH:, :] = two.astype(BF16)
            elif dz == 2:
                up_out[:PH, :] = one.astype(BF16)
                down_out[PH:, :] = two.astype(BF16)
            else:
                down_out[:PH, :] = one.astype(BF16)
                behind[...] = two

    z_up, z_down, z_ahead, z_behind = local_call(
        p_body,
        [array(PR, BF16), array(PR, BF16), array(PH, F32), array(PH, F32)],
        p_here, p_up, p_down, p_up2, p_down2,
    )
    z_up, z_down = move(z_up, "zh", 1), move(z_down, "zh", -1)

    def q_body(own, kept, up, down, up2, down2, up_out, down_out, ahead, behind, here):
        rest = PR - RH
        for dx in range(4):
            one, two = settle(kept, up, down, up2, down2, 4, QH, dx)
            first = own[dx * PR : dx * PR + RH, :]
            last = own[dx * PR + RH : (dx + 1) * PR, :]
            for ref, at_last, low in {
                0: ((here, RH, 0),),
                1: ((up_out, RH, 1),),
                2: ((down_out, RH, 1),),
                3: ((behind, 0, 0),),
            }[dx]:
                ref[at_last : at_last + rest, :] = last.astype(ref.dtype)
                ref[at_last + rest : at_last + rest + QH, :] = one.astype(ref.dtype)
                ref[at_last + rest + QH : at_last + RH, :] = two.astype(ref.dtype)
            ref = (here, ahead, up_out, down_out)[dx]
            ref[:RH, :] = first.astype(ref.dtype)

    x_up, x_down, x_ahead, x_behind, x_here = local_call(
        q_body,
        [array(ROWS, BF16), array(ROWS, BF16), array(RH, F32), array(RH, F32), array(ROWS, F32)],
        own, q_here, q_up, q_down, q_up2, q_down2,
    )
    x_up, x_down = move(x_up, "x", 1), move(x_down, "x", -1)

    z_up2, z_down2 = forward(z_ahead, z_behind, z_up, z_down, 1, PH)
    z_up2, z_down2 = move(z_up2, "zh", 1), move(z_down2, "zh", -1)
    x_up2, x_down2 = forward(x_ahead, x_behind, x_up, x_down, 1, RH)
    x_up2, x_down2 = move(x_up2, "x", 1), move(x_down2, "x", -1)

    def last_body(here, xu, xd, xu2, xd2, zu, zd, zu2, zd2, out):
        out[:RH, :] = here[:RH, :] + xd[:RH, :].astype(F32) + xu2[...].astype(F32)
        out[RH:, :] = here[RH:, :] + xu[RH:, :].astype(F32) + xd2[...].astype(F32)
        out[:PH, :] += zd[:PH, :].astype(F32) + zu2[...].astype(F32)
        out[PH:PR, :] += zu[PH:, :].astype(F32) + zd2[...].astype(F32)

    (out,) = local_call(
        last_body, [array(ROWS, F32)],
        x_here, x_up, x_down, x_up2, x_down2, z_up, z_down, z_up2, z_down2,
    )
    return out


def shards(hidden, head, targets, block_index, lse_rest, cotangent):
    zh, x, c = (lax.axis_index(a) for a in DP)
    first_row = lax.axis_index(TENSOR) * ROWS
    row_ids = first_row + lax.iota(jnp.int32, ROWS)
    block_of = row_ids // BLOCK
    block_match = (block_of[:, None] == lax.iota(jnp.int32, block_index.shape[0])[None, :]).astype(
        jnp.int32
    )
    vocab_ids = jnp.sum(block_match * block_index[None, :], axis=1) * BLOCK + row_ids % BLOCK

    k = lax.iota(jnp.int32, 16)
    at = (((zh + k // 4) % 4) * 4 + (x + k % 4) % 4) * 2
    at, sibling_at = at + c, at + (1 - c)

    facts = jnp.stack([targets.astype(F32), lse_rest, cotangent])
    facts = jnp.concatenate([facts, move(facts, "c", 1)], axis=1)
    hit = (vocab_ids[:, None] == facts[0].astype(jnp.int32)[None, :]).astype(F32)

    partial, blocks = gathered_logits(head, hidden, at, sibling_at)
    logits, stats = statistics(partial, move(partial, "c", 1), hit)
    stats = lax.all_to_all(
        jnp.broadcast_to(stats[None], (8,) + stats.shape), TENSOR, split_axis=0, concat_axis=0, tiled=True
    )
    loss, grad = gradient(
        logits, hit, jnp.swapaxes(stats, 0, 1), facts[1:2], facts[2:3]
    )
    return loss[0, :TOK], scattered_gradient(grad, blocks)


def solution(mesh):
    mesh = Mesh(mesh.devices.reshape(SIZES), AXES)
    placed = (P(DP, None), P(TENSOR, DP), P(DP), P(), P(DP), P(DP))
    return jax.shard_map(
        shards, mesh=mesh, in_specs=placed, out_specs=(P(DP), P(TENSOR, DP)), check_vma=False
    )
```

```python
import jax
import jax.numpy as jnp
from jax import lax
from jax.experimental import pallas as pl
from jax.experimental.pallas import tpu as pltpu
from jax.sharding import Mesh
from jax.sharding import PartitionSpec as P

BLOCK = 1024
z_weight = 0.0001

AXES = ("zh", "x", "c", "zl", "y")
SIZES = (4, 4, 2, 2, 4)
DP = ("zh", "x", "c")
TENSOR = ("zl", "y")

ROWS = 256
TOK = 512
WIDE = 512
PR, QR = 192, 64
PH, QH, RH = PR // 2, QR // 2, ROWS // 2

F32 = jnp.float32
BF16 = jnp.bfloat16
MIB = 1024 * 1024


def move(value, axis, by):
    n = SIZES[AXES.index(axis)]
    return lax.ppermute(value, axis, [(i, (i + by) % n) for i in range(n)])


def params(mib):
    return pltpu.CompilerParams(vmem_limit_bytes=mib * MIB)


def whole(shape):
    return pl.BlockSpec(shape, lambda: (0,) * len(shape))


def local_call(body, outs, *args):
    size = sum(a.size * a.dtype.itemsize for a in args) + sum(
        o.size * o.dtype.itemsize for o in outs
    )
    return pl.pallas_call(
        body,
        out_shape=outs,
        in_specs=[whole(a.shape) for a in args],
        out_specs=[whole(o.shape) for o in outs],
        compiler_params=params(16),
        cost_estimate=pl.CostEstimate(flops=0, bytes_accessed=size, transcendentals=0),
    )(*args)


def pick(hidden, at):
    n = at.shape[0]

    def body(at_ref, h_ref, o_ref, arrived):
        copies = [
            pltpu.make_async_copy(
                h_ref.at[:, pl.ds(pl.multiple_of(at_ref[k] * WIDE, WIDE), WIDE)],
                o_ref.at[k],
                arrived.at[k],
            )
            for k in range(n)
        ]
        for copy in copies:
            copy.start()
        for copy in copies:
            copy.wait()

    return pl.pallas_call(
        body,
        out_shape=jax.ShapeDtypeStruct((n, TOK, WIDE), BF16),
        in_specs=[
            pl.BlockSpec(memory_space=pltpu.SMEM),
            pl.BlockSpec(memory_space=pl.ANY),
        ],
        out_specs=pl.BlockSpec(memory_space=pltpu.VMEM),
        scratch_shapes=[pltpu.SemaphoreType.DMA((n,))],
        compiler_params=params(50),
        cost_estimate=pl.CostEstimate(
            flops=0, bytes_accessed=2 * n * TOK * WIDE * 2, transcendentals=0
        ),
    )(at, hidden)


def block_call(compute, slots, outs, blocks, others, rows):
    at, hidden, theirs = blocks
    places = max(slots) + 1

    def body(at_ref, h_ref, t_ref, *refs):
        hold, arrived = refs[-2:]

        def copies(place, slot):
            start = pl.multiple_of(at_ref[slot] * WIDE, WIDE)
            for side, ref in enumerate((h_ref.at[:, pl.ds(start, WIDE)], t_ref.at[slot])):
                yield pltpu.make_async_copy(
                    ref, hold.at[place, pl.ds(side * TOK, TOK)], arrived.at[place, side]
                )

        for place, slot in slots.items():
            for copy in copies(place, slot):
                copy.start()

        def block(place, wait=True):
            if wait:
                for copy in copies(place, 0):
                    copy.wait()
            return hold[place]

        compute(block, refs[: len(others)], refs[len(others) : -2])

    return pl.pallas_call(
        body,
        out_shape=outs,
        in_specs=[pl.BlockSpec(memory_space=pltpu.SMEM)]
        + [pl.BlockSpec(memory_space=pl.ANY)] * 2
        + [whole(o.shape) for o in others],
        out_specs=[whole(o.shape) for o in outs],
        scratch_shapes=[
            pltpu.VMEM((places, 2 * TOK, WIDE), BF16),
            pltpu.SemaphoreType.DMA((places, 2)),
        ],
        compiler_params=params(50),
        cost_estimate=pl.CostEstimate(
            flops=4 * rows * WIDE * TOK,
            bytes_accessed=2 * len(slots) * TOK * WIDE * 2,
            transcendentals=0,
        ),
    )(at, hidden, theirs, *others)


def times(a, block):
    return lax.dot_general(a, block, (((1,), (1,)), ((), ())), preferred_element_type=F32)


def rows_at(k, size):
    return pl.ds(pl.multiple_of(k * size, size), size)


LOGITS = jax.ShapeDtypeStruct((ROWS, 2 * TOK), F32)
AHEAD = (1, 3, 2)


def statistics(partial, other, hit):
    def body(mine, theirs, hit_ref, logits, stats):
        total = mine[...] + jnp.concatenate([theirs[:, TOK:], theirs[:, :TOK]], axis=1)
        logits[...] = total
        top = jnp.max(total, axis=0, keepdims=True)
        stats[0:1, :] = top
        stats[1:2, :] = jnp.sum(jnp.exp(total - top), axis=0, keepdims=True)
        stats[2:3, :] = jnp.sum(total * hit_ref[...], axis=0, keepdims=True)

    outs = [
        jax.ShapeDtypeStruct((ROWS, 2 * TOK), F32),
        jax.ShapeDtypeStruct((3, 2 * TOK), F32),
    ]
    return local_call(body, outs, partial, other, hit)


def gradient(logits, hit, stats, lse_rest, cotangent):
    def body(logits_ref, hit_ref, s, rest, cot, loss, grad):
        top = s[0]
        row_max = jnp.max(top, axis=0, keepdims=True)
        row_total = jnp.sum(s[1] * jnp.exp(top - row_max), axis=0, keepdims=True)
        target_logit = jnp.sum(s[2], axis=0, keepdims=True)
        lse_window = row_max + jnp.log(row_total)
        larger = jnp.maximum(lse_window, rest[...])
        log_total = larger + jnp.log(
            jnp.exp(lse_window - larger) + jnp.exp(rest[...] - larger)
        )
        loss[...] = log_total - target_logit + z_weight * log_total * log_total
        softmax = jnp.exp(logits_ref[...] - log_total)
        grad[...] = (
            cot[...] * (softmax * (1.0 + 2.0 * z_weight * log_total) - hit_ref[...])
        ).astype(BF16)

    outs = [
        jax.ShapeDtypeStruct((1, 2 * TOK), F32),
        jax.ShapeDtypeStruct((ROWS, 2 * TOK), BF16),
    ]
    return local_call(body, outs, logits, hit, stats, lse_rest, cotangent)


def gathered_logits(head, hidden, at, sibling_at):
    zb, za = move(head[:PR], "zh", 1), move(head[:PR], "zh", -1)
    xb, xa = move(head, "x", 1), move(head, "x", -1)
    picked = pick(hidden, sibling_at)
    zb, za, xb, xa, picked = lax.optimization_barrier((zb, za, xb, xa, picked))
    theirs = move(picked, "c", 1)
    zf1, zf2 = move(zb[:PH], "zh", 1), move(za[PH:], "zh", -1)
    xf1, xf2 = move(xb[:RH], "x", 1), move(xa[RH:], "x", -1)
    zf1, zf2, xf1, xf2 = lax.optimization_barrier((zf1, zf2, xf1, xf2))
    p = jnp.concatenate([za, zb, zf1, zf2], axis=0)
    q = jnp.concatenate([head[PR:], xa[PR:], xb[PR:], xf2[PR - RH :]], axis=0)
    pb, pa = move(p, "x", 1), move(p, "x", -1)
    qb, qa = move(q, "zh", 1), move(q, "zh", -1)
    blocks = (at, hidden, theirs)

    def first(block, refs, outs):
        (out,) = outs
        head_ref, xa_ref, xb_ref, xf1_ref, xf2_ref, p_ref = refs
        out[...] = times(head_ref[...], block(0))
        out[...] += times(xa_ref[...], block(1))
        out[...] += times(xb_ref[...], block(2))
        far = block(3)
        out[:RH, :] += times(xf1_ref[...], far)
        out[RH:, :] += times(xf2_ref[...], far)

        @pl.loop(0, 3)
        def _(k):
            out[:PR, :] += times(p_ref[rows_at(k, PR), :], block(4 + k))

    slots = {0: 0, 1: 1, 2: 3, 3: 2} | {4 + k: 4 * dz for k, dz in enumerate(AHEAD)}
    (total,) = block_call(
        first, slots, [LOGITS], blocks, [head, xa, xb, xf1, xf2, p], 4 * ROWS + 3 * PR
    )
    pb, pa, qb, qa, total = lax.optimization_barrier((pb, pa, qb, qa, total))
    pf1, pf2 = move(pb[: 3 * PH], "x", 1), move(pa[3 * PH :], "x", -1)
    qf1, qf2 = move(qb[: 2 * QR], "zh", 1), move(qa[2 * QR :], "zh", -1)

    places = {4 * i + j: 4 * dz + dx for i, dz in enumerate(AHEAD) for j, dx in enumerate((0,) + AHEAD)}

    def second(block, refs, outs):
        (out,) = outs
        pa_ref, pb_ref, qa_ref, qb_ref, total_ref = refs
        out[...] = total_ref[...]

        @pl.loop(0, 3)
        def _(k):
            part = rows_at(k, PR)
            out[:PR, :] += times(pa_ref[part, :], block(4 * k + 1))
            out[:PR, :] += times(pb_ref[part, :], block(4 * k + 2))

        for j in range(4):
            new = j in (0, 3)
            part = slice(j * QR, (j + 1) * QR)
            out[PR:, :] += times(qa_ref[part, :], block(j, new))
            out[PR:, :] += times(qb_ref[part, :], block(4 + j, new))

    slots = {k: v for k, v in places.items() if k not in (8, 11)}
    (total,) = block_call(
        second, slots, [LOGITS], blocks, [pa, pb, qa, qb, total], 6 * PR + 8 * QR
    )

    def third(block, refs, outs):
        (out,) = outs
        pf1_ref, pf2_ref, qf1_ref, qf2_ref, total_ref = refs
        out[...] = total_ref[...]
        out[:PR, :] += times(pf1_ref[:PR, :], block(3))
        middle = block(7)
        out[:PH, :] += times(pf1_ref[PR:, :], middle)
        out[PH:PR, :] += times(pf2_ref[:PH, :], middle)
        out[:PR, :] += times(pf2_ref[PH:, :], block(11))
        out[PR:, :] += times(qf1_ref[:QR, :], block(8))
        out[PR:, :] += times(qf1_ref[QR:, :], block(9))
        out[PR:, :] += times(qf2_ref[:QR, :], block(10))
        out[PR:, :] += times(qf2_ref[QR:, :], block(11, False))

    slots = {k: places[k] for k in (3, 7, 8, 9, 10, 11)}
    (total,) = block_call(
        third, slots, [LOGITS], blocks, [pf1, pf2, qf1, qf2, total], 3 * PR + 4 * QR
    )
    return total, blocks


def scattered_gradient(grad, blocks):
    def array(rows, dtype):
        return jax.ShapeDtypeStruct((rows, WIDE), dtype)

    outs = [
        array(3 * PR, BF16),
        array(3 * PR, BF16),
        array(4 * QR, BF16),
        array(4 * QR, BF16),
        array(3 * PH, F32),
        array(3 * PH, F32),
        array(3 * PR, F32),
        array(4 * QH, F32),
        array(4 * QH, F32),
    ]
    def others_terms(block, refs, outs):
        (g_ref,) = refs
        p_up, p_down, q_up, q_down, p_ahead, p_behind, p_here, q_ahead, q_behind = outs

        @pl.loop(0, 3)
        def _(k):
            first, last = pl.ds(pl.multiple_of(k * PR, PR), PH), pl.ds(pl.multiple_of(k * PR + PH, PH), PH)
            kept = rows_at(k, PH)
            for dx in range(4):
                term = jnp.dot(g_ref[...], block(4 * k + dx), preferred_element_type=F32)
                one, two, three, four = term[:PH], term[PH:PR], term[PR : PR + QH], term[PR + QH :]
                if dx == 0:
                    p_here[rows_at(k, PR), :] = term[:PR]
                elif dx == 1:
                    p_ahead[kept, :] = one
                    p_up[last, :] = two.astype(BF16)
                elif dx == 2:
                    p_up[first, :] = one.astype(BF16)
                    p_down[last, :] = two.astype(BF16)
                else:
                    p_down[first, :] = one.astype(BF16)
                    p_behind[kept, :] = two
                start, middle = dx * QR, dx * QR + QH

                @pl.when(k == 0)
                def _():
                    q_ahead[dx * QH : (dx + 1) * QH, :] = three
                    q_up[middle : middle + QH, :] = four.astype(BF16)

                @pl.when(k == 1)
                def _():
                    q_up[start:middle, :] = three.astype(BF16)
                    q_down[middle : middle + QH, :] = four.astype(BF16)

                @pl.when(k == 2)
                def _():
                    q_down[start:middle, :] = three.astype(BF16)
                    q_behind[dx * QH : (dx + 1) * QH, :] = four

    slots = {place: 4 + place for place in range(12)}
    p_up, p_down, q_up, q_down, p_ahead, p_behind, p_here, q_ahead, q_behind = block_call(
        others_terms, slots, outs, blocks, [grad], 12 * ROWS
    )
    p_up, p_down = move(p_up, "x", 1), move(p_down, "x", -1)
    q_up, q_down = move(q_up, "zh", 1), move(q_down, "zh", -1)
    def own_terms(block, refs, outs):
        (g_ref,) = refs
        own, q_here = outs

        @pl.loop(0, 4)
        def _(dx):
            term = jnp.dot(g_ref[...], block(dx), preferred_element_type=F32)
            own[rows_at(dx, PR), :] = term[:PR]
            q_here[rows_at(dx, QR), :] = term[PR:]

    outs = [array(4 * PR, F32), array(4 * QR, F32)]
    own, q_here = block_call(
        own_terms, {dx: dx for dx in range(4)}, outs, blocks, [grad], 4 * ROWS
    )
    p_up, p_down, own, q_here = lax.optimization_barrier((p_up, p_down, own, q_here))

    def forward(kept_ahead, kept_behind, up, down, n, half):
        def body(a, b, u, d, up_out, down_out):
            for k in range(n):
                to, first, last = k * half, 2 * k * half, (2 * k + 1) * half
                up_out[to : to + half, :] = (
                    a[to : to + half, :] + u[first : first + half, :].astype(F32)
                ).astype(BF16)
                down_out[to : to + half, :] = (
                    b[to : to + half, :] + d[last : last + half, :].astype(F32)
                ).astype(BF16)

        return local_call(
            body, [array(n * half, BF16)] * 2, kept_ahead, kept_behind, up, down
        )

    def settle(kept, up, down, up2, down2, n, half, k):
        to, first, last = k * half, 2 * k * half, (2 * k + 1) * half
        one = kept[first : first + half, :] + down[first : first + half, :].astype(F32)
        two = kept[last : last + half, :] + up[last : last + half, :].astype(F32)
        return (
            one + up2[to : to + half, :].astype(F32),
            two + down2[to : to + half, :].astype(F32),
        )

    p_up2, p_down2 = forward(p_ahead, p_behind, p_up, p_down, 3, PH)
    p_up2, p_down2 = move(p_up2, "x", 1), move(p_down2, "x", -1)
    q_up2, q_down2 = forward(q_ahead, q_behind, q_up, q_down, 4, QH)
    q_up2, q_down2 = move(q_up2, "zh", 1), move(q_down2, "zh", -1)

    def p_body(kept, up, down, up2, down2, up_out, down_out, ahead, behind):
        for dz in (1, 2, 3):
            one, two = settle(kept, up, down, up2, down2, 3, PH, dz - 1)
            if dz == 1:
                ahead[...] = one
                up_out[PH:, :] = two.astype(BF16)
            elif dz == 2:
                up_out[:PH, :] = one.astype(BF16)
                down_out[PH:, :] = two.astype(BF16)
            else:
                down_out[:PH, :] = one.astype(BF16)
                behind[...] = two

    z_up, z_down, z_ahead, z_behind = local_call(
        p_body,
        [array(PR, BF16), array(PR, BF16), array(PH, F32), array(PH, F32)],
        p_here, p_up, p_down, p_up2, p_down2,
    )
    z_up, z_down = move(z_up, "zh", 1), move(z_down, "zh", -1)

    def q_body(own, kept, up, down, up2, down2, up_out, down_out, ahead, behind, here):
        rest = PR - RH
        for dx in range(4):
            one, two = settle(kept, up, down, up2, down2, 4, QH, dx)
            first = own[dx * PR : dx * PR + RH, :]
            last = own[dx * PR + RH : (dx + 1) * PR, :]
            for ref, at_last, low in {
                0: ((here, RH, 0),),
                1: ((up_out, RH, 1),),
                2: ((down_out, RH, 1),),
                3: ((behind, 0, 0),),
            }[dx]:
                ref[at_last : at_last + rest, :] = last.astype(ref.dtype)
                ref[at_last + rest : at_last + rest + QH, :] = one.astype(ref.dtype)
                ref[at_last + rest + QH : at_last + RH, :] = two.astype(ref.dtype)
            ref = (here, ahead, up_out, down_out)[dx]
            ref[:RH, :] = first.astype(ref.dtype)

    x_up, x_down, x_ahead, x_behind, x_here = local_call(
        q_body,
        [array(ROWS, BF16), array(ROWS, BF16), array(RH, F32), array(RH, F32), array(ROWS, F32)],
        own, q_here, q_up, q_down, q_up2, q_down2,
    )
    x_up, x_down = move(x_up, "x", 1), move(x_down, "x", -1)

    z_up2, z_down2 = forward(z_ahead, z_behind, z_up, z_down, 1, PH)
    z_up2, z_down2 = move(z_up2, "zh", 1), move(z_down2, "zh", -1)
    x_up2, x_down2 = forward(x_ahead, x_behind, x_up, x_down, 1, RH)
    x_up2, x_down2 = move(x_up2, "x", 1), move(x_down2, "x", -1)

    def last_body(here, xu, xd, xu2, xd2, zu, zd, zu2, zd2, out):
        out[:RH, :] = here[:RH, :] + xd[:RH, :].astype(F32) + xu2[...].astype(F32)
        out[RH:, :] = here[RH:, :] + xu[RH:, :].astype(F32) + xd2[...].astype(F32)
        out[:PH, :] += zd[:PH, :].astype(F32) + zu2[...].astype(F32)
        out[PH:PR, :] += zu[PH:, :].astype(F32) + zd2[...].astype(F32)

    (out,) = local_call(
        last_body, [array(ROWS, F32)],
        x_here, x_up, x_down, x_up2, x_down2, z_up, z_down, z_up2, z_down2,
    )
    return out


def shards(hidden, head, targets, block_index, lse_rest, cotangent):
    zh, x, c = (lax.axis_index(a) for a in DP)
    first_row = lax.axis_index(TENSOR) * ROWS
    row_ids = first_row + lax.iota(jnp.int32, ROWS)
    block_of = row_ids // BLOCK
    block_match = (block_of[:, None] == lax.iota(jnp.int32, block_index.shape[0])[None, :]).astype(
        jnp.int32
    )
    vocab_ids = jnp.sum(block_match * block_index[None, :], axis=1) * BLOCK + row_ids % BLOCK

    k = lax.iota(jnp.int32, 16)
    at = (((zh + k // 4) % 4) * 4 + (x + k % 4) % 4) * 2
    at, sibling_at = at + c, at + (1 - c)

    facts = jnp.stack([targets.astype(F32), lse_rest, cotangent])
    facts = jnp.concatenate([facts, move(facts, "c", 1)], axis=1)
    hit = (vocab_ids[:, None] == facts[0].astype(jnp.int32)[None, :]).astype(F32)

    partial, blocks = gathered_logits(head, hidden, at, sibling_at)
    logits, stats = statistics(partial, move(partial, "c", 1), hit)
    stats = lax.all_to_all(
        jnp.broadcast_to(stats[None], (8,) + stats.shape), TENSOR, split_axis=0, concat_axis=0, tiled=True
    )
    loss, grad = gradient(
        logits, hit, jnp.swapaxes(stats, 0, 1), facts[1:2], facts[2:3]
    )
    return loss[0, :TOK], scattered_gradient(grad, blocks)


def solution(mesh):
    mesh = Mesh(mesh.devices.reshape(SIZES), AXES)
    placed = (P(DP, None), P(TENSOR, DP), P(DP), P(), P(DP), P(DP))
    return jax.shard_map(
        shards, mesh=mesh, in_specs=placed, out_specs=(P(DP), P(TENSOR, DP)), check_vma=False
    )
```

```python
import jax
import jax.numpy as jnp
from jax import lax
from jax.experimental import pallas as pl
from jax.experimental.pallas import tpu as pltpu
from jax.sharding import Mesh
from jax.sharding import PartitionSpec as P

BLOCK = 1024
z_weight = 0.0001

AXES = ("zh", "x", "c", "zl", "y")
SIZES = (4, 4, 2, 2, 4)
DP = ("zh", "x", "c")
TENSOR = ("zl", "y")

ROWS = 256
TOK = 512
WIDE = 512
PR, QR = 192, 64
PH, QH, RH = PR // 2, QR // 2, ROWS // 2

F32 = jnp.float32
BF16 = jnp.bfloat16
MIB = 1024 * 1024


def move(value, axis, by):
    n = SIZES[AXES.index(axis)]
    return lax.ppermute(value, axis, [(i, (i + by) % n) for i in range(n)])


def params(mib):
    return pltpu.CompilerParams(vmem_limit_bytes=mib * MIB)


def whole(shape):
    return pl.BlockSpec(shape, lambda: (0,) * len(shape))


def local_call(body, outs, *args):
    size = sum(a.size * a.dtype.itemsize for a in args) + sum(
        o.size * o.dtype.itemsize for o in outs
    )
    return pl.pallas_call(
        body,
        out_shape=outs,
        in_specs=[whole(a.shape) for a in args],
        out_specs=[whole(o.shape) for o in outs],
        compiler_params=params(16),
        cost_estimate=pl.CostEstimate(flops=0, bytes_accessed=size, transcendentals=0),
    )(*args)


def pick(hidden, at, mib):
    n = at.shape[0]

    def body(at_ref, h_ref, o_ref, arrived):
        copies = [
            pltpu.make_async_copy(
                h_ref.at[:, pl.ds(pl.multiple_of(at_ref[k] * WIDE, WIDE), WIDE)],
                o_ref.at[k],
                arrived.at[k],
            )
            for k in range(n)
        ]
        for copy in copies:
            copy.start()
        for copy in copies:
            copy.wait()

    return pl.pallas_call(
        body,
        out_shape=jax.ShapeDtypeStruct((n, TOK, WIDE), BF16),
        in_specs=[
            pl.BlockSpec(memory_space=pltpu.SMEM),
            pl.BlockSpec(memory_space=pl.ANY),
        ],
        out_specs=pl.BlockSpec(memory_space=pltpu.VMEM),
        scratch_shapes=[pltpu.SemaphoreType.DMA((n,))],
        compiler_params=params(mib),
        cost_estimate=pl.CostEstimate(
            flops=0, bytes_accessed=2 * n * TOK * WIDE * 2, transcendentals=0
        ),
    )(at, hidden)


def block_call(compute, slots, outs, blocks, others, rows):
    mine, theirs = blocks
    places = max(slots) + 1

    def body(m_ref, t_ref, *refs):
        hold, arrived = refs[-2:]

        def copies(place, slot):
            for side, ref in enumerate((m_ref.at[slot], t_ref.at[slot])):
                yield pltpu.make_async_copy(
                    ref, hold.at[place, pl.ds(side * TOK, TOK)], arrived.at[place, side]
                )

        for place, slot in slots.items():
            for copy in copies(place, slot):
                copy.start()

        def block(place, wait=True):
            if wait:
                for copy in copies(place, 0):
                    copy.wait()
            return hold[place]

        compute(block, refs[: len(others)], refs[len(others) : -2])

    return pl.pallas_call(
        body,
        out_shape=outs,
        in_specs=[pl.BlockSpec(memory_space=pl.ANY)] * 2
        + [whole(o.shape) for o in others],
        out_specs=[whole(o.shape) for o in outs],
        scratch_shapes=[
            pltpu.VMEM((places, 2 * TOK, WIDE), BF16),
            pltpu.SemaphoreType.DMA((places, 2)),
        ],
        compiler_params=params(50),
        cost_estimate=pl.CostEstimate(
            flops=4 * rows * WIDE * TOK,
            bytes_accessed=2 * len(slots) * TOK * WIDE * 2,
            transcendentals=0,
        ),
    )(mine, theirs, *others)


def logits_call(compute, blocks, others):
    mine, theirs = blocks

    def body(m_ref, t_ref, *refs):
        def add(out, a, slot):
            out[:, :TOK] += times(a, m_ref[slot])
            out[:, TOK:] += times(a, t_ref[slot])

        compute(add, refs[:-1], refs[-1])

    return local_call(body, [LOGITS], mine, theirs, *others)[0]


def times(a, block):
    return lax.dot_general(a, block, (((1,), (1,)), ((), ())), preferred_element_type=F32)


def rows_at(k, size):
    return pl.ds(pl.multiple_of(k * size, size), size)


LOGITS = jax.ShapeDtypeStruct((ROWS, 2 * TOK), F32)
AHEAD = (1, 3, 2)


def statistics(partial, other, hit):
    def body(mine, theirs, hit_ref, logits, stats):
        total = mine[...] + jnp.concatenate([theirs[:, TOK:], theirs[:, :TOK]], axis=1)
        logits[...] = total
        top = jnp.max(total, axis=0, keepdims=True)
        stats[0:1, :] = top
        stats[1:2, :] = jnp.sum(jnp.exp(total - top), axis=0, keepdims=True)
        stats[2:3, :] = jnp.sum(total * hit_ref[...], axis=0, keepdims=True)

    outs = [
        jax.ShapeDtypeStruct((ROWS, 2 * TOK), F32),
        jax.ShapeDtypeStruct((3, 2 * TOK), F32),
    ]
    return local_call(body, outs, partial, other, hit)


def gradient(logits, hit, stats, lse_rest, cotangent):
    def body(logits_ref, hit_ref, s, rest, cot, loss, grad):
        top = s[0]
        row_max = jnp.max(top, axis=0, keepdims=True)
        row_total = jnp.sum(s[1] * jnp.exp(top - row_max), axis=0, keepdims=True)
        target_logit = jnp.sum(s[2], axis=0, keepdims=True)
        lse_window = row_max + jnp.log(row_total)
        larger = jnp.maximum(lse_window, rest[...])
        log_total = larger + jnp.log(
            jnp.exp(lse_window - larger) + jnp.exp(rest[...] - larger)
        )
        loss[...] = log_total - target_logit + z_weight * log_total * log_total
        softmax = jnp.exp(logits_ref[...] - log_total)
        grad[...] = (
            cot[...] * (softmax * (1.0 + 2.0 * z_weight * log_total) - hit_ref[...])
        ).astype(BF16)

    outs = [
        jax.ShapeDtypeStruct((1, 2 * TOK), F32),
        jax.ShapeDtypeStruct((ROWS, 2 * TOK), BF16),
    ]
    return local_call(body, outs, logits, hit, stats, lse_rest, cotangent)


def gathered_logits(head, hidden, at, sibling_at):
    zb, za = move(head[:PR], "zh", 1), move(head[:PR], "zh", -1)
    xb, xa = move(head, "x", 1), move(head, "x", -1)
    picked = pick(hidden, sibling_at, 50)
    zb, za, xb, xa, picked = lax.optimization_barrier((zb, za, xb, xa, picked))
    theirs = move(picked, "c", 1)
    zf1, zf2 = move(zb[:PH], "zh", 1), move(za[PH:], "zh", -1)
    xf1, xf2 = move(xb[PR : PR + QH], "x", 1), move(xa[PR + QH :], "x", -1)
    p = jnp.concatenate([za, zb, zf1, zf2], axis=0)
    q = jnp.concatenate([head[PR:], xa[PR:], xb[PR:], xf1, xf2], axis=0)
    pb, pa = move(p, "x", 1), move(p, "x", -1)
    qb, qa = move(q, "zh", 1), move(q, "zh", -1)
    zf1, zf2, at = lax.optimization_barrier((zf1, zf2, at))
    mine = pick(hidden, at, 40)
    blocks = (mine, theirs)

    def first(add, refs, out):
        head_ref, xa_ref, xb_ref, xf1_ref, xf2_ref, p_ref = refs
        out[...] = jnp.zeros_like(out)
        add(out, head_ref[...], 0)
        add(out, xa_ref[...], 1)
        add(out, xb_ref[...], 3)
        add(out.at[PR : PR + QH], xf1_ref[...], 2)
        add(out.at[PR + QH :], xf2_ref[...], 2)
        for k, dz in enumerate(AHEAD):
            add(out.at[:PR], p_ref[k * PR : (k + 1) * PR, :], 4 * dz)

    total = logits_call(first, blocks, [head, xa, xb, xf1, xf2, p])
    pb, pa, qb, qa, total = lax.optimization_barrier((pb, pa, qb, qa, total))
    pf1 = jnp.concatenate([pb[: 3 * PH], xb[:PH]], axis=0)
    pf2 = jnp.concatenate([pa[3 * PH :], xa[PH:PR]], axis=0)
    pf1, pf2 = move(pf1, "x", 1), move(pf2, "x", -1)
    qf1, qf2 = move(qb[: 2 * QR], "zh", 1), move(qa[2 * QR :], "zh", -1)

    def second(add, refs, out):
        pa_ref, pb_ref, qa_ref, qb_ref, total_ref = refs
        out[...] = total_ref[...]
        for k, dz in enumerate(AHEAD):
            part = slice(k * PR, (k + 1) * PR)
            add(out.at[:PR], pa_ref[part, :], 4 * dz + 1)
            add(out.at[:PR], pb_ref[part, :], 4 * dz + 3)
        for j, dx in enumerate((0,) + AHEAD):
            part = slice(j * QR, (j + 1) * QR)
            add(out.at[PR:], qa_ref[part, :], 4 + dx)
            add(out.at[PR:], qb_ref[part, :], 12 + dx)

    total = logits_call(second, blocks, [pa, pb, qa, qb, total])

    def third(add, refs, out):
        pf1_ref, pf2_ref, qf1_ref, qf2_ref, total_ref = refs
        out[...] = total_ref[...]
        add(out.at[:PR], pf1_ref[:PR, :], 4 + 2)
        add(out.at[:PH], pf1_ref[PR : 3 * PH, :], 12 + 2)
        add(out.at[PH:PR], pf2_ref[:PH, :], 12 + 2)
        add(out.at[:PR], pf2_ref[PH : 3 * PH, :], 8 + 2)
        add(out.at[:PH], pf1_ref[3 * PH :, :], 2)
        add(out.at[PH:PR], pf2_ref[3 * PH :, :], 2)
        add(out.at[PR:], qf1_ref[:QR, :], 8)
        add(out.at[PR:], qf1_ref[QR:, :], 8 + 1)
        add(out.at[PR:], qf2_ref[:QR, :], 8 + 3)
        add(out.at[PR:], qf2_ref[QR:, :], 8 + 2)

    total = logits_call(third, blocks, [pf1, pf2, qf1, qf2, total])
    return total, blocks


def scattered_gradient(grad, blocks):
    def array(rows, dtype):
        return jax.ShapeDtypeStruct((rows, WIDE), dtype)

    outs = [
        array(3 * PR, BF16),
        array(3 * PR, BF16),
        array(4 * QR, BF16),
        array(4 * QR, BF16),
        array(3 * PH, F32),
        array(3 * PH, F32),
        array(3 * PR, F32),
        array(4 * QH, F32),
        array(4 * QH, F32),
    ]
    def others_terms(block, refs, outs):
        (g_ref,) = refs
        p_up, p_down, q_up, q_down, p_ahead, p_behind, p_here, q_ahead, q_behind = outs

        @pl.loop(0, 3)
        def _(k):
            first, last = pl.ds(pl.multiple_of(k * PR, PR), PH), pl.ds(pl.multiple_of(k * PR + PH, PH), PH)
            kept = rows_at(k, PH)
            for dx in range(4):
                term = jnp.dot(g_ref[...], block(4 * k + dx), preferred_element_type=F32)
                one, two, three, four = term[:PH], term[PH:PR], term[PR : PR + QH], term[PR + QH :]
                if dx == 0:
                    p_here[rows_at(k, PR), :] = term[:PR]
                elif dx == 1:
                    p_ahead[kept, :] = one
                    p_up[last, :] = two.astype(BF16)
                elif dx == 2:
                    p_up[first, :] = one.astype(BF16)
                    p_down[last, :] = two.astype(BF16)
                else:
                    p_down[first, :] = one.astype(BF16)
                    p_behind[kept, :] = two
                start, middle = dx * QR, dx * QR + QH

                @pl.when(k == 0)
                def _():
                    q_ahead[dx * QH : (dx + 1) * QH, :] = three
                    q_up[middle : middle + QH, :] = four.astype(BF16)

                @pl.when(k == 1)
                def _():
                    q_up[start:middle, :] = three.astype(BF16)
                    q_down[middle : middle + QH, :] = four.astype(BF16)

                @pl.when(k == 2)
                def _():
                    q_down[start:middle, :] = three.astype(BF16)
                    q_behind[dx * QH : (dx + 1) * QH, :] = four

    slots = {place: 4 + place for place in range(12)}
    p_up, p_down, q_up, q_down, p_ahead, p_behind, p_here, q_ahead, q_behind = block_call(
        others_terms, slots, outs, blocks, [grad], 12 * ROWS
    )
    p_up, p_down = move(p_up, "x", 1), move(p_down, "x", -1)
    q_up, q_down = move(q_up, "zh", 1), move(q_down, "zh", -1)
    def own_terms(block, refs, outs):
        (g_ref,) = refs
        own, q_here = outs

        @pl.loop(0, 4)
        def _(dx):
            term = jnp.dot(g_ref[...], block(dx), preferred_element_type=F32)
            own[rows_at(dx, PR), :] = term[:PR]
            q_here[rows_at(dx, QR), :] = term[PR:]

    outs = [array(4 * PR, F32), array(4 * QR, F32)]
    own, q_here = block_call(
        own_terms, {dx: dx for dx in range(4)}, outs, blocks, [grad], 4 * ROWS
    )
    p_up, p_down, own, q_here = lax.optimization_barrier((p_up, p_down, own, q_here))

    def forward(kept_ahead, kept_behind, up, down, n, half, *after):
        def body(a, b, u, d, *rest):
            up_out, down_out = rest[-2:]
            for k in range(n):
                to, first, last = k * half, 2 * k * half, (2 * k + 1) * half
                up_out[to : to + half, :] = (
                    a[to : to + half, :] + u[first : first + half, :].astype(F32)
                ).astype(BF16)
                down_out[to : to + half, :] = (
                    b[to : to + half, :] + d[last : last + half, :].astype(F32)
                ).astype(BF16)

        return local_call(
            body, [array(n * half, BF16)] * 2, kept_ahead, kept_behind, up, down, *after
        )

    def settle(kept, up, down, up2, down2, n, half, k):
        to, first, last = k * half, 2 * k * half, (2 * k + 1) * half
        one = kept[first : first + half, :] + down[first : first + half, :].astype(F32)
        two = kept[last : last + half, :] + up[last : last + half, :].astype(F32)
        return (
            one + up2[to : to + half, :].astype(F32),
            two + down2[to : to + half, :].astype(F32),
        )

    p_up2, p_down2 = forward(p_ahead, p_behind, p_up, p_down, 3, PH)
    p_up2, p_down2 = move(p_up2, "x", 1), move(p_down2, "x", -1)
    q_up2, q_down2 = forward(q_ahead, q_behind, q_up, q_down, 4, QH)
    q_up2, q_down2 = move(q_up2, "zh", 1), move(q_down2, "zh", -1)

    def p_body(kept, up, down, up2, down2, up_out, down_out, ahead, behind):
        for dz in (1, 2, 3):
            one, two = settle(kept, up, down, up2, down2, 3, PH, dz - 1)
            if dz == 1:
                ahead[...] = one
                up_out[PH:, :] = two.astype(BF16)
            elif dz == 2:
                up_out[:PH, :] = one.astype(BF16)
                down_out[PH:, :] = two.astype(BF16)
            else:
                down_out[:PH, :] = one.astype(BF16)
                behind[...] = two

    z_up, z_down, z_ahead, z_behind = local_call(
        p_body,
        [array(PR, BF16), array(PR, BF16), array(PH, F32), array(PH, F32)],
        p_here, p_up, p_down, p_up2, p_down2,
    )
    p_sent = z_up
    z_up, z_down = move(z_up, "zh", 1), move(z_down, "zh", -1)

    def q_body(own, kept, up, down, up2, down2, _, up_out, down_out, ahead, behind, here):
        rest = PR - RH
        for dx in range(4):
            one, two = settle(kept, up, down, up2, down2, 4, QH, dx)
            first = own[dx * PR : dx * PR + RH, :]
            last = own[dx * PR + RH : (dx + 1) * PR, :]
            for ref, at_last, low in {
                0: ((here, RH, 0),),
                1: ((up_out, RH, 1),),
                2: ((down_out, RH, 1),),
                3: ((behind, 0, 0),),
            }[dx]:
                ref[at_last : at_last + rest, :] = last.astype(ref.dtype)
                ref[at_last + rest : at_last + rest + QH, :] = one.astype(ref.dtype)
                ref[at_last + rest + QH : at_last + RH, :] = two.astype(ref.dtype)
            ref = (here, ahead, up_out, down_out)[dx]
            ref[:RH, :] = first.astype(ref.dtype)

    x_up, x_down, x_ahead, x_behind, x_here = local_call(
        q_body,
        [array(ROWS, BF16), array(ROWS, BF16), array(RH, F32), array(RH, F32), array(ROWS, F32)],
        own, q_here, q_up, q_down, q_up2, q_down2, p_sent,
    )
    x_up, x_down = move(x_up, "x", 1), move(x_down, "x", -1)

    z_up2, z_down2 = forward(z_ahead, z_behind, z_up, z_down, 1, PH)
    x_up2, x_down2 = forward(x_ahead, x_behind, x_up, x_down, 1, RH, z_up2)
    z_up2, z_down2 = move(z_up2, "zh", 1), move(z_down2, "zh", -1)
    x_up2, x_down2 = move(x_up2, "x", 1), move(x_down2, "x", -1)

    def last_body(here, xu, xd, xu2, xd2, zu, zd, zu2, zd2, out):
        out[:RH, :] = here[:RH, :] + xd[:RH, :].astype(F32) + xu2[...].astype(F32)
        out[RH:, :] = here[RH:, :] + xu[RH:, :].astype(F32) + xd2[...].astype(F32)
        out[:PH, :] += zd[:PH, :].astype(F32) + zu2[...].astype(F32)
        out[PH:PR, :] += zu[PH:, :].astype(F32) + zd2[...].astype(F32)

    (out,) = local_call(
        last_body, [array(ROWS, F32)],
        x_here, x_up, x_down, x_up2, x_down2, z_up, z_down, z_up2, z_down2,
    )
    return out


def shards(hidden, head, targets, block_index, lse_rest, cotangent):
    zh, x, c = (lax.axis_index(a) for a in DP)
    first_row = lax.axis_index(TENSOR) * ROWS
    row_ids = first_row + lax.iota(jnp.int32, ROWS)
    block_of = row_ids // BLOCK
    block_match = (block_of[:, None] == lax.iota(jnp.int32, block_index.shape[0])[None, :]).astype(
        jnp.int32
    )
    vocab_ids = jnp.sum(block_match * block_index[None, :], axis=1) * BLOCK + row_ids % BLOCK

    k = lax.iota(jnp.int32, 16)
    at = (((zh + k // 4) % 4) * 4 + (x + k % 4) % 4) * 2
    at, sibling_at = at + c, at + (1 - c)

    facts = jnp.stack([targets.astype(F32), lse_rest, cotangent])
    facts = jnp.concatenate([facts, move(facts, "c", 1)], axis=1)
    hit = (vocab_ids[:, None] == facts[0].astype(jnp.int32)[None, :]).astype(F32)

    partial, blocks = gathered_logits(head, hidden, at, sibling_at)
    logits, stats = statistics(partial, move(partial, "c", 1), hit)
    stats = lax.all_to_all(
        jnp.broadcast_to(stats[None], (8,) + stats.shape), TENSOR, split_axis=0, concat_axis=0, tiled=True
    )
    loss, grad = gradient(
        logits, hit, jnp.swapaxes(stats, 0, 1), facts[1:2], facts[2:3]
    )
    return loss[0, :TOK], scattered_gradient(grad, blocks)


def solution(mesh):
    mesh = Mesh(mesh.devices.reshape(SIZES), AXES)
    placed = (P(DP, None), P(TENSOR, DP), P(DP), P(), P(DP), P(DP))
    return jax.shard_map(
        shards, mesh=mesh, in_specs=placed, out_specs=(P(DP), P(TENSOR, DP)), check_vma=False
    )
```

```python
import jax
import jax.numpy as jnp
from jax import lax
from jax.experimental import pallas as pl
from jax.experimental.pallas import tpu as pltpu
from jax.sharding import Mesh
from jax.sharding import PartitionSpec as P

BLOCK = 1024
z_weight = 0.0001

AXES = ("zh", "x", "c", "zl", "y")
SIZES = (4, 4, 2, 2, 4)
DP = ("zh", "x", "c")
TENSOR = ("zl", "y")

ROWS = 256
TOK = 512
WIDE = 512
PR, QR = 192, 64
PH, QH, RH = PR // 2, QR // 2, ROWS // 2

F32 = jnp.float32
BF16 = jnp.bfloat16
MIB = 1024 * 1024


def move(value, axis, by):
    n = SIZES[AXES.index(axis)]
    return lax.ppermute(value, axis, [(i, (i + by) % n) for i in range(n)])


def params(mib):
    return pltpu.CompilerParams(vmem_limit_bytes=mib * MIB)


def whole(shape):
    return pl.BlockSpec(shape, lambda: (0,) * len(shape))


def local_call(body, outs, *args):
    size = sum(a.size * a.dtype.itemsize for a in args) + sum(
        o.size * o.dtype.itemsize for o in outs
    )
    return pl.pallas_call(
        body,
        out_shape=outs,
        in_specs=[whole(a.shape) for a in args],
        out_specs=[whole(o.shape) for o in outs],
        compiler_params=params(16),
        cost_estimate=pl.CostEstimate(flops=0, bytes_accessed=size, transcendentals=0),
    )(*args)


def pick(hidden, at, mib):
    n = at.shape[0]

    def body(at_ref, h_ref, o_ref, arrived):
        copies = [
            pltpu.make_async_copy(
                h_ref.at[:, pl.ds(pl.multiple_of(at_ref[k] * WIDE, WIDE), WIDE)],
                o_ref.at[k],
                arrived.at[k],
            )
            for k in range(n)
        ]
        for copy in copies:
            copy.start()
        for copy in copies:
            copy.wait()

    return pl.pallas_call(
        body,
        out_shape=jax.ShapeDtypeStruct((n, TOK, WIDE), BF16),
        in_specs=[
            pl.BlockSpec(memory_space=pltpu.SMEM),
            pl.BlockSpec(memory_space=pl.ANY),
        ],
        out_specs=pl.BlockSpec(memory_space=pltpu.VMEM),
        scratch_shapes=[pltpu.SemaphoreType.DMA((n,))],
        compiler_params=params(mib),
        cost_estimate=pl.CostEstimate(
            flops=0, bytes_accessed=2 * n * TOK * WIDE * 2, transcendentals=0
        ),
    )(at, hidden)


def block_call(compute, slots, outs, blocks, others, rows):
    mine, theirs = blocks
    places = max(slots) + 1

    def body(m_ref, t_ref, *refs):
        hold, arrived = refs[-2:]

        def copies(place, slot):
            for side, ref in enumerate((m_ref.at[slot], t_ref.at[slot])):
                yield pltpu.make_async_copy(
                    ref, hold.at[place, pl.ds(side * TOK, TOK)], arrived.at[place, side]
                )

        for place, slot in slots.items():
            for copy in copies(place, slot):
                copy.start()

        def block(place, wait=True):
            if wait:
                for copy in copies(place, 0):
                    copy.wait()
            return hold[place]

        compute(block, refs[: len(others)], refs[len(others) : -2])

    return pl.pallas_call(
        body,
        out_shape=outs,
        in_specs=[pl.BlockSpec(memory_space=pl.ANY)] * 2
        + [whole(o.shape) for o in others],
        out_specs=[whole(o.shape) for o in outs],
        scratch_shapes=[
            pltpu.VMEM((places, 2 * TOK, WIDE), BF16),
            pltpu.SemaphoreType.DMA((places, 2)),
        ],
        compiler_params=params(50),
        cost_estimate=pl.CostEstimate(
            flops=4 * rows * WIDE * TOK,
            bytes_accessed=2 * len(slots) * TOK * WIDE * 2,
            transcendentals=0,
        ),
    )(mine, theirs, *others)


def logits_call(compute, blocks, others):
    mine, theirs = blocks

    def body(m_ref, t_ref, *refs):
        def add(out, a, slot):
            out[:, :TOK] += times(a, m_ref[slot])
            out[:, TOK:] += times(a, t_ref[slot])

        compute(add, refs[:-1], refs[-1])

    return local_call(body, [LOGITS], mine, theirs, *others)[0]


def times(a, block):
    return lax.dot_general(a, block, (((1,), (1,)), ((), ())), preferred_element_type=F32)


def rows_at(k, size):
    return pl.ds(pl.multiple_of(k * size, size), size)


LOGITS = jax.ShapeDtypeStruct((ROWS, 2 * TOK), F32)
AHEAD = (1, 3, 2)


def statistics(partial, other, hit):
    def body(mine, theirs, hit_ref, logits, stats):
        total = mine[...] + jnp.concatenate([theirs[:, TOK:], theirs[:, :TOK]], axis=1)
        logits[...] = total
        top = jnp.max(total, axis=0, keepdims=True)
        stats[0:1, :] = top
        stats[1:2, :] = jnp.sum(jnp.exp(total - top), axis=0, keepdims=True)
        stats[2:3, :] = jnp.sum(total * hit_ref[...], axis=0, keepdims=True)

    outs = [
        jax.ShapeDtypeStruct((ROWS, 2 * TOK), F32),
        jax.ShapeDtypeStruct((3, 2 * TOK), F32),
    ]
    return local_call(body, outs, partial, other, hit)


def gradient(logits, hit, stats, lse_rest, cotangent):
    def body(logits_ref, hit_ref, s, rest, cot, loss, grad):
        top = s[0]
        row_max = jnp.max(top, axis=0, keepdims=True)
        row_total = jnp.sum(s[1] * jnp.exp(top - row_max), axis=0, keepdims=True)
        target_logit = jnp.sum(s[2], axis=0, keepdims=True)
        lse_window = row_max + jnp.log(row_total)
        larger = jnp.maximum(lse_window, rest[...])
        log_total = larger + jnp.log(
            jnp.exp(lse_window - larger) + jnp.exp(rest[...] - larger)
        )
        loss[...] = log_total - target_logit + z_weight * log_total * log_total
        softmax = jnp.exp(logits_ref[...] - log_total)
        grad[...] = (
            cot[...] * (softmax * (1.0 + 2.0 * z_weight * log_total) - hit_ref[...])
        ).astype(BF16)

    outs = [
        jax.ShapeDtypeStruct((1, 2 * TOK), F32),
        jax.ShapeDtypeStruct((ROWS, 2 * TOK), BF16),
    ]
    return local_call(body, outs, logits, hit, stats, lse_rest, cotangent)


def gathered_logits(head, hidden, at, sibling_at):
    def split(h, *outs):
        for out, start in zip(outs, (0, PH, PR)):
            out[...] = h[start : start + out.shape[0], :]

    over_zh, over_x, far_x = local_call(
        split, [jax.ShapeDtypeStruct((r, WIDE), BF16) for r in (PR, ROWS - PH, QR)], head
    )
    zb, za, zf = (move(over_zh, "zh", by) for by in (1, -1, 2))
    xb, xa = move(over_x, "x", 1), move(over_x, "x", -1)
    xf = move(far_x, "x", 2)
    picked = pick(hidden, sibling_at, 50)
    zb, za, zf, xb, xa, xf, picked = lax.optimization_barrier((zb, za, zf, xb, xa, xf, picked))
    theirs = move(picked, "c", 1)
    p = jnp.concatenate([za, zb, zf, head[:PH]], axis=0)
    q = jnp.concatenate([head[PR:], xa[PH:], xb[PH:], xf], axis=0)
    pb, pa = move(p, "x", 1), move(p, "x", -1)
    qb, qa = move(q, "zh", 1), move(q, "zh", -1)
    zf, at = lax.optimization_barrier((zf, at))
    mine = pick(hidden, at, 40)
    pb, pa, qb, qa, mine = lax.optimization_barrier((pb, pa, qb, qa, mine))
    pf1 = jnp.concatenate([pb[: 3 * PH], pb[3 * PR :]], axis=0)
    pf2 = jnp.concatenate([pa[3 * PH : 3 * PR], xa[:PH]], axis=0)
    pf1, pf2 = move(pf1, "x", 1), move(pf2, "x", -1)
    qf1, qf2 = move(qb[: 2 * QR], "zh", 1), move(qa[2 * QR :], "zh", -1)

    blocks = (mine, theirs)

    def first(add, refs, out):
        head_ref, xa_ref, xb_ref, xf_ref, p_ref = refs
        out[...] = jnp.zeros_like(out)
        add(out, head_ref[...], 0)
        add(out.at[PH:], xa_ref[...], 1)
        add(out.at[PH:], xb_ref[...], 3)
        add(out.at[PR:], xf_ref[...], 2)
        for k, dz in enumerate(AHEAD):
            add(out.at[:PR], p_ref[k * PR : (k + 1) * PR, :], 4 * dz)

    total = logits_call(first, blocks, [head, xa, xb, xf, p])
    def second(add, refs, out):
        pa_ref, pb_ref, qa_ref, qb_ref, total_ref = refs
        out[...] = total_ref[...]
        for k, dz in enumerate(AHEAD):
            part = slice(k * PR, (k + 1) * PR)
            add(out.at[:PR], pa_ref[part, :], 4 * dz + 1)
            add(out.at[:PR], pb_ref[part, :], 4 * dz + 3)
        add(out.at[:PH], pa_ref[3 * PR :, :], 1)
        add(out.at[:PH], pb_ref[3 * PR :, :], 3)
        for j, dx in enumerate((0,) + AHEAD):
            part = slice(j * QR, (j + 1) * QR)
            add(out.at[PR:], qa_ref[part, :], 4 + dx)
            add(out.at[PR:], qb_ref[part, :], 12 + dx)

    total = logits_call(second, blocks, [pa, pb, qa, qb, total])

    def third(add, refs, out):
        pf1_ref, pf2_ref, qf1_ref, qf2_ref, total_ref = refs
        out[...] = total_ref[...]
        add(out.at[:PR], pf1_ref[:PR, :], 4 + 2)
        add(out.at[:PH], pf1_ref[PR : 3 * PH, :], 12 + 2)
        add(out.at[PH:PR], pf2_ref[:PH, :], 12 + 2)
        add(out.at[:PR], pf2_ref[PH : 3 * PH, :], 8 + 2)
        add(out.at[:PH], pf1_ref[3 * PH :, :], 2)
        add(out.at[PH:PR], pf2_ref[3 * PH :, :], 2)
        add(out.at[PR:], qf1_ref[:QR, :], 8)
        add(out.at[PR:], qf1_ref[QR:, :], 8 + 1)
        add(out.at[PR:], qf2_ref[:QR, :], 8 + 3)
        add(out.at[PR:], qf2_ref[QR:, :], 8 + 2)

    total = logits_call(third, blocks, [pf1, pf2, qf1, qf2, total])
    return total, blocks


def scattered_gradient(grad, blocks):
    def array(rows, dtype):
        return jax.ShapeDtypeStruct((rows, WIDE), dtype)

    outs = [
        array(3 * PR, BF16),
        array(3 * PR, BF16),
        array(4 * QR, BF16),
        array(4 * QR, BF16),
        array(3 * PH, F32),
        array(3 * PH, F32),
        array(3 * PR, F32),
        array(4 * QH, F32),
        array(4 * QH, F32),
    ]
    def others_terms(block, refs, outs):
        (g_ref,) = refs
        p_up, p_down, q_up, q_down, p_ahead, p_behind, p_here, q_ahead, q_behind = outs

        @pl.loop(0, 3)
        def _(k):
            first, last = pl.ds(pl.multiple_of(k * PR, PR), PH), pl.ds(pl.multiple_of(k * PR + PH, PH), PH)
            kept = rows_at(k, PH)
            for dx in range(4):
                term = jnp.dot(g_ref[...], block(4 * k + dx), preferred_element_type=F32)
                one, two, three, four = term[:PH], term[PH:PR], term[PR : PR + QH], term[PR + QH :]
                if dx == 0:
                    p_here[rows_at(k, PR), :] = term[:PR]
                elif dx == 1:
                    p_ahead[kept, :] = one
                    p_up[last, :] = two.astype(BF16)
                elif dx == 2:
                    p_up[first, :] = one.astype(BF16)
                    p_down[last, :] = two.astype(BF16)
                else:
                    p_down[first, :] = one.astype(BF16)
                    p_behind[kept, :] = two
                start, middle = dx * QR, dx * QR + QH

                @pl.when(k == 0)
                def _():
                    q_ahead[dx * QH : (dx + 1) * QH, :] = three
                    q_up[middle : middle + QH, :] = four.astype(BF16)

                @pl.when(k == 1)
                def _():
                    q_up[start:middle, :] = three.astype(BF16)
                    q_down[middle : middle + QH, :] = four.astype(BF16)

                @pl.when(k == 2)
                def _():
                    q_down[start:middle, :] = three.astype(BF16)
                    q_behind[dx * QH : (dx + 1) * QH, :] = four

    slots = {place: 4 + place for place in range(12)}
    p_up, p_down, q_up, q_down, p_ahead, p_behind, p_here, q_ahead, q_behind = block_call(
        others_terms, slots, outs, blocks, [grad], 12 * ROWS
    )
    p_up, p_down = move(p_up, "x", 1), move(p_down, "x", -1)
    q_up, q_down = move(q_up, "zh", 1), move(q_down, "zh", -1)
    def own_terms(block, refs, outs):
        (g_ref,) = refs
        own, q_here = outs

        @pl.loop(0, 4)
        def _(dx):
            term = jnp.dot(g_ref[...], block(dx), preferred_element_type=F32)
            own[rows_at(dx, PR), :] = term[:PR]
            q_here[rows_at(dx, QR), :] = term[PR:]

    outs = [array(4 * PR, F32), array(4 * QR, F32)]
    own, q_here = block_call(
        own_terms, {dx: dx for dx in range(4)}, outs, blocks, [grad], 4 * ROWS
    )
    p_up, p_down, own, q_here = lax.optimization_barrier((p_up, p_down, own, q_here))

    def forward(kept_ahead, kept_behind, up, down, n, half):
        def body(a, b, u, d, up_out, down_out):
            for k in range(n):
                to, first, last = k * half, 2 * k * half, (2 * k + 1) * half
                up_out[to : to + half, :] = (
                    a[to : to + half, :] + u[first : first + half, :].astype(F32)
                ).astype(BF16)
                down_out[to : to + half, :] = (
                    b[to : to + half, :] + d[last : last + half, :].astype(F32)
                ).astype(BF16)

        return local_call(
            body, [array(n * half, BF16)] * 2, kept_ahead, kept_behind, up, down
        )

    def settle(kept, up, down, up2, down2, n, half, k):
        to, first, last = k * half, 2 * k * half, (2 * k + 1) * half
        one = kept[first : first + half, :] + down[first : first + half, :].astype(F32)
        two = kept[last : last + half, :] + up[last : last + half, :].astype(F32)
        return (
            one + up2[to : to + half, :].astype(F32),
            two + down2[to : to + half, :].astype(F32),
        )

    p_up2, p_down2 = forward(p_ahead, p_behind, p_up, p_down, 3, PH)
    p_up2, p_down2 = move(p_up2, "x", 1), move(p_down2, "x", -1)
    q_up2, q_down2 = forward(q_ahead, q_behind, q_up, q_down, 4, QH)
    q_up2, q_down2 = move(q_up2, "zh", 1), move(q_down2, "zh", -1)

    def p_body(kept, up, down, up2, down2, *outs):
        for k in range(3):
            one, two = settle(kept, up, down, up2, down2, 3, PH, k)
            outs[k][:PH, :] = one.astype(BF16)
            outs[k][PH:, :] = two.astype(BF16)

    z1, z2, z3 = local_call(
        p_body, [array(PR, BF16)] * 3, p_here, p_up, p_down, p_up2, p_down2
    )
    p_sent = z1
    z1, z2, z3 = move(z1, "zh", 1), move(z2, "zh", 2), move(z3, "zh", -1)

    def q_body(own, kept, up, down, up2, down2, _, up_out, down_out, ahead, behind, here):
        rest = PR - RH
        for dx in range(4):
            one, two = settle(kept, up, down, up2, down2, 4, QH, dx)
            first = own[dx * PR : dx * PR + RH, :]
            last = own[dx * PR + RH : (dx + 1) * PR, :]
            for ref, at_last, low in {
                0: ((here, RH, 0),),
                1: ((up_out, RH, 1),),
                2: ((down_out, RH, 1),),
                3: ((behind, 0, 0),),
            }[dx]:
                ref[at_last : at_last + rest, :] = last.astype(ref.dtype)
                ref[at_last + rest : at_last + rest + QH, :] = one.astype(ref.dtype)
                ref[at_last + rest + QH : at_last + RH, :] = two.astype(ref.dtype)
            ref = (here, ahead, up_out, down_out)[dx]
            ref[:RH, :] = first.astype(ref.dtype)

    x_up, x_down, x_ahead, x_behind, x_here = local_call(
        q_body,
        [array(ROWS, BF16), array(ROWS, BF16), array(RH, F32), array(RH, F32), array(ROWS, F32)],
        own, q_here, q_up, q_down, q_up2, q_down2, p_sent,
    )
    x_up, x_down = move(x_up, "x", 1), move(x_down, "x", -1)

    x_up2, x_down2 = forward(x_ahead, x_behind, x_up, x_down, 1, RH)
    x_up2, x_down2 = move(x_up2, "x", 1), move(x_down2, "x", -1)

    def last_body(here, xu, xd, xu2, xd2, z1, z2, z3, out):
        out[:RH, :] = here[:RH, :] + xd[:RH, :].astype(F32) + xu2[...].astype(F32)
        out[RH:, :] = here[RH:, :] + xu[RH:, :].astype(F32) + xd2[...].astype(F32)
        out[:PR, :] += z1[...].astype(F32) + z2[...].astype(F32) + z3[...].astype(F32)

    (out,) = local_call(
        last_body, [array(ROWS, F32)], x_here, x_up, x_down, x_up2, x_down2, z1, z2, z3
    )
    return out


def shards(hidden, head, targets, block_index, lse_rest, cotangent):
    zh, x, c = (lax.axis_index(a) for a in DP)
    first_row = lax.axis_index(TENSOR) * ROWS
    row_ids = first_row + lax.iota(jnp.int32, ROWS)
    block_of = row_ids // BLOCK
    block_match = (block_of[:, None] == lax.iota(jnp.int32, block_index.shape[0])[None, :]).astype(
        jnp.int32
    )
    vocab_ids = jnp.sum(block_match * block_index[None, :], axis=1) * BLOCK + row_ids % BLOCK

    k = lax.iota(jnp.int32, 16)
    at = (((zh + k // 4) % 4) * 4 + (x + k % 4) % 4) * 2
    at, sibling_at = at + c, at + (1 - c)

    facts = jnp.stack([targets.astype(F32), lse_rest, cotangent])
    facts = jnp.concatenate([facts, move(facts, "c", 1)], axis=1)
    hit = (vocab_ids[:, None] == facts[0].astype(jnp.int32)[None, :]).astype(F32)

    partial, blocks = gathered_logits(head, hidden, at, sibling_at)
    logits, stats = statistics(partial, move(partial, "c", 1), hit)
    stats = lax.all_to_all(
        jnp.broadcast_to(stats[None], (8,) + stats.shape), TENSOR, split_axis=0, concat_axis=0, tiled=True
    )
    loss, grad = gradient(
        logits, hit, jnp.swapaxes(stats, 0, 1), facts[1:2], facts[2:3]
    )
    return loss[0, :TOK], scattered_gradient(grad, blocks)


def solution(mesh):
    mesh = Mesh(mesh.devices.reshape(SIZES), AXES)
    placed = (P(DP, None), P(TENSOR, DP), P(DP), P(), P(DP), P(DP))
    return jax.shard_map(
        shards, mesh=mesh, in_specs=placed, out_specs=(P(DP), P(TENSOR, DP)), check_vma=False
    )
```

```python
import jax
import jax.numpy as jnp
from jax import lax
from jax.experimental import pallas as pl
from jax.experimental.pallas import tpu as pltpu
from jax.sharding import Mesh
from jax.sharding import PartitionSpec as P

BLOCK = 1024
z_weight = 0.0001

AXES = ("zh", "x", "c", "zl", "y")
SIZES = (4, 4, 2, 2, 4)
DP = ("zh", "x", "c")
TENSOR = ("zl", "y")

ROWS = 256
TOK = 512
WIDE = 512
PR, QR = 192, 64
PH, QH, RH = PR // 2, QR // 2, ROWS // 2

F32 = jnp.float32
BF16 = jnp.bfloat16
MIB = 1024 * 1024


def move(value, axis, by):
    n = SIZES[AXES.index(axis)]
    return lax.ppermute(value, axis, [(i, (i + by) % n) for i in range(n)])


def params(mib):
    return pltpu.CompilerParams(vmem_limit_bytes=mib * MIB)


def whole(shape):
    return pl.BlockSpec(shape, lambda: (0,) * len(shape))


def local_call(body, outs, *args):
    size = sum(a.size * a.dtype.itemsize for a in args) + sum(
        o.size * o.dtype.itemsize for o in outs
    )
    return pl.pallas_call(
        body,
        out_shape=outs,
        in_specs=[whole(a.shape) for a in args],
        out_specs=[whole(o.shape) for o in outs],
        compiler_params=params(16),
        cost_estimate=pl.CostEstimate(flops=0, bytes_accessed=size, transcendentals=0),
    )(*args)


def pick(hidden, at, mib):
    n = at.shape[0]

    def body(at_ref, h_ref, o_ref, arrived):
        copies = [
            pltpu.make_async_copy(
                h_ref.at[:, pl.ds(pl.multiple_of(at_ref[k] * WIDE, WIDE), WIDE)],
                o_ref.at[k],
                arrived.at[k],
            )
            for k in range(n)
        ]
        for copy in copies:
            copy.start()
        for copy in copies:
            copy.wait()

    return pl.pallas_call(
        body,
        out_shape=jax.ShapeDtypeStruct((n, TOK, WIDE), BF16),
        in_specs=[
            pl.BlockSpec(memory_space=pltpu.SMEM),
            pl.BlockSpec(memory_space=pl.ANY),
        ],
        out_specs=pl.BlockSpec(memory_space=pltpu.VMEM),
        scratch_shapes=[pltpu.SemaphoreType.DMA((n,))],
        compiler_params=params(mib),
        cost_estimate=pl.CostEstimate(
            flops=0, bytes_accessed=2 * n * TOK * WIDE * 2, transcendentals=0
        ),
    )(at, hidden)


def block_call(compute, slots, outs, blocks, others, rows):
    mine, theirs = blocks
    places = max(slots) + 1

    def body(m_ref, t_ref, *refs):
        hold, arrived = refs[-2:]

        def copies(place, slot):
            for side, ref in enumerate((m_ref.at[slot], t_ref.at[slot])):
                yield pltpu.make_async_copy(
                    ref, hold.at[place, pl.ds(side * TOK, TOK)], arrived.at[place, side]
                )

        for place, slot in slots.items():
            for copy in copies(place, slot):
                copy.start()

        def block(place, wait=True):
            if wait:
                for copy in copies(place, 0):
                    copy.wait()
            return hold[place]

        compute(block, refs[: len(others)], refs[len(others) : -2])

    return pl.pallas_call(
        body,
        out_shape=outs,
        in_specs=[pl.BlockSpec(memory_space=pl.ANY)] * 2
        + [whole(o.shape) for o in others],
        out_specs=[whole(o.shape) for o in outs],
        scratch_shapes=[
            pltpu.VMEM((places, 2 * TOK, WIDE), BF16),
            pltpu.SemaphoreType.DMA((places, 2)),
        ],
        compiler_params=params(50),
        cost_estimate=pl.CostEstimate(
            flops=4 * rows * WIDE * TOK,
            bytes_accessed=2 * len(slots) * TOK * WIDE * 2,
            transcendentals=0,
        ),
    )(mine, theirs, *others)


def logits_call(compute, blocks, others):
    mine, theirs = blocks

    def body(m_ref, t_ref, *refs):
        def add(out, a, slot):
            out[:, :TOK] += times(a, m_ref[slot])
            out[:, TOK:] += times(a, t_ref[slot])

        compute(add, refs[:-1], refs[-1])

    return local_call(body, [LOGITS], mine, theirs, *others)[0]


def times(a, block):
    return lax.dot_general(a, block, (((1,), (1,)), ((), ())), preferred_element_type=F32)


def rows_at(k, size):
    return pl.ds(pl.multiple_of(k * size, size), size)


LOGITS = jax.ShapeDtypeStruct((ROWS, 2 * TOK), F32)


def statistics(partial, other, hit):
    def body(mine, theirs, hit_ref, logits, stats):
        total = mine[...] + jnp.concatenate([theirs[:, TOK:], theirs[:, :TOK]], axis=1)
        logits[...] = total
        top = jnp.max(total, axis=0, keepdims=True)
        stats[0:1, :] = top
        stats[1:2, :] = jnp.sum(jnp.exp(total - top), axis=0, keepdims=True)
        stats[2:3, :] = jnp.sum(total * hit_ref[...], axis=0, keepdims=True)

    outs = [
        jax.ShapeDtypeStruct((ROWS, 2 * TOK), F32),
        jax.ShapeDtypeStruct((3, 2 * TOK), F32),
    ]
    return local_call(body, outs, partial, other, hit)


def merged(one, two):
    top = jnp.maximum(one[0:1, :], two[0:1, :])
    total = one[1:2, :] * jnp.exp(one[0:1, :] - top) + two[1:2, :] * jnp.exp(two[0:1, :] - top)
    return jnp.concatenate([top, total, one[2:3, :] + two[2:3, :]], axis=0)


def merge_four(mine, one, two, three):
    def body(a, b, c, d, out):
        out[...] = merged(merged(a[...], c[...]), merged(b[...], d[...]))

    return local_call(body, [jax.ShapeDtypeStruct(mine.shape, F32)], mine, one, two, three)[0]


def gradient(logits, hit, stats, other, lse_rest, cotangent):
    def body(logits_ref, hit_ref, s, o, rest, cot, loss, grad):
        whole_stats = merged(s[...], o[...])
        row_max, row_total, target_logit = (whole_stats[k : k + 1, :] for k in range(3))
        lse_window = row_max + jnp.log(row_total)
        larger = jnp.maximum(lse_window, rest[...])
        log_total = larger + jnp.log(
            jnp.exp(lse_window - larger) + jnp.exp(rest[...] - larger)
        )
        loss[...] = log_total - target_logit + z_weight * log_total * log_total
        softmax = jnp.exp(logits_ref[...] - log_total)
        grad[...] = (
            cot[...] * (softmax * (1.0 + 2.0 * z_weight * log_total) - hit_ref[...])
        ).astype(BF16)

    outs = [
        jax.ShapeDtypeStruct((1, 2 * TOK), F32),
        jax.ShapeDtypeStruct((ROWS, 2 * TOK), BF16),
    ]
    return local_call(body, outs, logits, hit, stats, other, lse_rest, cotangent)


def gathered_logits(head, hidden, at, sibling_at):
    zb, za = move(head[:PR], "zh", 1), move(head[:PR], "zh", -1)
    xb, xa = move(head, "x", 1), move(head, "x", -1)
    picked = pick(hidden, sibling_at, 50)
    zb, za, xb, xa, picked = lax.optimization_barrier((zb, za, xb, xa, picked))
    theirs = move(picked, "c", 1)
    zf1, zf2 = move(zb[:PH], "zh", 1), move(za[PH:], "zh", -1)
    xf1, xf2 = move(xb[PR : PR + QH], "x", 1), move(xa[PR + QH :], "x", -1)
    p = jnp.concatenate([za, zf1, zf2, zb], axis=0)
    q = jnp.concatenate([head[PR:], xa[PR:], xf1, xf2, xb[PR:]], axis=0)
    pb, pa = move(p, "x", 1), move(p, "x", -1)
    qb, qa = move(q, "zh", 1), move(q, "zh", -1)
    zf1, zf2, at = lax.optimization_barrier((zf1, zf2, at))
    mine = pick(hidden, at, 40)
    blocks = (mine, theirs)

    def first(add, refs, out):
        head_ref, xa_ref, xb_ref, xf1_ref, xf2_ref, p_ref = refs
        out[...] = jnp.zeros_like(out)
        add(out, head_ref[...], 0)
        add(out, xa_ref[...], 1)
        add(out, xb_ref[...], 3)
        add(out.at[PR : PR + QH], xf1_ref[...], 2)
        add(out.at[PR + QH :], xf2_ref[...], 2)
        for dz in (1, 2, 3):
            add(out.at[:PR], p_ref[(dz - 1) * PR : dz * PR, :], 4 * dz)

    total = logits_call(first, blocks, [head, xa, xb, xf1, xf2, p])
    pb, pa, qb, qa, total = lax.optimization_barrier((pb, pa, qb, qa, total))
    pf1 = jnp.concatenate([pb[: 3 * PH], xb[:PH]], axis=0)
    pf2 = jnp.concatenate([pa[3 * PH :], xa[PH:PR]], axis=0)
    pf1, pf2 = move(pf1, "x", 1), move(pf2, "x", -1)
    qf1, qf2 = move(qb[: 2 * QR], "zh", 1), move(qa[2 * QR :], "zh", -1)

    def second(add, refs, out):
        pa_ref, pb_ref, qa_ref, qb_ref, total_ref = refs
        out[...] = total_ref[...]

        @pl.loop(0, 3)
        def _(k):
            part = rows_at(k, PR)
            add(out.at[:PR], pa_ref[part, :], 4 * k + 5)
            add(out.at[:PR], pb_ref[part, :], 4 * k + 7)

        @pl.loop(0, 4)
        def _(dx):
            part = rows_at(dx, QR)
            add(out.at[PR:], qa_ref[part, :], 4 + dx)
            add(out.at[PR:], qb_ref[part, :], 12 + dx)

    total = logits_call(second, blocks, [pa, pb, qa, qb, total])

    def third(add, refs, out):
        pf1_ref, pf2_ref, qf1_ref, qf2_ref, total_ref = refs
        out[...] = total_ref[...]
        add(out.at[:PR], pf1_ref[:PR, :], 4 + 2)
        add(out.at[:PH], pf1_ref[PR : 3 * PH, :], 8 + 2)
        add(out.at[PH:PR], pf2_ref[:PH, :], 8 + 2)
        add(out.at[:PR], pf2_ref[PH : 3 * PH, :], 12 + 2)
        add(out.at[:PH], pf1_ref[3 * PH :, :], 2)
        add(out.at[PH:PR], pf2_ref[3 * PH :, :], 2)
        add(out.at[PR:], qf1_ref[:QR, :], 8)
        add(out.at[PR:], qf1_ref[QR:, :], 8 + 1)
        add(out.at[PR:], qf2_ref[:QR, :], 8 + 2)
        add(out.at[PR:], qf2_ref[QR:, :], 8 + 3)

    total = logits_call(third, blocks, [pf1, pf2, qf1, qf2, total])
    return total, blocks


def scattered_gradient(grad, blocks):
    def array(rows, dtype):
        return jax.ShapeDtypeStruct((rows, WIDE), dtype)

    outs = [
        array(3 * PR, BF16),
        array(3 * PR, BF16),
        array(4 * QR, BF16),
        array(4 * QR, BF16),
        array(3 * PH, F32),
        array(3 * PH, F32),
        array(3 * PR, F32),
        array(4 * QH, F32),
        array(4 * QH, F32),
    ]
    def others_terms(block, refs, outs):
        (g_ref,) = refs
        p_up, p_down, q_up, q_down, p_ahead, p_behind, p_here, q_ahead, q_behind = outs

        @pl.loop(0, 3)
        def _(k):
            first, last = pl.ds(pl.multiple_of(k * PR, PR), PH), pl.ds(pl.multiple_of(k * PR + PH, PH), PH)
            kept = rows_at(k, PH)
            for dx in range(4):
                term = jnp.dot(g_ref[...], block(4 * k + dx), preferred_element_type=F32)
                one, two, three, four = term[:PH], term[PH:PR], term[PR : PR + QH], term[PR + QH :]
                if dx == 0:
                    p_here[rows_at(k, PR), :] = term[:PR]
                elif dx == 1:
                    p_ahead[kept, :] = one
                    p_up[last, :] = two.astype(BF16)
                elif dx == 2:
                    p_up[first, :] = one.astype(BF16)
                    p_down[last, :] = two.astype(BF16)
                else:
                    p_down[first, :] = one.astype(BF16)
                    p_behind[kept, :] = two
                start, middle = dx * QR, dx * QR + QH

                @pl.when(k == 0)
                def _():
                    q_ahead[dx * QH : (dx + 1) * QH, :] = three
                    q_up[middle : middle + QH, :] = four.astype(BF16)

                @pl.when(k == 1)
                def _():
                    q_up[start:middle, :] = three.astype(BF16)
                    q_down[middle : middle + QH, :] = four.astype(BF16)

                @pl.when(k == 2)
                def _():
                    q_down[start:middle, :] = three.astype(BF16)
                    q_behind[dx * QH : (dx + 1) * QH, :] = four

    slots = {place: 4 + place for place in range(12)}
    p_up, p_down, q_up, q_down, p_ahead, p_behind, p_here, q_ahead, q_behind = block_call(
        others_terms, slots, outs, blocks, [grad], 12 * ROWS
    )
    p_up, p_down = move(p_up, "x", 1), move(p_down, "x", -1)
    q_up, q_down = move(q_up, "zh", 1), move(q_down, "zh", -1)
    def own_terms(block, refs, outs):
        (g_ref,) = refs
        own, q_here = outs

        @pl.loop(0, 4)
        def _(dx):
            term = jnp.dot(g_ref[...], block(dx), preferred_element_type=F32)
            own[rows_at(dx, PR), :] = term[:PR]
            q_here[rows_at(dx, QR), :] = term[PR:]

    outs = [array(4 * PR, F32), array(4 * QR, F32)]
    own, q_here = block_call(
        own_terms, {dx: dx for dx in range(4)}, outs, blocks, [grad], 4 * ROWS
    )
    p_up, p_down, own, q_here = lax.optimization_barrier((p_up, p_down, own, q_here))

    def forward(kept_ahead, kept_behind, up, down, n, half):
        def body(a, b, u, d, up_out, down_out):
            for k in range(n):
                to, first, last = k * half, 2 * k * half, (2 * k + 1) * half
                up_out[to : to + half, :] = (
                    a[to : to + half, :] + u[first : first + half, :].astype(F32)
                ).astype(BF16)
                down_out[to : to + half, :] = (
                    b[to : to + half, :] + d[last : last + half, :].astype(F32)
                ).astype(BF16)

        return local_call(
            body, [array(n * half, BF16)] * 2, kept_ahead, kept_behind, up, down
        )

    def settle(kept, up, down, up2, down2, n, half, k):
        to, first, last = k * half, 2 * k * half, (2 * k + 1) * half
        one = kept[first : first + half, :] + down[first : first + half, :].astype(F32)
        two = kept[last : last + half, :] + up[last : last + half, :].astype(F32)
        return (
            one + up2[to : to + half, :].astype(F32),
            two + down2[to : to + half, :].astype(F32),
        )

    p_up2, p_down2 = forward(p_ahead, p_behind, p_up, p_down, 3, PH)
    p_up2, p_down2 = move(p_up2, "x", 1), move(p_down2, "x", -1)
    q_up2, q_down2 = forward(q_ahead, q_behind, q_up, q_down, 4, QH)
    q_up2, q_down2 = move(q_up2, "zh", 1), move(q_down2, "zh", -1)

    def p_body(kept, up, down, up2, down2, *outs):
        for k in range(3):
            one, two = settle(kept, up, down, up2, down2, 3, PH, k)
            outs[k][:PH, :] = one.astype(BF16)
            outs[k][PH:, :] = two.astype(BF16)

    z1, z2, z3 = local_call(
        p_body, [array(PR, BF16)] * 3, p_here, p_up, p_down, p_up2, p_down2
    )
    p_sent = z1
    z1, z2, z3 = move(z1, "zh", 1), move(z2, "zh", 2), move(z3, "zh", -1)

    def q_body(own, kept, up, down, up2, down2, _, up_out, down_out, ahead, behind, here):
        rest = PR - RH
        for dx in range(4):
            one, two = settle(kept, up, down, up2, down2, 4, QH, dx)
            first = own[dx * PR : dx * PR + RH, :]
            last = own[dx * PR + RH : (dx + 1) * PR, :]
            for ref, at_last, low in {
                0: ((here, RH, 0),),
                1: ((up_out, RH, 1),),
                2: ((down_out, RH, 1),),
                3: ((behind, 0, 0),),
            }[dx]:
                ref[at_last : at_last + rest, :] = last.astype(ref.dtype)
                ref[at_last + rest : at_last + rest + QH, :] = one.astype(ref.dtype)
                ref[at_last + rest + QH : at_last + RH, :] = two.astype(ref.dtype)
            ref = (here, ahead, up_out, down_out)[dx]
            ref[:RH, :] = first.astype(ref.dtype)

    x_up, x_down, x_ahead, x_behind, x_here = local_call(
        q_body,
        [array(ROWS, BF16), array(ROWS, BF16), array(RH, F32), array(RH, F32), array(ROWS, F32)],
        own, q_here, q_up, q_down, q_up2, q_down2, p_sent,
    )
    x_up, x_down = move(x_up, "x", 1), move(x_down, "x", -1)

    x_up2, x_down2 = forward(x_ahead, x_behind, x_up, x_down, 1, RH)
    x_up2, x_down2 = move(x_up2, "x", 1), move(x_down2, "x", -1)

    def last_body(here, xu, xd, xu2, xd2, z1, z2, z3, out):
        out[:RH, :] = here[:RH, :] + xd[:RH, :].astype(F32) + xu2[...].astype(F32)
        out[RH:, :] = here[RH:, :] + xu[RH:, :].astype(F32) + xd2[...].astype(F32)
        out[:PR, :] += z1[...].astype(F32) + z2[...].astype(F32) + z3[...].astype(F32)

    (out,) = local_call(
        last_body, [array(ROWS, F32)], x_here, x_up, x_down, x_up2, x_down2, z1, z2, z3
    )
    return out


def shards(hidden, head, targets, block_index, lse_rest, cotangent):
    zh, x, c = (lax.axis_index(a) for a in DP)
    first_row = lax.axis_index(TENSOR) * ROWS
    row_ids = first_row + lax.iota(jnp.int32, ROWS)
    block_of = row_ids // BLOCK
    block_match = (block_of[:, None] == lax.iota(jnp.int32, block_index.shape[0])[None, :]).astype(
        jnp.int32
    )
    vocab_ids = jnp.sum(block_match * block_index[None, :], axis=1) * BLOCK + row_ids % BLOCK

    k = lax.iota(jnp.int32, 16)
    at = (((zh + k // 4) % 4) * 4 + (x + k % 4) % 4) * 2
    at, sibling_at = at + c, at + (1 - c)

    facts = jnp.stack([targets.astype(F32), lse_rest, cotangent])
    facts = jnp.concatenate([facts, move(facts, "c", 1)], axis=1)
    hit = (vocab_ids[:, None] == facts[0].astype(jnp.int32)[None, :]).astype(F32)

    partial, blocks = gathered_logits(head, hidden, at, sibling_at)
    logits, stats = statistics(partial, move(partial, "c", 1), hit)
    stats = merge_four(stats, *(move(stats, "y", by) for by in (1, 2, 3)))
    loss, grad = gradient(
        logits, hit, stats, move(stats, "zl", 1), facts[1:2], facts[2:3]
    )
    return loss[0, :TOK], scattered_gradient(grad, blocks)


def solution(mesh):
    mesh = Mesh(mesh.devices.reshape(SIZES), AXES)
    placed = (P(DP, None), P(TENSOR, DP), P(DP), P(), P(DP), P(DP))
    return jax.shard_map(
        shards, mesh=mesh, in_specs=placed, out_specs=(P(DP), P(TENSOR, DP)), check_vma=False
    )
```

```python
import jax
import jax.numpy as jnp
from jax import lax
from jax.experimental import pallas as pl
from jax.experimental.pallas import tpu as pltpu
from jax.sharding import Mesh
from jax.sharding import PartitionSpec as P

BLOCK = 1024
z_weight = 0.0001

AXES = ("zh", "x", "c", "zl", "y")
SIZES = (4, 4, 2, 2, 4)
DP = ("zh", "x", "c")
TENSOR = ("zl", "y")

ROWS = 256
TOK = 512
WIDE = 512
PR, QR = 192, 64
PH, QH, RH = PR // 2, QR // 2, ROWS // 2

F32 = jnp.float32
BF16 = jnp.bfloat16
MIB = 1024 * 1024


def move(value, axis, by):
    n = SIZES[AXES.index(axis)]
    return lax.ppermute(value, axis, [(i, (i + by) % n) for i in range(n)])


def params(mib):
    return pltpu.CompilerParams(vmem_limit_bytes=mib * MIB)


def whole(shape):
    return pl.BlockSpec(shape, lambda: (0,) * len(shape))


def local_call(body, outs, *args):
    size = sum(a.size * a.dtype.itemsize for a in args) + sum(
        o.size * o.dtype.itemsize for o in outs
    )
    return pl.pallas_call(
        body,
        out_shape=outs,
        in_specs=[whole(a.shape) for a in args],
        out_specs=[whole(o.shape) for o in outs],
        compiler_params=params(16),
        cost_estimate=pl.CostEstimate(flops=0, bytes_accessed=size, transcendentals=0),
    )(*args)


def pick(hidden, at, mib):
    n = at.shape[0]

    def body(at_ref, h_ref, o_ref, arrived):
        copies = [
            pltpu.make_async_copy(
                h_ref.at[:, pl.ds(pl.multiple_of(at_ref[k] * WIDE, WIDE), WIDE)],
                o_ref.at[k],
                arrived.at[k],
            )
            for k in range(n)
        ]
        for copy in copies:
            copy.start()
        for copy in copies:
            copy.wait()

    return pl.pallas_call(
        body,
        out_shape=jax.ShapeDtypeStruct((n, TOK, WIDE), BF16),
        in_specs=[
            pl.BlockSpec(memory_space=pltpu.SMEM),
            pl.BlockSpec(memory_space=pl.ANY),
        ],
        out_specs=pl.BlockSpec(memory_space=pltpu.VMEM),
        scratch_shapes=[pltpu.SemaphoreType.DMA((n,))],
        compiler_params=params(mib),
        cost_estimate=pl.CostEstimate(
            flops=0, bytes_accessed=2 * n * TOK * WIDE * 2, transcendentals=0
        ),
    )(at, hidden)


def block_call(compute, slots, outs, blocks, others, rows):
    mine, theirs = blocks
    places = max(slots) + 1

    def body(m_ref, t_ref, *refs):
        hold, arrived = refs[-2:]

        def copies(place, slot):
            for side, ref in enumerate((m_ref.at[slot], t_ref.at[slot])):
                yield pltpu.make_async_copy(
                    ref, hold.at[place, pl.ds(side * TOK, TOK)], arrived.at[place, side]
                )

        for place, slot in slots.items():
            for copy in copies(place, slot):
                copy.start()

        def block(place, wait=True):
            if wait:
                for copy in copies(place, 0):
                    copy.wait()
            return hold[place]

        compute(block, refs[: len(others)], refs[len(others) : -2])

    return pl.pallas_call(
        body,
        out_shape=outs,
        in_specs=[pl.BlockSpec(memory_space=pl.ANY)] * 2
        + [whole(o.shape) for o in others],
        out_specs=[whole(o.shape) for o in outs],
        scratch_shapes=[
            pltpu.VMEM((places, 2 * TOK, WIDE), BF16),
            pltpu.SemaphoreType.DMA((places, 2)),
        ],
        compiler_params=params(46),
        cost_estimate=pl.CostEstimate(
            flops=4 * rows * WIDE * TOK,
            bytes_accessed=2 * len(slots) * TOK * WIDE * 2,
            transcendentals=0,
        ),
    )(mine, theirs, *others)


def logits_call(compute, blocks, others):
    mine, theirs = blocks

    def body(m_ref, t_ref, *refs):
        def add(out, a, slot):
            out[:, :TOK] += times(a, m_ref[slot])
            out[:, TOK:] += times(a, t_ref[slot])

        compute(add, refs[:-1], refs[-1])

    return local_call(body, [LOGITS], mine, theirs, *others)[0]


def times(a, block):
    return lax.dot_general(a, block, (((1,), (1,)), ((), ())), preferred_element_type=F32)


def rows_at(k, size):
    return pl.ds(pl.multiple_of(k * size, size), size)


LOGITS = jax.ShapeDtypeStruct((ROWS, 2 * TOK), F32)


def statistics(partial, other, hit):
    def body(mine, theirs, hit_ref, logits, stats):
        total = mine[...] + jnp.concatenate([theirs[:, TOK:], theirs[:, :TOK]], axis=1)
        logits[...] = total
        top = jnp.max(total, axis=0, keepdims=True)
        stats[0:1, :] = top
        stats[1:2, :] = jnp.sum(jnp.exp(total - top), axis=0, keepdims=True)
        stats[2:3, :] = jnp.sum(total * hit_ref[...], axis=0, keepdims=True)

    outs = [
        jax.ShapeDtypeStruct((ROWS, 2 * TOK), F32),
        jax.ShapeDtypeStruct((3, 2 * TOK), F32),
    ]
    return local_call(body, outs, partial, other, hit)


def merged(one, two):
    top = jnp.maximum(one[0:1, :], two[0:1, :])
    total = one[1:2, :] * jnp.exp(one[0:1, :] - top) + two[1:2, :] * jnp.exp(two[0:1, :] - top)
    return jnp.concatenate([top, total, one[2:3, :] + two[2:3, :]], axis=0)


def merge_four(mine, one, two, three):
    def body(a, b, c, d, out):
        out[...] = merged(merged(a[...], c[...]), merged(b[...], d[...]))

    return local_call(body, [jax.ShapeDtypeStruct(mine.shape, F32)], mine, one, two, three)[0]


def gradient(logits, hit, stats, other, lse_rest, cotangent):
    def body(logits_ref, hit_ref, s, o, rest, cot, loss, grad):
        whole_stats = merged(s[...], o[...])
        row_max, row_total, target_logit = (whole_stats[k : k + 1, :] for k in range(3))
        lse_window = row_max + jnp.log(row_total)
        larger = jnp.maximum(lse_window, rest[...])
        log_total = larger + jnp.log(
            jnp.exp(lse_window - larger) + jnp.exp(rest[...] - larger)
        )
        loss[...] = log_total - target_logit + z_weight * log_total * log_total
        softmax = jnp.exp(logits_ref[...] - log_total)
        grad[...] = (
            cot[...] * (softmax * (1.0 + 2.0 * z_weight * log_total) - hit_ref[...])
        ).astype(BF16)

    outs = [
        jax.ShapeDtypeStruct((1, 2 * TOK), F32),
        jax.ShapeDtypeStruct((ROWS, 2 * TOK), BF16),
    ]
    return local_call(body, outs, logits, hit, stats, other, lse_rest, cotangent)


def gathered_logits(head, hidden, at, sibling_at):
    zb, za = move(head[:PR], "zh", 1), move(head[:PR], "zh", -1)
    xb, xa = move(head, "x", 1), move(head, "x", -1)
    picked = pick(hidden, sibling_at, 44)
    zb, za, xb, xa, picked = lax.optimization_barrier((zb, za, xb, xa, picked))
    theirs = move(picked, "c", 1)
    zf1, zf2 = move(zb[:PH], "zh", 1), move(za[PH:], "zh", -1)
    xf1, xf2 = move(xb[PR : PR + QH], "x", 1), move(xa[PR + QH :], "x", -1)
    p = jnp.concatenate([za, zf1, zf2, zb], axis=0)
    q = jnp.concatenate([head[PR:], xa[PR:], xf1, xf2, xb[PR:]], axis=0)
    pb, pa = move(p, "x", 1), move(p, "x", -1)
    qb, qa = move(q, "zh", 1), move(q, "zh", -1)
    zf1, zf2, at = lax.optimization_barrier((zf1, zf2, at))
    mine = pick(hidden, at, 30)
    blocks = (mine, theirs)

    def first(add, refs, out):
        head_ref, xa_ref, xb_ref, xf1_ref, xf2_ref, p_ref = refs
        out[...] = jnp.zeros_like(out)
        add(out, head_ref[...], 0)
        add(out, xa_ref[...], 1)
        add(out, xb_ref[...], 3)
        add(out.at[PR : PR + QH], xf1_ref[...], 2)
        add(out.at[PR + QH :], xf2_ref[...], 2)
        for dz in (1, 2, 3):
            add(out.at[:PR], p_ref[(dz - 1) * PR : dz * PR, :], 4 * dz)

    total = logits_call(first, blocks, [head, xa, xb, xf1, xf2, p])
    pb, pa, qb, qa, total = lax.optimization_barrier((pb, pa, qb, qa, total))
    pf1 = jnp.concatenate([pb[: 3 * PH], xb[:PH]], axis=0)
    pf2 = jnp.concatenate([pa[3 * PH :], xa[PH:PR]], axis=0)
    pf1, pf2 = move(pf1, "x", 1), move(pf2, "x", -1)
    qf1, qf2 = move(qb[: 2 * QR], "zh", 1), move(qa[2 * QR :], "zh", -1)

    def second(add, refs, out):
        pa_ref, pb_ref, qa_ref, qb_ref, total_ref = refs
        out[...] = total_ref[...]

        @pl.loop(0, 3)
        def _(k):
            part = rows_at(k, PR)
            add(out.at[:PR], pa_ref[part, :], 4 * k + 5)
            add(out.at[:PR], pb_ref[part, :], 4 * k + 7)

        @pl.loop(0, 4)
        def _(dx):
            part = rows_at(dx, QR)
            add(out.at[PR:], qa_ref[part, :], 4 + dx)
            add(out.at[PR:], qb_ref[part, :], 12 + dx)

    total = logits_call(second, blocks, [pa, pb, qa, qb, total])

    def third(add, refs, out):
        pf1_ref, pf2_ref, qf1_ref, qf2_ref, total_ref = refs
        out[...] = total_ref[...]
        add(out.at[:PR], pf1_ref[:PR, :], 4 + 2)
        add(out.at[:PH], pf1_ref[PR : 3 * PH, :], 8 + 2)
        add(out.at[PH:PR], pf2_ref[:PH, :], 8 + 2)
        add(out.at[:PR], pf2_ref[PH : 3 * PH, :], 12 + 2)
        add(out.at[:PH], pf1_ref[3 * PH :, :], 2)
        add(out.at[PH:PR], pf2_ref[3 * PH :, :], 2)
        add(out.at[PR:], qf1_ref[:QR, :], 8)
        add(out.at[PR:], qf1_ref[QR:, :], 8 + 1)
        add(out.at[PR:], qf2_ref[:QR, :], 8 + 2)
        add(out.at[PR:], qf2_ref[QR:, :], 8 + 3)

    total = logits_call(third, blocks, [pf1, pf2, qf1, qf2, total])
    return total, blocks


def scattered_gradient(grad, blocks):
    def array(rows, dtype):
        return jax.ShapeDtypeStruct((rows, WIDE), dtype)

    outs = [
        array(3 * PR, BF16),
        array(3 * PR, BF16),
        array(4 * QR, BF16),
        array(4 * QR, BF16),
        array(3 * PH, F32),
        array(3 * PH, F32),
        array(3 * PR, F32),
        array(4 * QH, F32),
        array(4 * QH, F32),
    ]
    def others_terms(block, refs, outs):
        (g_ref,) = refs
        p_up, p_down, q_up, q_down, p_ahead, p_behind, p_here, q_ahead, q_behind, q_scratch = outs

        @pl.loop(0, 3)
        def _(k):
            first, last = pl.ds(pl.multiple_of(k * PR, PR), PH), pl.ds(pl.multiple_of(k * PR + PH, PH), PH)
            kept = rows_at(k, PH)
            held = [block(4 * k + dx) for dx in range(4)]
            for dx in (2, 1, 3, 0):
                term = jnp.dot(g_ref[:, :TOK], held[dx][:TOK], preferred_element_type=F32)
                term += jnp.dot(g_ref[:, TOK:], held[dx][TOK:], preferred_element_type=F32)
                one, two = term[:PH], term[PH:PR]
                if dx == 0:
                    p_here[rows_at(k, PR), :] = term[:PR]
                elif dx == 1:
                    p_ahead[kept, :] = one
                    p_up[last, :] = two.astype(BF16)
                elif dx == 2:
                    p_up[first, :] = one.astype(BF16)
                    p_down[last, :] = two.astype(BF16)
                else:
                    p_down[first, :] = one.astype(BF16)
                    p_behind[kept, :] = two
                q_scratch[dx] = term[PR:]

            for dx in range(4):
                start, middle = dx * QR, dx * QR + QH
                three, four = q_scratch[dx, :QH], q_scratch[dx, QH:]

                @pl.when(k == 0)
                def _():
                    q_ahead[dx * QH : (dx + 1) * QH, :] = three
                    q_up[middle : middle + QH, :] = four.astype(BF16)

                @pl.when(k == 1)
                def _():
                    q_up[start:middle, :] = three.astype(BF16)
                    q_down[middle : middle + QH, :] = four.astype(BF16)

                @pl.when(k == 2)
                def _():
                    q_down[start:middle, :] = three.astype(BF16)
                    q_behind[dx * QH : (dx + 1) * QH, :] = four

    slots = {place: 4 + place for place in range(12)}
    q_rows = jax.ShapeDtypeStruct((4, QR, WIDE), F32)
    p_up, p_down, q_up, q_down, p_ahead, p_behind, p_here, q_ahead, q_behind, _ = block_call(
        others_terms, slots, outs + [q_rows], blocks, [grad], 12 * ROWS
    )
    p_up, p_down = move(p_up, "x", 1), move(p_down, "x", -1)
    q_up, q_down = move(q_up, "zh", 1), move(q_down, "zh", -1)
    def own_terms(block, refs, outs):
        (g_ref,) = refs
        own, q_here = outs

        @pl.loop(0, 4)
        def _(dx):
            term = jnp.dot(g_ref[...], block(dx), preferred_element_type=F32)
            own[rows_at(dx, PR), :] = term[:PR]
            q_here[rows_at(dx, QR), :] = term[PR:]

    outs = [array(4 * PR, F32), array(4 * QR, F32)]
    own, q_here = block_call(
        own_terms, {dx: dx for dx in range(4)}, outs, blocks, [grad], 4 * ROWS
    )
    p_up, p_down, own, q_here = lax.optimization_barrier((p_up, p_down, own, q_here))

    def forward(kept_ahead, kept_behind, up, down, n, half):
        def body(a, b, u, d, up_out, down_out):
            for k in range(n):
                to, first, last = k * half, 2 * k * half, (2 * k + 1) * half
                up_out[to : to + half, :] = (
                    a[to : to + half, :] + u[first : first + half, :].astype(F32)
                ).astype(BF16)
                down_out[to : to + half, :] = (
                    b[to : to + half, :] + d[last : last + half, :].astype(F32)
                ).astype(BF16)

        return local_call(
            body, [array(n * half, BF16)] * 2, kept_ahead, kept_behind, up, down
        )

    def settle(kept, up, down, up2, down2, n, half, k):
        to, first, last = k * half, 2 * k * half, (2 * k + 1) * half
        one = kept[first : first + half, :] + down[first : first + half, :].astype(F32)
        two = kept[last : last + half, :] + up[last : last + half, :].astype(F32)
        return (
            one + up2[to : to + half, :].astype(F32),
            two + down2[to : to + half, :].astype(F32),
        )

    p_up2, p_down2 = forward(p_ahead, p_behind, p_up, p_down, 3, PH)
    p_up2, p_down2 = move(p_up2, "x", 1), move(p_down2, "x", -1)
    q_up2, q_down2 = forward(q_ahead, q_behind, q_up, q_down, 4, QH)
    q_up2, q_down2 = move(q_up2, "zh", 1), move(q_down2, "zh", -1)

    def p_body(kept, up, down, up2, down2, *outs):
        for k in range(3):
            one, two = settle(kept, up, down, up2, down2, 3, PH, k)
            outs[k][:PH, :] = one.astype(BF16)
            outs[k][PH:, :] = two.astype(BF16)

    z1, z2, z3 = local_call(
        p_body, [array(PR, BF16)] * 3, p_here, p_up, p_down, p_up2, p_down2
    )
    p_sent = z1
    z1, z2, z3 = move(z1, "zh", 1), move(z2, "zh", 2), move(z3, "zh", -1)

    def q_body(own, kept, up, down, up2, down2, _, up_out, down_out, ahead, behind, here):
        rest = PR - RH
        for dx in range(4):
            one, two = settle(kept, up, down, up2, down2, 4, QH, dx)
            first = own[dx * PR : dx * PR + RH, :]
            last = own[dx * PR + RH : (dx + 1) * PR, :]
            for ref, at_last, low in {
                0: ((here, RH, 0),),
                1: ((up_out, RH, 1),),
                2: ((down_out, RH, 1),),
                3: ((behind, 0, 0),),
            }[dx]:
                ref[at_last : at_last + rest, :] = last.astype(ref.dtype)
                ref[at_last + rest : at_last + rest + QH, :] = one.astype(ref.dtype)
                ref[at_last + rest + QH : at_last + RH, :] = two.astype(ref.dtype)
            ref = (here, ahead, up_out, down_out)[dx]
            ref[:RH, :] = first.astype(ref.dtype)

    x_up, x_down, x_ahead, x_behind, x_here = local_call(
        q_body,
        [array(ROWS, BF16), array(ROWS, BF16), array(RH, F32), array(RH, F32), array(ROWS, F32)],
        own, q_here, q_up, q_down, q_up2, q_down2, p_sent,
    )
    x_up, x_down = move(x_up, "x", 1), move(x_down, "x", -1)

    x_up2, x_down2 = forward(x_ahead, x_behind, x_up, x_down, 1, RH)
    x_up2, x_down2 = move(x_up2, "x", 1), move(x_down2, "x", -1)

    def last_body(here, xu, xd, xu2, xd2, z1, z2, z3, out):
        out[:RH, :] = here[:RH, :] + xd[:RH, :].astype(F32) + xu2[...].astype(F32)
        out[RH:, :] = here[RH:, :] + xu[RH:, :].astype(F32) + xd2[...].astype(F32)
        out[:PR, :] += z1[...].astype(F32) + z2[...].astype(F32) + z3[...].astype(F32)

    (out,) = local_call(
        last_body, [array(ROWS, F32)], x_here, x_up, x_down, x_up2, x_down2, z1, z2, z3
    )
    return out


def shards(hidden, head, targets, block_index, lse_rest, cotangent):
    zh, x, c = (lax.axis_index(a) for a in DP)
    first_row = lax.axis_index(TENSOR) * ROWS
    row_ids = first_row + lax.iota(jnp.int32, ROWS)
    block_of = row_ids // BLOCK
    block_match = (block_of[:, None] == lax.iota(jnp.int32, block_index.shape[0])[None, :]).astype(
        jnp.int32
    )
    vocab_ids = jnp.sum(block_match * block_index[None, :], axis=1) * BLOCK + row_ids % BLOCK

    k = lax.iota(jnp.int32, 16)
    at = (((zh + k // 4) % 4) * 4 + (x + k % 4) % 4) * 2
    at, sibling_at = at + c, at + (1 - c)

    facts = jnp.stack([targets.astype(F32), lse_rest, cotangent])
    facts = jnp.concatenate([facts, move(facts, "c", 1)], axis=1)
    hit = (vocab_ids[:, None] == facts[0].astype(jnp.int32)[None, :]).astype(F32)

    partial, blocks = gathered_logits(head, hidden, at, sibling_at)
    logits, stats = statistics(partial, move(partial, "c", 1), hit)
    stats = merge_four(stats, *(move(stats, "y", by) for by in (1, 2, 3)))
    loss, grad = gradient(
        logits, hit, stats, move(stats, "zl", 1), facts[1:2], facts[2:3]
    )
    return loss[0, :TOK], scattered_gradient(grad, blocks)


def solution(mesh):
    mesh = Mesh(mesh.devices.reshape(SIZES), AXES)
    placed = (P(DP, None), P(TENSOR, DP), P(DP), P(), P(DP), P(DP))
    return jax.shard_map(
        shards, mesh=mesh, in_specs=placed, out_specs=(P(DP), P(TENSOR, DP)), check_vma=False
    )
```

```python
import jax
import jax.numpy as jnp
from jax import lax
from jax.experimental import pallas as pl
from jax.experimental.pallas import tpu as pltpu
from jax.sharding import Mesh
from jax.sharding import PartitionSpec as P

BLOCK = 1024
z_weight = 0.0001

AXES = ("zh", "x", "c", "zl", "y")
SIZES = (4, 4, 2, 2, 4)
DP = ("zh", "x", "c")
TENSOR = ("zl", "y")

ROWS = 256
TOK = 512
WIDE = 512
PR, QR = 192, 64
PH, QH, RH = PR // 2, QR // 2, ROWS // 2

F32 = jnp.float32
BF16 = jnp.bfloat16
MIB = 1024 * 1024


def move(value, axis, by):
    n = SIZES[AXES.index(axis)]
    return lax.ppermute(value, axis, [(i, (i + by) % n) for i in range(n)])


def params(mib):
    return pltpu.CompilerParams(vmem_limit_bytes=mib * MIB)


def whole(shape):
    return pl.BlockSpec(shape, lambda: (0,) * len(shape))


def local_call(body, outs, *args):
    size = sum(a.size * a.dtype.itemsize for a in args) + sum(
        o.size * o.dtype.itemsize for o in outs
    )
    return pl.pallas_call(
        body,
        out_shape=outs,
        in_specs=[whole(a.shape) for a in args],
        out_specs=[whole(o.shape) for o in outs],
        compiler_params=params(16),
        cost_estimate=pl.CostEstimate(flops=0, bytes_accessed=size, transcendentals=0),
    )(*args)


def joined(*parts, after=()):
    def body(*refs):
        to = 0
        for ref, (_, start, rows) in zip(refs, parts):
            refs[-1][to : to + rows, :] = ref[start : start + rows, :]
            to += rows

    out = jax.ShapeDtypeStruct((sum(rows for _, _, rows in parts), WIDE), BF16)
    return local_call(body, [out], *(array for array, _, _ in parts), *after)[0]


def pick(hidden, at, mib):
    n = at.shape[0]

    def body(at_ref, h_ref, o_ref, arrived):
        copies = [
            pltpu.make_async_copy(
                h_ref.at[:, pl.ds(pl.multiple_of(at_ref[k] * WIDE, WIDE), WIDE)],
                o_ref.at[k],
                arrived.at[k],
            )
            for k in range(n)
        ]
        for copy in copies:
            copy.start()
        for copy in copies:
            copy.wait()

    return pl.pallas_call(
        body,
        out_shape=jax.ShapeDtypeStruct((n, TOK, WIDE), BF16),
        in_specs=[
            pl.BlockSpec(memory_space=pltpu.SMEM),
            pl.BlockSpec(memory_space=pl.ANY),
        ],
        out_specs=pl.BlockSpec(memory_space=pltpu.VMEM),
        scratch_shapes=[pltpu.SemaphoreType.DMA((n,))],
        compiler_params=params(mib),
        cost_estimate=pl.CostEstimate(
            flops=0, bytes_accessed=2 * n * TOK * WIDE * 2, transcendentals=0
        ),
    )(at, hidden)


def block_call(compute, slots, outs, blocks, others, rows):
    mine, theirs = blocks
    places = max(slots) + 1

    def body(m_ref, t_ref, *refs):
        hold, arrived = refs[-2:]

        def copies(place, slot):
            for side, ref in enumerate((m_ref.at[slot], t_ref.at[slot])):
                yield pltpu.make_async_copy(
                    ref, hold.at[place, pl.ds(side * TOK, TOK)], arrived.at[place, side]
                )

        for place, slot in slots.items():
            for copy in copies(place, slot):
                copy.start()

        def block(place, wait=True):
            if wait:
                for copy in copies(place, 0):
                    copy.wait()
            return hold[place]

        compute(block, refs[: len(others)], refs[len(others) : -2])

    return pl.pallas_call(
        body,
        out_shape=outs,
        in_specs=[pl.BlockSpec(memory_space=pl.ANY)] * 2
        + [whole(o.shape) for o in others],
        out_specs=[whole(o.shape) for o in outs],
        scratch_shapes=[
            pltpu.VMEM((places, 2 * TOK, WIDE), BF16),
            pltpu.SemaphoreType.DMA((places, 2)),
        ],
        compiler_params=params(46),
        cost_estimate=pl.CostEstimate(
            flops=4 * rows * WIDE * TOK,
            bytes_accessed=2 * len(slots) * TOK * WIDE * 2,
            transcendentals=0,
        ),
    )(mine, theirs, *others)


def logits_call(compute, blocks, others):
    mine, theirs = blocks

    def body(m_ref, t_ref, *refs):
        def add(out, a, slot):
            out[:, :TOK] += times(a, m_ref[slot])
            out[:, TOK:] += times(a, t_ref[slot])

        compute(add, refs[:-1], refs[-1])

    return local_call(body, [LOGITS], mine, theirs, *others)[0]


def times(a, block):
    return lax.dot_general(a, block, (((1,), (1,)), ((), ())), preferred_element_type=F32)


def rows_at(k, size):
    return pl.ds(pl.multiple_of(k * size, size), size)


LOGITS = jax.ShapeDtypeStruct((ROWS, 2 * TOK), F32)


def statistics(partial, other, hit):
    def body(mine, theirs, hit_ref, logits, stats):
        total = mine[...] + jnp.concatenate([theirs[:, TOK:], theirs[:, :TOK]], axis=1)
        logits[...] = total
        top = jnp.max(total, axis=0, keepdims=True)
        stats[0:1, :] = top
        stats[1:2, :] = jnp.sum(jnp.exp(total - top), axis=0, keepdims=True)
        stats[2:3, :] = jnp.sum(total * hit_ref[...], axis=0, keepdims=True)

    outs = [
        jax.ShapeDtypeStruct((ROWS, 2 * TOK), F32),
        jax.ShapeDtypeStruct((3, 2 * TOK), F32),
    ]
    return local_call(body, outs, partial, other, hit)


def merged(one, two):
    top = jnp.maximum(one[0:1, :], two[0:1, :])
    total = one[1:2, :] * jnp.exp(one[0:1, :] - top) + two[1:2, :] * jnp.exp(two[0:1, :] - top)
    return jnp.concatenate([top, total, one[2:3, :] + two[2:3, :]], axis=0)


def merge_four(mine, one, two, three):
    def body(a, b, c, d, out):
        out[...] = merged(merged(a[...], c[...]), merged(b[...], d[...]))

    return local_call(body, [jax.ShapeDtypeStruct(mine.shape, F32)], mine, one, two, three)[0]


def gradient(logits, hit, stats, other, lse_rest, cotangent):
    def body(logits_ref, hit_ref, s, o, rest, cot, loss, grad):
        whole_stats = merged(s[...], o[...])
        row_max, row_total, target_logit = (whole_stats[k : k + 1, :] for k in range(3))
        lse_window = row_max + jnp.log(row_total)
        larger = jnp.maximum(lse_window, rest[...])
        log_total = larger + jnp.log(
            jnp.exp(lse_window - larger) + jnp.exp(rest[...] - larger)
        )
        loss[...] = log_total - target_logit + z_weight * log_total * log_total
        softmax = jnp.exp(logits_ref[...] - log_total)
        grad[...] = (
            cot[...] * (softmax * (1.0 + 2.0 * z_weight * log_total) - hit_ref[...])
        ).astype(BF16)

    outs = [
        jax.ShapeDtypeStruct((1, 2 * TOK), F32),
        jax.ShapeDtypeStruct((ROWS, 2 * TOK), BF16),
    ]
    return local_call(body, outs, logits, hit, stats, other, lse_rest, cotangent)


def gathered_logits(head, hidden, at, sibling_at):
    def split(h, over_zh, over_x):
        over_zh[...] = h[:PR, :]
        over_x[...] = h[PH:, :]

    over_zh, over_x = local_call(
        split, [jax.ShapeDtypeStruct((r, WIDE), BF16) for r in (PR, ROWS - PH)], head
    )
    zb, za = move(over_zh, "zh", 1), move(over_zh, "zh", -1)
    xb, xa = move(over_x, "x", 1), move(over_x, "x", -1)
    picked = pick(hidden, sibling_at, 44)
    zb, za, xb, xa, picked = lax.optimization_barrier((zb, za, xb, xa, picked))
    theirs = move(picked, "c", 1)
    zf1, zf2 = move(zb[:PH], "zh", 1), move(za[PH:], "zh", -1)
    xf1, xf2 = move(xb[PH : PH + QH], "x", 1), move(xa[PH + QH :], "x", -1)
    q = joined((over_x, PH, QR), (xa, PH, QR), (xf1, 0, QH), (xf2, 0, QH), (xb, PH, QR))
    p = joined((za, 0, PR), (zf1, 0, PH), (zf2, 0, PH), (zb, 0, PR), (over_zh, 0, PH), after=[q])
    pb, pa = move(p, "x", 1), move(p, "x", -1)
    qb, qa = move(q, "zh", 1), move(q, "zh", -1)
    zf1, zf2, at = lax.optimization_barrier((zf1, zf2, at))
    mine = pick(hidden, at, 30)
    blocks = (mine, theirs)

    def first(add, refs, out):
        head_ref, xa_ref, xb_ref, xf1_ref, xf2_ref, p_ref = refs
        out[...] = jnp.zeros_like(out)
        add(out, head_ref[...], 0)
        add(out.at[PH:], xa_ref[...], 1)
        add(out.at[PH:], xb_ref[...], 3)
        add(out.at[PR : PR + QH], xf1_ref[...], 2)
        add(out.at[PR + QH :], xf2_ref[...], 2)
        for dz in (1, 2, 3):
            add(out.at[:PR], p_ref[(dz - 1) * PR : dz * PR, :], 4 * dz)

    total = logits_call(first, blocks, [head, xa, xb, xf1, xf2, p])
    pb, pa, qb, qa, total = lax.optimization_barrier((pb, pa, qb, qa, total))
    pf1 = joined((pb, 0, 3 * PH), (pb, 3 * PR, PH))
    pf2 = joined((pa, 3 * PH, 3 * PH), (xa, 0, PH))
    pf1, pf2 = move(pf1, "x", 1), move(pf2, "x", -1)
    qf1, qf2 = move(qb[: 2 * QR], "zh", 1), move(qa[2 * QR :], "zh", -1)

    def second(add, refs, out):
        pa_ref, pb_ref, qa_ref, qb_ref, total_ref = refs
        out[...] = total_ref[...]

        add(out.at[:PH], pa_ref[3 * PR :, :], 1)
        add(out.at[:PH], pb_ref[3 * PR :, :], 3)

        @pl.loop(0, 3)
        def _(k):
            part = rows_at(k, PR)
            add(out.at[:PR], pa_ref[part, :], 4 * k + 5)
            add(out.at[:PR], pb_ref[part, :], 4 * k + 7)

        @pl.loop(0, 4)
        def _(dx):
            part = rows_at(dx, QR)
            add(out.at[PR:], qa_ref[part, :], 4 + dx)
            add(out.at[PR:], qb_ref[part, :], 12 + dx)

    total = logits_call(second, blocks, [pa, pb, qa, qb, total])

    def third(add, refs, out):
        pf1_ref, pf2_ref, qf1_ref, qf2_ref, total_ref = refs
        out[...] = total_ref[...]
        add(out.at[:PR], pf1_ref[:PR, :], 4 + 2)
        add(out.at[:PH], pf1_ref[PR : 3 * PH, :], 8 + 2)
        add(out.at[PH:PR], pf2_ref[:PH, :], 8 + 2)
        add(out.at[:PR], pf2_ref[PH : 3 * PH, :], 12 + 2)
        add(out.at[:PH], pf1_ref[3 * PH :, :], 2)
        add(out.at[PH:PR], pf2_ref[3 * PH :, :], 2)
        add(out.at[PR:], qf1_ref[:QR, :], 8)
        add(out.at[PR:], qf1_ref[QR:, :], 8 + 1)
        add(out.at[PR:], qf2_ref[:QR, :], 8 + 2)
        add(out.at[PR:], qf2_ref[QR:, :], 8 + 3)

    total = logits_call(third, blocks, [pf1, pf2, qf1, qf2, total])
    return total, blocks


def scattered_gradient(grad, blocks):
    def array(rows, dtype):
        return jax.ShapeDtypeStruct((rows, WIDE), dtype)

    outs = [
        array(3 * PR, BF16),
        array(3 * PR, BF16),
        array(4 * QR, BF16),
        array(4 * QR, BF16),
        array(3 * PH, F32),
        array(3 * PH, F32),
        array(3 * PR, F32),
        array(4 * QH, F32),
        array(4 * QH, F32),
    ]
    def others_terms(block, refs, outs):
        (g_ref,) = refs
        p_up, p_down, q_up, q_down, p_ahead, p_behind, p_here, q_ahead, q_behind, q_scratch = outs

        @pl.loop(0, 3)
        def _(k):
            first, last = pl.ds(pl.multiple_of(k * PR, PR), PH), pl.ds(pl.multiple_of(k * PR + PH, PH), PH)
            kept = rows_at(k, PH)
            held = [block(4 * k + dx) for dx in range(4)]
            for dx in (2, 1, 3, 0):
                term = jnp.dot(g_ref[:, :TOK], held[dx][:TOK], preferred_element_type=F32)
                term += jnp.dot(g_ref[:, TOK:], held[dx][TOK:], preferred_element_type=F32)
                one, two = term[:PH], term[PH:PR]
                if dx == 0:
                    p_here[rows_at(k, PR), :] = term[:PR]
                elif dx == 1:
                    p_ahead[kept, :] = one
                    p_up[last, :] = two.astype(BF16)
                elif dx == 2:
                    p_up[first, :] = one.astype(BF16)
                    p_down[last, :] = two.astype(BF16)
                else:
                    p_down[first, :] = one.astype(BF16)
                    p_behind[kept, :] = two
                q_scratch[dx] = term[PR:]

            for dx in range(4):
                start, middle = dx * QR, dx * QR + QH
                three, four = q_scratch[dx, :QH], q_scratch[dx, QH:]

                @pl.when(k == 0)
                def _():
                    q_ahead[dx * QH : (dx + 1) * QH, :] = three
                    q_up[middle : middle + QH, :] = four.astype(BF16)

                @pl.when(k == 1)
                def _():
                    q_up[start:middle, :] = three.astype(BF16)
                    q_down[middle : middle + QH, :] = four.astype(BF16)

                @pl.when(k == 2)
                def _():
                    q_down[start:middle, :] = three.astype(BF16)
                    q_behind[dx * QH : (dx + 1) * QH, :] = four

    slots = {place: 4 + place for place in range(12)}
    q_rows = jax.ShapeDtypeStruct((4, QR, WIDE), F32)
    p_up, p_down, q_up, q_down, p_ahead, p_behind, p_here, q_ahead, q_behind, _ = block_call(
        others_terms, slots, outs + [q_rows], blocks, [grad], 12 * ROWS
    )
    p_up, p_down = move(p_up, "x", 1), move(p_down, "x", -1)
    q_up, q_down = move(q_up, "zh", 1), move(q_down, "zh", -1)
    def own_terms(block, refs, outs):
        (g_ref,) = refs
        own, q_here = outs

        @pl.loop(0, 4)
        def _(dx):
            term = jnp.dot(g_ref[...], block(dx), preferred_element_type=F32)
            own[rows_at(dx, PR), :] = term[:PR]
            q_here[rows_at(dx, QR), :] = term[PR:]

    outs = [array(4 * PR, F32), array(4 * QR, F32)]
    own, q_here = block_call(
        own_terms, {dx: dx for dx in range(4)}, outs, blocks, [grad], 4 * ROWS
    )
    p_up, p_down, own, q_here = lax.optimization_barrier((p_up, p_down, own, q_here))

    def forward(kept_ahead, kept_behind, up, down, n, half):
        def body(a, b, u, d, up_out, down_out):
            for k in range(n):
                to, first, last = k * half, 2 * k * half, (2 * k + 1) * half
                up_out[to : to + half, :] = (
                    a[to : to + half, :] + u[first : first + half, :].astype(F32)
                ).astype(BF16)
                down_out[to : to + half, :] = (
                    b[to : to + half, :] + d[last : last + half, :].astype(F32)
                ).astype(BF16)

        return local_call(
            body, [array(n * half, BF16)] * 2, kept_ahead, kept_behind, up, down
        )

    def settle(kept, up, down, up2, down2, n, half, k):
        to, first, last = k * half, 2 * k * half, (2 * k + 1) * half
        one = kept[first : first + half, :] + down[first : first + half, :].astype(F32)
        two = kept[last : last + half, :] + up[last : last + half, :].astype(F32)
        return (
            one + up2[to : to + half, :].astype(F32),
            two + down2[to : to + half, :].astype(F32),
        )

    p_up2, p_down2 = forward(p_ahead, p_behind, p_up, p_down, 3, PH)
    p_up2, p_down2 = move(p_up2, "x", 1), move(p_down2, "x", -1)
    q_up2, q_down2 = forward(q_ahead, q_behind, q_up, q_down, 4, QH)
    q_up2, q_down2 = move(q_up2, "zh", 1), move(q_down2, "zh", -1)

    def p_body(kept, up, down, up2, down2, *outs):
        for k in range(3):
            one, two = settle(kept, up, down, up2, down2, 3, PH, k)
            outs[k][:PH, :] = one.astype(BF16)
            outs[k][PH:, :] = two.astype(BF16)

    z1, z2, z3 = local_call(
        p_body, [array(PR, BF16)] * 3, p_here, p_up, p_down, p_up2, p_down2
    )
    p_sent = z1
    z1, z2, z3 = move(z1, "zh", 1), move(z2, "zh", 2), move(z3, "zh", -1)

    def q_body(own, kept, up, down, up2, down2, _, up_out, down_out, ahead, behind, here):
        rest = PR - RH
        for dx in range(4):
            one, two = settle(kept, up, down, up2, down2, 4, QH, dx)
            first = own[dx * PR : dx * PR + RH, :]
            last = own[dx * PR + RH : (dx + 1) * PR, :]
            for ref, at_last, low in {
                0: ((here, RH, 0),),
                1: ((up_out, RH, 1),),
                2: ((down_out, RH, 1),),
                3: ((behind, 0, 0),),
            }[dx]:
                ref[at_last : at_last + rest, :] = last.astype(ref.dtype)
                ref[at_last + rest : at_last + rest + QH, :] = one.astype(ref.dtype)
                ref[at_last + rest + QH : at_last + RH, :] = two.astype(ref.dtype)
            ref = (here, ahead, up_out, down_out)[dx]
            ref[:RH, :] = first.astype(ref.dtype)

    x_up, x_down, x_ahead, x_behind, x_here = local_call(
        q_body,
        [array(ROWS, BF16), array(ROWS, BF16), array(RH, F32), array(RH, F32), array(ROWS, F32)],
        own, q_here, q_up, q_down, q_up2, q_down2, p_sent,
    )
    x_up, x_down = move(x_up, "x", 1), move(x_down, "x", -1)

    x_up2, x_down2 = forward(x_ahead, x_behind, x_up, x_down, 1, RH)
    x_up2, x_down2 = move(x_up2, "x", 1), move(x_down2, "x", -1)

    def last_body(here, xu, xd, xu2, xd2, z1, z2, z3, out):
        out[:RH, :] = here[:RH, :] + xd[:RH, :].astype(F32) + xu2[...].astype(F32)
        out[RH:, :] = here[RH:, :] + xu[RH:, :].astype(F32) + xd2[...].astype(F32)
        out[:PR, :] += z1[...].astype(F32) + z2[...].astype(F32) + z3[...].astype(F32)

    (out,) = local_call(
        last_body, [array(ROWS, F32)], x_here, x_up, x_down, x_up2, x_down2, z1, z2, z3
    )
    return out


def shards(hidden, head, targets, block_index, lse_rest, cotangent):
    zh, x, c = (lax.axis_index(a) for a in DP)
    first_row = lax.axis_index(TENSOR) * ROWS
    row_ids = first_row + lax.iota(jnp.int32, ROWS)
    block_of = row_ids // BLOCK
    block_match = (block_of[:, None] == lax.iota(jnp.int32, block_index.shape[0])[None, :]).astype(
        jnp.int32
    )
    vocab_ids = jnp.sum(block_match * block_index[None, :], axis=1) * BLOCK + row_ids % BLOCK

    k = lax.iota(jnp.int32, 16)
    at = (((zh + k // 4) % 4) * 4 + (x + k % 4) % 4) * 2
    at, sibling_at = at + c, at + (1 - c)

    facts = jnp.stack([targets.astype(F32), lse_rest, cotangent])
    facts = jnp.concatenate([facts, move(facts, "c", 1)], axis=1)
    hit = (vocab_ids[:, None] == facts[0].astype(jnp.int32)[None, :]).astype(F32)

    partial, blocks = gathered_logits(head, hidden, at, sibling_at)
    logits, stats = statistics(partial, move(partial, "c", 1), hit)
    stats = merge_four(stats, *(move(stats, "y", by) for by in (1, 2, 3)))
    loss, grad = gradient(
        logits, hit, stats, move(stats, "zl", 1), facts[1:2], facts[2:3]
    )
    return loss[0, :TOK], scattered_gradient(grad, blocks)


def solution(mesh):
    mesh = Mesh(mesh.devices.reshape(SIZES), AXES)
    placed = (P(DP, None), P(TENSOR, DP), P(DP), P(), P(DP), P(DP))
    return jax.shard_map(
        shards, mesh=mesh, in_specs=placed, out_specs=(P(DP), P(TENSOR, DP)), check_vma=False
    )
```

```python
import jax
import jax.numpy as jnp
from jax import lax
from jax.experimental import pallas as pl
from jax.experimental.pallas import tpu as pltpu
from jax.sharding import Mesh
from jax.sharding import PartitionSpec as P

BLOCK = 1024
z_weight = 0.0001

AXES = ("zh", "x", "c", "zl", "y")
SIZES = (4, 4, 2, 2, 4)
DP = ("zh", "x", "c")
TENSOR = ("zl", "y")

ROWS = 256
TOK = 512
WIDE = 512
PR, QR = 192, 64
PH, QH, RH = PR // 2, QR // 2, ROWS // 2

F32 = jnp.float32
BF16 = jnp.bfloat16
MIB = 1024 * 1024


def move(value, axis, by):
    n = SIZES[AXES.index(axis)]
    return lax.ppermute(value, axis, [(i, (i + by) % n) for i in range(n)])


def params(mib):
    return pltpu.CompilerParams(vmem_limit_bytes=mib * MIB)


def whole(shape):
    return pl.BlockSpec(shape, lambda: (0,) * len(shape))


def local_call(body, outs, *args):
    size = sum(a.size * a.dtype.itemsize for a in args) + sum(
        o.size * o.dtype.itemsize for o in outs
    )
    return pl.pallas_call(
        body,
        out_shape=outs,
        in_specs=[whole(a.shape) for a in args],
        out_specs=[whole(o.shape) for o in outs],
        compiler_params=params(16),
        cost_estimate=pl.CostEstimate(flops=0, bytes_accessed=size, transcendentals=0),
    )(*args)


def joined(*parts, after=()):
    def body(*refs):
        to = 0
        for ref, (_, start, rows) in zip(refs, parts):
            refs[-1][to : to + rows, :] = ref[start : start + rows, :]
            to += rows

    out = jax.ShapeDtypeStruct((sum(rows for _, _, rows in parts), WIDE), BF16)
    return local_call(body, [out], *(array for array, _, _ in parts), *after)[0]


def pick(hidden, at, mib):
    n = at.shape[0]

    def body(at_ref, h_ref, o_ref, arrived):
        copies = [
            pltpu.make_async_copy(
                h_ref.at[:, pl.ds(pl.multiple_of(at_ref[k] * WIDE, WIDE), WIDE)],
                o_ref.at[k],
                arrived.at[k],
            )
            for k in range(n)
        ]
        for copy in copies:
            copy.start()
        for copy in copies:
            copy.wait()

    return pl.pallas_call(
        body,
        out_shape=jax.ShapeDtypeStruct((n, TOK, WIDE), BF16),
        in_specs=[
            pl.BlockSpec(memory_space=pltpu.SMEM),
            pl.BlockSpec(memory_space=pl.ANY),
        ],
        out_specs=pl.BlockSpec(memory_space=pltpu.VMEM),
        scratch_shapes=[pltpu.SemaphoreType.DMA((n,))],
        compiler_params=params(mib),
        cost_estimate=pl.CostEstimate(
            flops=0, bytes_accessed=2 * n * TOK * WIDE * 2, transcendentals=0
        ),
    )(at, hidden)


def block_call(compute, slots, outs, blocks, others, rows):
    mine, theirs = blocks
    places = max(slots) + 1

    def body(m_ref, t_ref, *refs):
        hold, arrived = refs[-2:]

        def copies(place, slot):
            for side, ref in enumerate((m_ref.at[slot], t_ref.at[slot])):
                yield pltpu.make_async_copy(
                    ref, hold.at[place, pl.ds(side * TOK, TOK)], arrived.at[place, side]
                )

        for place, slot in slots.items():
            for copy in copies(place, slot):
                copy.start()

        def block(place, wait=True):
            if wait:
                for copy in copies(place, 0):
                    copy.wait()
            return hold[place]

        compute(block, refs[: len(others)], refs[len(others) : -2])

    return pl.pallas_call(
        body,
        out_shape=outs,
        in_specs=[pl.BlockSpec(memory_space=pl.ANY)] * 2
        + [whole(o.shape) for o in others],
        out_specs=[whole(o.shape) for o in outs],
        scratch_shapes=[
            pltpu.VMEM((places, 2 * TOK, WIDE), BF16),
            pltpu.SemaphoreType.DMA((places, 2)),
        ],
        compiler_params=params(46),
        cost_estimate=pl.CostEstimate(
            flops=4 * rows * WIDE * TOK,
            bytes_accessed=2 * len(slots) * TOK * WIDE * 2,
            transcendentals=0,
        ),
    )(mine, theirs, *others)


def logits_call(compute, blocks, others):
    mine, theirs = blocks

    def body(m_ref, t_ref, *refs):
        def add(out, a, slot):
            out[:, :TOK] += times(a, m_ref[slot])
            out[:, TOK:] += times(a, t_ref[slot])

        compute(add, refs[:-1], refs[-1])

    return local_call(body, [LOGITS], mine, theirs, *others)[0]


def times(a, block):
    return lax.dot_general(a, block, (((1,), (1,)), ((), ())), preferred_element_type=F32)


def rows_at(k, size):
    return pl.ds(pl.multiple_of(k * size, size), size)


LOGITS = jax.ShapeDtypeStruct((ROWS, 2 * TOK), F32)


def statistics(partial, other, hit):
    def body(mine, theirs, hit_ref, logits, stats):
        total = mine[...] + jnp.concatenate([theirs[:, TOK:], theirs[:, :TOK]], axis=1)
        logits[...] = total
        top = jnp.max(total, axis=0, keepdims=True)
        stats[0:1, :] = top
        stats[1:2, :] = jnp.sum(jnp.exp(total - top), axis=0, keepdims=True)
        stats[2:3, :] = jnp.sum(total * hit_ref[...], axis=0, keepdims=True)

    outs = [
        jax.ShapeDtypeStruct((ROWS, 2 * TOK), F32),
        jax.ShapeDtypeStruct((3, 2 * TOK), F32),
    ]
    return local_call(body, outs, partial, other, hit)


def merged(one, two):
    top = jnp.maximum(one[0:1, :], two[0:1, :])
    total = one[1:2, :] * jnp.exp(one[0:1, :] - top) + two[1:2, :] * jnp.exp(two[0:1, :] - top)
    return jnp.concatenate([top, total, one[2:3, :] + two[2:3, :]], axis=0)


def merge_four(mine, one, two, three):
    def body(a, b, c, d, out):
        out[...] = merged(merged(a[...], c[...]), merged(b[...], d[...]))

    return local_call(body, [jax.ShapeDtypeStruct(mine.shape, F32)], mine, one, two, three)[0]


def gradient(logits, hit, stats, other, lse_rest, cotangent):
    def body(logits_ref, hit_ref, s, o, rest, cot, loss, grad):
        whole_stats = merged(s[...], o[...])
        row_max, row_total, target_logit = (whole_stats[k : k + 1, :] for k in range(3))
        lse_window = row_max + jnp.log(row_total)
        larger = jnp.maximum(lse_window, rest[...])
        log_total = larger + jnp.log(
            jnp.exp(lse_window - larger) + jnp.exp(rest[...] - larger)
        )
        loss[...] = log_total - target_logit + z_weight * log_total * log_total
        softmax = jnp.exp(logits_ref[...] - log_total)
        grad[...] = (
            cot[...] * (softmax * (1.0 + 2.0 * z_weight * log_total) - hit_ref[...])
        ).astype(BF16)

    outs = [
        jax.ShapeDtypeStruct((1, 2 * TOK), F32),
        jax.ShapeDtypeStruct((ROWS, 2 * TOK), BF16),
    ]
    return local_call(body, outs, logits, hit, stats, other, lse_rest, cotangent)


def gathered_logits(head, hidden, at, sibling_at):
    zb, za = move(head[:PR], "zh", 1), move(head[:PR], "zh", -1)
    xb, xa = move(head, "x", 1), move(head, "x", -1)
    picked = pick(hidden, sibling_at, 44)
    zb, za, xb, xa, picked = lax.optimization_barrier((zb, za, xb, xa, picked))
    theirs = move(picked, "c", 1)
    zf1, zf2 = move(zb[:PH], "zh", 1), move(za[PH:], "zh", -1)
    xf1, xf2 = move(xb[PR : PR + QH], "x", 1), move(xa[PR + QH :], "x", -1)
    q = joined((head, PR, QR), (xa, PR, QR), (xf1, 0, QH), (xf2, 0, QH), (xb, PR, QR))
    p = joined((za, 0, PR), (zf1, 0, PH), (zf2, 0, PH), (zb, 0, PR), after=[q])
    pb, pa = move(p, "x", 1), move(p, "x", -1)
    qb, qa = move(q, "zh", 1), move(q, "zh", -1)
    zf1, zf2, at = lax.optimization_barrier((zf1, zf2, at))
    mine = pick(hidden, at, 30)
    blocks = (mine, theirs)

    def first(add, refs, out):
        head_ref, xa_ref, xb_ref, xf1_ref, xf2_ref, p_ref = refs
        out[...] = jnp.zeros_like(out)
        add(out, head_ref[...], 0)
        add(out, xa_ref[...], 1)
        add(out, xb_ref[...], 3)
        add(out.at[PR : PR + QH], xf1_ref[...], 2)
        add(out.at[PR + QH :], xf2_ref[...], 2)
        for dz in (1, 2, 3):
            add(out.at[:PR], p_ref[(dz - 1) * PR : dz * PR, :], 4 * dz)

    total = logits_call(first, blocks, [head, xa, xb, xf1, xf2, p])
    pb, pa, qb, qa, total = lax.optimization_barrier((pb, pa, qb, qa, total))
    pf1 = joined((pb, 0, 3 * PH), (xb, 0, PH))
    pf2 = joined((pa, 3 * PH, 3 * PH), (xa, PH, PH))
    pf1, pf2 = move(pf1, "x", 1), move(pf2, "x", -1)
    qf1, qf2 = move(qb[: 2 * QR], "zh", 1), move(qa[2 * QR :], "zh", -1)

    def second(add, refs, out):
        pa_ref, pb_ref, qa_ref, qb_ref, total_ref = refs
        out[...] = total_ref[...]

        @pl.loop(0, 3)
        def _(k):
            part = rows_at(k, PR)
            add(out.at[:PR], pa_ref[part, :], 4 * k + 5)
            add(out.at[:PR], pb_ref[part, :], 4 * k + 7)

        @pl.loop(0, 4)
        def _(dx):
            part = rows_at(dx, QR)
            add(out.at[PR:], qa_ref[part, :], 4 + dx)
            add(out.at[PR:], qb_ref[part, :], 12 + dx)

    total = logits_call(second, blocks, [pa, pb, qa, qb, total])

    def third(add, refs, out):
        pf1_ref, pf2_ref, qf1_ref, qf2_ref, total_ref = refs
        out[...] = total_ref[...]
        add(out.at[:PR], pf1_ref[:PR, :], 4 + 2)
        add(out.at[:PH], pf1_ref[PR : 3 * PH, :], 8 + 2)
        add(out.at[PH:PR], pf2_ref[:PH, :], 8 + 2)
        add(out.at[:PR], pf2_ref[PH : 3 * PH, :], 12 + 2)
        add(out.at[:PH], pf1_ref[3 * PH :, :], 2)
        add(out.at[PH:PR], pf2_ref[3 * PH :, :], 2)
        add(out.at[PR:], qf1_ref[:QR, :], 8)
        add(out.at[PR:], qf1_ref[QR:, :], 8 + 1)
        add(out.at[PR:], qf2_ref[:QR, :], 8 + 2)
        add(out.at[PR:], qf2_ref[QR:, :], 8 + 3)

    total = logits_call(third, blocks, [pf1, pf2, qf1, qf2, total])
    return total, blocks


def scattered_gradient(grad, blocks):
    def array(rows, dtype):
        return jax.ShapeDtypeStruct((rows, WIDE), dtype)

    outs = [
        array(3 * PR, BF16),
        array(3 * PR, BF16),
        array(4 * QR, BF16),
        array(4 * QR, BF16),
        array(3 * PH, F32),
        array(3 * PH, F32),
        array(3 * PR, F32),
        array(4 * QH, F32),
        array(4 * QH, F32),
    ]
    def others_terms(block, refs, outs):
        (g_ref,) = refs
        p_up, p_down, q_up, q_down, p_ahead, p_behind, p_here, q_ahead, q_behind, q_scratch = outs

        @pl.loop(0, 3)
        def _(k):
            first, last = pl.ds(pl.multiple_of(k * PR, PR), PH), pl.ds(pl.multiple_of(k * PR + PH, PH), PH)
            kept = rows_at(k, PH)
            held = [block(4 * k + dx) for dx in range(4)]
            for dx in (2, 1, 3, 0):
                term = jnp.dot(g_ref[:, :TOK], held[dx][:TOK], preferred_element_type=F32)
                term += jnp.dot(g_ref[:, TOK:], held[dx][TOK:], preferred_element_type=F32)
                one, two = term[:PH], term[PH:PR]
                if dx == 0:
                    p_here[rows_at(k, PR), :] = term[:PR]
                elif dx == 1:
                    p_ahead[kept, :] = one
                    p_up[last, :] = two.astype(BF16)
                elif dx == 2:
                    p_up[first, :] = one.astype(BF16)
                    p_down[last, :] = two.astype(BF16)
                else:
                    p_down[first, :] = one.astype(BF16)
                    p_behind[kept, :] = two
                q_scratch[dx] = term[PR:]

            for dx in range(4):
                start, middle = dx * QR, dx * QR + QH
                three, four = q_scratch[dx, :QH], q_scratch[dx, QH:]

                @pl.when(k == 0)
                def _():
                    q_ahead[dx * QH : (dx + 1) * QH, :] = three
                    q_up[middle : middle + QH, :] = four.astype(BF16)

                @pl.when(k == 1)
                def _():
                    q_up[start:middle, :] = three.astype(BF16)
                    q_down[middle : middle + QH, :] = four.astype(BF16)

                @pl.when(k == 2)
                def _():
                    q_down[start:middle, :] = three.astype(BF16)
                    q_behind[dx * QH : (dx + 1) * QH, :] = four

    slots = {place: 4 + place for place in range(12)}
    q_rows = jax.ShapeDtypeStruct((4, QR, WIDE), F32)
    p_up, p_down, q_up, q_down, p_ahead, p_behind, p_here, q_ahead, q_behind, _ = block_call(
        others_terms, slots, outs + [q_rows], blocks, [grad], 12 * ROWS
    )
    p_up, p_down = move(p_up, "x", 1), move(p_down, "x", -1)
    q_up, q_down = move(q_up, "zh", 1), move(q_down, "zh", -1)
    def own_terms(block, refs, outs):
        (g_ref,) = refs
        own, q_here = outs

        @pl.loop(0, 4)
        def _(dx):
            term = jnp.dot(g_ref[...], block(dx), preferred_element_type=F32)
            own[rows_at(dx, PR), :] = term[:PR]
            q_here[rows_at(dx, QR), :] = term[PR:]

    outs = [array(4 * PR, F32), array(4 * QR, F32)]
    own, q_here = block_call(
        own_terms, {dx: dx for dx in range(4)}, outs, blocks, [grad], 4 * ROWS
    )
    p_up, p_down, own, q_here = lax.optimization_barrier((p_up, p_down, own, q_here))

    def forward(kept_ahead, kept_behind, up, down, n, half):
        def body(a, b, u, d, up_out, down_out):
            for k in range(n):
                to, first, last = k * half, 2 * k * half, (2 * k + 1) * half
                up_out[to : to + half, :] = (
                    a[to : to + half, :] + u[first : first + half, :].astype(F32)
                ).astype(BF16)
                down_out[to : to + half, :] = (
                    b[to : to + half, :] + d[last : last + half, :].astype(F32)
                ).astype(BF16)

        return local_call(
            body, [array(n * half, BF16)] * 2, kept_ahead, kept_behind, up, down
        )

    def settle(kept, up, down, up2, down2, n, half, k):
        to, first, last = k * half, 2 * k * half, (2 * k + 1) * half
        one = kept[first : first + half, :] + down[first : first + half, :].astype(F32)
        two = kept[last : last + half, :] + up[last : last + half, :].astype(F32)
        return (
            one + up2[to : to + half, :].astype(F32),
            two + down2[to : to + half, :].astype(F32),
        )

    p_up2, p_down2 = forward(p_ahead, p_behind, p_up, p_down, 3, PH)
    p_up2, p_down2 = move(p_up2, "x", 1), move(p_down2, "x", -1)
    q_up2, q_down2 = forward(q_ahead, q_behind, q_up, q_down, 4, QH)
    q_up2, q_down2 = move(q_up2, "zh", 1), move(q_down2, "zh", -1)

    def p_body(kept, up, down, up2, down2, *outs):
        for k in range(3):
            one, two = settle(kept, up, down, up2, down2, 3, PH, k)
            outs[k][:PH, :] = one.astype(BF16)
            outs[k][PH:, :] = two.astype(BF16)

    z1, z2, z3 = local_call(
        p_body, [array(PR, BF16)] * 3, p_here, p_up, p_down, p_up2, p_down2
    )
    p_sent = z1
    z1, z2, z3 = move(z1, "zh", 1), move(z2, "zh", 2), move(z3, "zh", -1)

    def q_body(own, kept, up, down, up2, down2, _, up_out, down_out, ahead, behind, here):
        rest = PR - RH
        for dx in range(4):
            one, two = settle(kept, up, down, up2, down2, 4, QH, dx)
            first = own[dx * PR : dx * PR + RH, :]
            last = own[dx * PR + RH : (dx + 1) * PR, :]
            for ref, at_last, low in {
                0: ((here, RH, 0),),
                1: ((up_out, RH, 1),),
                2: ((down_out, RH, 1),),
                3: ((behind, 0, 0),),
            }[dx]:
                ref[at_last : at_last + rest, :] = last.astype(ref.dtype)
                ref[at_last + rest : at_last + rest + QH, :] = one.astype(ref.dtype)
                ref[at_last + rest + QH : at_last + RH, :] = two.astype(ref.dtype)
            ref = (here, ahead, up_out, down_out)[dx]
            ref[:RH, :] = first.astype(ref.dtype)

    x_up, x_down, x_ahead, x_behind, x_here = local_call(
        q_body,
        [array(ROWS, BF16), array(ROWS, BF16), array(RH, F32), array(RH, F32), array(ROWS, F32)],
        own, q_here, q_up, q_down, q_up2, q_down2, p_sent,
    )
    x_up, x_down = move(x_up, "x", 1), move(x_down, "x", -1)

    x_up2, x_down2 = forward(x_ahead, x_behind, x_up, x_down, 1, RH)
    x_up2, x_down2 = move(x_up2, "x", 1), move(x_down2, "x", -1)

    def last_body(here, xu, xd, xu2, xd2, z1, z2, z3, out):
        out[:RH, :] = here[:RH, :] + xd[:RH, :].astype(F32) + xu2[...].astype(F32)
        out[RH:, :] = here[RH:, :] + xu[RH:, :].astype(F32) + xd2[...].astype(F32)
        out[:PR, :] += z1[...].astype(F32) + z2[...].astype(F32) + z3[...].astype(F32)

    (out,) = local_call(
        last_body, [array(ROWS, F32)], x_here, x_up, x_down, x_up2, x_down2, z1, z2, z3
    )
    return out


def shards(hidden, head, targets, block_index, lse_rest, cotangent):
    zh, x, c = (lax.axis_index(a) for a in DP)
    first_row = lax.axis_index(TENSOR) * ROWS
    row_ids = first_row + lax.iota(jnp.int32, ROWS)
    block_of = row_ids // BLOCK
    block_match = (block_of[:, None] == lax.iota(jnp.int32, block_index.shape[0])[None, :]).astype(
        jnp.int32
    )
    vocab_ids = jnp.sum(block_match * block_index[None, :], axis=1) * BLOCK + row_ids % BLOCK

    k = lax.iota(jnp.int32, 16)
    at = (((zh + k // 4) % 4) * 4 + (x + k % 4) % 4) * 2
    at, sibling_at = at + c, at + (1 - c)

    facts = jnp.stack([targets.astype(F32), lse_rest, cotangent])
    facts = jnp.concatenate([facts, move(facts, "c", 1)], axis=1)
    hit = (vocab_ids[:, None] == facts[0].astype(jnp.int32)[None, :]).astype(F32)

    partial, blocks = gathered_logits(head, hidden, at, sibling_at)
    logits, stats = statistics(partial, move(partial, "c", 1), hit)
    stats = merge_four(stats, *(move(stats, "y", by) for by in (1, 2, 3)))
    loss, grad = gradient(
        logits, hit, stats, move(stats, "zl", 1), facts[1:2], facts[2:3]
    )
    return loss[0, :TOK], scattered_gradient(grad, blocks)


def solution(mesh):
    mesh = Mesh(mesh.devices.reshape(SIZES), AXES)
    placed = (P(DP, None), P(TENSOR, DP), P(DP), P(), P(DP), P(DP))
    return jax.shard_map(
        shards, mesh=mesh, in_specs=placed, out_specs=(P(DP), P(TENSOR, DP)), check_vma=False
    )
```
